32 devices in a mesh: blk: 16 (over z, x, core), batch: 2 (over y).
Axes of the slice: x: 2, y: 2, z: 4, core: 2. Of those that a mesh axis runs over, the one named last changes fastest.
Arguments:
- residues: bfloat16 [2, 2048, 512], P('batch', 'blk'), may hold values from -6 to 6
- memory: bfloat16 [2, 2048, 512], P('batch', 'blk'), may hold values from -6 to 6
- lengths: int32 [2, 4], P('batch'), may hold values from 1 to 2000, as said below
- cotangent: bfloat16 [2, 2048, 512], P('batch', 'blk'), may hold values from -6 to 6
- self_norm_gain: float32 [512], replicated, may hold values from 0.5 to 1.5
- self_norm_bias: float32 [512], replicated, may hold values from -3 to 3
- self_query: bfloat16 [512, 512], replicated, may hold values from -0.25 to 0.25
- self_query_bias: float32 [512], replicated, may hold values from -3 to 3
- self_key: bfloat16 [512, 512], replicated, may hold values from -0.25 to 0.25
- self_value: bfloat16 [512, 512], replicated, may hold values from -0.25 to 0.25
- self_value_bias: float32 [512], replicated, may hold values from -0.6 to 0.6
- self_output: bfloat16 [512, 512], replicated, may hold values from -4 to 4
- self_output_bias: float32 [512], replicated, may hold values from -3 to 3
- cross_norm_gain: float32 [512], replicated, may hold values from 0.5 to 1.5
- cross_norm_bias: float32 [512], replicated, may hold values from -3 to 3
- cross_query: bfloat16 [512, 512], replicated, may hold values from -0.25 to 0.25
- cross_query_bias: float32 [512], replicated, may hold values from -3 to 3
- cross_key: bfloat16 [512, 512], replicated, may hold values from -0.25 to 0.25
- cross_value: bfloat16 [512, 512], replicated, may hold values from -0.25 to 0.25
- cross_value_bias: float32 [512], replicated, may hold values from -0.6 to 0.6
- cross_output: bfloat16 [512, 512], replicated, may hold values from -4 to 4
- cross_output_bias: float32 [512], replicated, may hold values from -3 to 3
- feed_norm_gain: float32 [512], replicated, may hold values from 0.1 to 1.9
- feed_norm_bias: float32 [512], replicated, may hold values from -3 to 3
- feed_in: bfloat16 [512, 2048], replicated, may hold values from -0.25 to 0.25
- feed_in_bias: float32 [2048], replicated, may hold values from -3 to 3
- feed_out: bfloat16 [2048, 512], replicated, may hold values from -0.125 to 0.125
- feed_out_bias: float32 [512], replicated, may hold values from -6 to 6
Outputs:
- layer_out: float32 [2, 2048, 512], P('batch', 'blk')
- residues_grad: float32 [2, 2048, 512], P('batch', 'blk')
- memory_grad: float32 [2, 2048, 512], P('batch', 'blk')
- grad_self_norm_gain: float32 [512], P('blk')
- grad_self_norm_bias: float32 [512], P('blk')
- grad_self_query: float32 [512, 512], P('blk')
- grad_self_query_bias: float32 [512], P('blk')
- grad_self_key: float32 [512, 512], P('blk')
- grad_self_value: float32 [512, 512], P('blk')
- grad_self_value_bias: float32 [512], P('blk')
- grad_self_output: float32 [512, 512], P('blk')
- grad_self_output_bias: float32 [512], P('blk')
- grad_cross_norm_gain: float32 [512], P('blk')
- grad_cross_norm_bias: float32 [512], P('blk')
- grad_cross_query: float32 [512, 512], P('blk')
- grad_cross_query_bias: float32 [512], P('blk')
- grad_cross_key: float32 [512, 512], P('blk')
- grad_cross_value: float32 [512, 512], P('blk')
- grad_cross_value_bias: float32 [512], P('blk')
- grad_cross_output: float32 [512, 512], P('blk')
- grad_cross_output_bias: float32 [512], P('blk')
- grad_feed_norm_gain: float32 [512], P('blk')
- grad_feed_norm_bias: float32 [512], P('blk')
- grad_feed_in: float32 [512, 2048], P('blk')
- grad_feed_in_bias: float32 [2048], P('blk')
- grad_feed_out: float32 [2048, 512], P('blk')
- grad_feed_out_bias: float32 [512], P('blk')
The draws below stay inside these ranges and needn't reach their ends.
Inputs may be any that keep to these rules, and one draw needn't show every extreme that they name: Each row of lengths sums to 2048 and holds positive counts. In every group one complex, at a position that varies, has exactly 2048 - 3 * (16) residues, so it begins within the first 128 residues and ends within the last 128; the shortest complex of every group has 1 residue.
All inputs are finite; a program needn't handle non-finite values.
Results may differ from the reference program's by a relative error of at most 0.034.
Values may be sent and summed in bfloat16 or wider, within the bound.
A program may use at most 384 MiB of HBM per device.

```python
import math
import jax
import jax.numpy as jnp
from jax import lax

D = 512
HEADS = 8
FF = 2048
TOK_DEV = 128
DOCS = 4
SEQ = 2048
GROUPS = 2


def draw_lengths(key, part):
    key = jax.random.fold_in(key, 7)
    first_key, second_key = jax.random.split(key)
    piece = TOK_DEV // 8
    short_total = (DOCS - 1) * piece
    drawn = jax.random.randint(first_key, (GROUPS, DOCS - 2), 1, piece + 1)
    drawn = drawn - jnp.min(drawn, 1, keepdims=True) + 1
    remainder = short_total - jnp.sum(drawn, 1, keepdims=True)
    others = jnp.concatenate([drawn, remainder], 1).astype(jnp.int32)
    chosen = jax.random.randint(second_key, (GROUPS, 1), 0, DOCS)
    slots = jnp.arange(DOCS, dtype=jnp.int32)[None, :]
    marked = slots == chosen
    source = jnp.clip(slots - (slots > chosen).astype(jnp.int32), 0, DOCS - 2)
    placed = jnp.take_along_axis(others, source, 1)
    return jnp.where(marked, SEQ - short_total, placed).astype(jnp.int32)


def levels(key, extent, cuts, smallest, high):
    factor_of, own = 1.0, jax.random.fold_in(key, 6)
    for axis_at, parts in cuts:
        draws = jnp.exp(jax.random.uniform(jax.random.fold_in(own, axis_at), (parts,), jnp.float32, smallest / len(cuts), high / len(cuts)))
        factor_of = factor_of * jnp.repeat(draws, extent[axis_at] // parts).reshape([-1 if axis == axis_at else 1 for axis in range(len(extent))])
    return factor_of


def gaussian(key, extent, width, bound, cuts=(), kind=jnp.bfloat16):
    values = jax.random.normal(key, extent, jnp.float32) * width
    if len(cuts) > 0:
        values = levels(key, extent, cuts, -0.22, 0.18) * values
    return jnp.clip(values, min=-bound, max=bound).astype(kind)


def setup_inputs(seed: int = 0) -> dict:
    key_of = jax.random.split(jax.random.key(seed), 29)
    return {
        "residues": gaussian(key_of[0], (GROUPS, SEQ, D), 1.0, 6.0, ((0, 2), (1, 16))),
        "memory": gaussian(key_of[1], (GROUPS, SEQ, D), 1.0, 6.0, ((0, 2), (1, 16))),
        "lengths": draw_lengths(jax.random.fold_in(key_of[28], 71), 0),
        "cotangent": gaussian(key_of[3], (GROUPS, SEQ, D), 1.0, 6.0, ((0, 2), (1, 16))),
        "self_norm_gain": jnp.clip(1.0 + 0.1 * jax.random.normal(key_of[4], (D,), jnp.float32), 0.5, 1.5),
        "self_norm_bias": gaussian(key_of[5], (D,), 0.5, 3.0, (), jnp.float32),
        "self_query": gaussian(key_of[6], (D, D), D ** -0.5, 0.25),
        "self_query_bias": gaussian(key_of[7], (D,), 0.5, 3.0, (), jnp.float32),
        "self_key": gaussian(key_of[8], (D, D), D ** -0.5, 0.25),
        "self_value": gaussian(key_of[9], (D, D), D ** -0.5, 0.25),
        "self_value_bias": gaussian(key_of[10], (D,), 0.1, 0.6, (), jnp.float32),
        "self_output": gaussian(key_of[11], (D, D), 2 ** -0.5, 4.0),
        "self_output_bias": gaussian(key_of[12], (D,), 0.5, 3.0, (), jnp.float32),
        "cross_norm_gain": jnp.clip(1.0 + 0.1 * jax.random.normal(key_of[13], (D,), jnp.float32), 0.5, 1.5),
        "cross_norm_bias": gaussian(key_of[14], (D,), 0.5, 3.0, (), jnp.float32),
        "cross_query": gaussian(key_of[15], (D, D), D ** -0.5, 0.25),
        "cross_query_bias": gaussian(key_of[16], (D,), 0.5, 3.0, (), jnp.float32),
        "cross_key": gaussian(key_of[17], (D, D), D ** -0.5, 0.25),
        "cross_value": gaussian(key_of[18], (D, D), D ** -0.5, 0.25),
        "cross_value_bias": gaussian(key_of[19], (D,), 0.1, 0.6, (), jnp.float32),
        "cross_output": gaussian(key_of[20], (D, D), 2 ** -0.5, 4.0),
        "cross_output_bias": gaussian(key_of[21], (D,), 0.5, 3.0, (), jnp.float32),
        "feed_norm_gain": jnp.clip(1.0 + 0.18 * jax.random.normal(key_of[22], (D,), jnp.float32), 0.1, 1.9),
        "feed_norm_bias": gaussian(key_of[23], (D,), 0.5, 3.0, (), jnp.float32),
        "feed_in": gaussian(key_of[24], (D, FF), D ** -0.5, 0.25),
        "feed_in_bias": gaussian(key_of[25], (FF,), 0.5, 3.0, (), jnp.float32),
        "feed_out": gaussian(key_of[26], (FF, D), FF ** -0.5, 0.125),
        "feed_out_bias": gaussian(key_of[27], (D,), 1.0, 6.0, (), jnp.float32),
    }


NEG = -1e+30
EPS = 1e-05
HIGH = lax.Precision.HIGHEST
SQRT_HALF = 0.7071067811865476

@jax.custom_vjp
def low(v):
    return lax.optimization_barrier(v.astype(jnp.bfloat16)).astype(jnp.float32)

@jax.custom_vjp
def low_back(v):
    return v

def low_keep(v):
    return (low(v), None)

def low_pass(kept, grad):
    return (grad,)

def back_keep(v):
    return (v, None)

def back_low(kept, grad):
    return (low(grad),)
low.defvjp(low_keep, low_pass)
low_back.defvjp(back_keep, back_low)

def layer_norm(values, gain, shift):
    average = lax.optimization_barrier(jnp.mean(values, -1, keepdims=True))
    centred = values - average
    factor = lax.rsqrt(lax.optimization_barrier(jnp.mean(centred * centred, -1, keepdims=True)) + EPS)
    return centred * factor * gain + shift

def matmul(left, right):
    return jnp.dot(left, right, precision=HIGH)

def gelu_value(values):
    return 0.5 * values * (1.0 + lax.erf(values * SQRT_HALF))

def complex_ids(lengths_row, positions):
    bounds = jnp.cumsum(lengths_row)
    return lax.optimization_barrier(jnp.sum((positions[:, None] >= bounds[None, :]).astype(jnp.int32), 1))

def attend(queries, key_rows, value_rows, docs, causal):
    total_rows = queries.shape[0]
    block = math.gcd(total_rows, 512)
    query_heads = queries.reshape(total_rows, HEADS, -1)
    key_heads = key_rows.reshape(total_rows, HEADS, -1)
    value_heads = value_rows.reshape(total_rows, HEADS, -1)
    factor = query_heads.shape[-1] ** (-0.5)
    key_pos = jnp.arange(total_rows, dtype=jnp.int32)

    def one_block(number):
        begin = (number * block).astype(jnp.int32)
        rows = lax.dynamic_slice_in_dim(query_heads, begin, block, 0)
        query_pos = begin + jnp.arange(block, dtype=jnp.int32)
        query_doc = lax.dynamic_slice_in_dim(docs, begin, block, 0)
        scores = low_back(jnp.einsum('qhd,khd->hqk', rows, key_heads, precision=HIGH) * factor)
        allowed = query_doc[:, None] == docs[None, :]
        if causal:
            allowed = allowed & (key_pos[None, :] <= query_pos[:, None])
        scores = jnp.where(allowed[None], scores, NEG)
        highest = lax.optimization_barrier(jnp.max(scores, -1, keepdims=True))
        raised = jnp.exp(scores - highest)
        probs = low(raised / lax.optimization_barrier(jnp.sum(raised, -1, keepdims=True)))
        return jnp.einsum('hqk,khd->qhd', probs, value_heads, precision=HIGH)
    blocks = lax.map(jax.checkpoint(one_block), jnp.arange(total_rows // block, dtype=jnp.int32))
    return blocks.reshape(total_rows, -1)

def layer(inputs, encoded, docs, params):
    self_norm_gain, self_norm_bias, self_query, self_query_bias, self_key, self_value, self_value_bias, self_output, self_output_bias, cross_norm_gain, cross_norm_bias, cross_query, cross_query_bias, cross_key, cross_value, cross_value_bias, cross_output, cross_output_bias, feed_norm_gain, feed_norm_bias, feed_in, feed_in_bias, feed_out, feed_out_bias = params
    normed = low(layer_norm(inputs, self_norm_gain, self_norm_bias))
    queries = low(low_back(matmul(normed, self_query) + self_query_bias))
    key_rows = low(low_back(matmul(normed, self_key)))
    value_rows = low(low_back(matmul(normed, self_value) + self_value_bias))
    attended = low(low_back(attend(queries, key_rows, value_rows, docs, True)))
    after_self = inputs + low_back(matmul(attended, self_output) + self_output_bias)
    normed = low(layer_norm(after_self, cross_norm_gain, cross_norm_bias))
    queries = low(low_back(matmul(normed, cross_query) + cross_query_bias))
    key_rows = low(low_back(matmul(encoded, cross_key)))
    value_rows = low(low_back(matmul(encoded, cross_value) + cross_value_bias))
    attended = low(low_back(attend(queries, key_rows, value_rows, docs, False)))
    after_cross = after_self + low_back(matmul(attended, cross_output) + cross_output_bias)
    normed = low(layer_norm(after_cross, feed_norm_gain, feed_norm_bias))
    inner = low_back(matmul(normed, feed_in) + feed_in_bias)
    activation = low(gelu_value(inner))
    return after_cross + low_back(matmul(activation, feed_out) + feed_out_bias)

def reference(residues, memory, lengths, cotangent, self_norm_gain, self_norm_bias, self_query, self_query_bias, self_key, self_value, self_value_bias, self_output, self_output_bias, cross_norm_gain, cross_norm_bias, cross_query, cross_query_bias, cross_key, cross_value, cross_value_bias, cross_output, cross_output_bias, feed_norm_gain, feed_norm_bias, feed_in, feed_in_bias, feed_out, feed_out_bias):
    params = tuple((value.astype(jnp.float32) for value in (self_norm_gain, self_norm_bias, self_query, self_query_bias, self_key, self_value, self_value_bias, self_output, self_output_bias, cross_norm_gain, cross_norm_bias, cross_query, cross_query_bias, cross_key, cross_value, cross_value_bias, cross_output, cross_output_bias, feed_norm_gain, feed_norm_bias, feed_in, feed_in_bias, feed_out, feed_out_bias)))
    positions = jnp.arange(SEQ, dtype=jnp.int32)
    doc_rows = [complex_ids(lengths[number], positions) for number in range(GROUPS)]

    def whole(inputs, encoded, weights):
        return jnp.stack([layer(inputs[number], encoded[number], doc_rows[number], weights) for number in range(GROUPS)])
    result, pullback = jax.vjp(whole, residues.astype(jnp.float32), memory.astype(jnp.float32), params)
    grad_inputs, grad_memory, grads = pullback(cotangent.astype(jnp.float32))
    return (result, grad_inputs, grad_memory, grads[0], grads[1], grads[2], grads[3], grads[4], grads[5], grads[6], grads[7], grads[8], grads[9], grads[10], grads[11], grads[12], grads[13], grads[14], grads[15], grads[16], grads[17], grads[18], grads[19], grads[20], grads[21], grads[22], grads[23])
```

```python
import functools
import typing

import jax
import jax.numpy as jnp
from jax import lax
from jax.experimental import pallas as pl
from jax.experimental.pallas import tpu as pltpu
from jax.sharding import PartitionSpec as P

HEADS = 8


NEG = -1e30
EPS = 1e-05
SQRT_HALF = 0.7071067811865476
INV_ROOT_TAU = 0.3989422804014327


def layer_norm(values, gain, shift):
    average = jnp.mean(values, -1, keepdims=True)
    centred = values - average
    factor = lax.rsqrt(jnp.mean(centred * centred, -1, keepdims=True) + EPS)
    normal = centred * factor
    return (normal * gain + shift, normal, factor)


def norm_back(gradient, normal, factor, gain):
    weighted = gradient * gain
    average_one = jnp.mean(weighted, -1, keepdims=True)
    average_two = jnp.mean(weighted * normal, -1, keepdims=True)
    return (
        factor * (weighted - average_one - normal * average_two),
        jnp.sum(gradient * normal, 0),
        jnp.sum(gradient, 0),
    )


def gelu_value(values):
    return 0.5 * values * (1.0 + lax.erf(values * SQRT_HALF))


def gelu_slope(values):
    return (
        0.5 * (1.0 + lax.erf(values * SQRT_HALF))
        + values * jnp.exp(-0.5 * values * values) * INV_ROOT_TAU
    )


def heads_of(matrix):
    return matrix.reshape(matrix.shape[0], HEADS, -1)


def complex_ids(lengths_row, positions):
    bounds = jnp.cumsum(lengths_row)
    return jnp.sum((positions[:, None] >= bounds[None, :]).astype(jnp.int32), 1)


def visible(query_pos, query_doc, key_pos, key_doc, causal):
    allowed = query_doc[:, None] == key_doc[None, :]
    if causal:
        allowed = allowed & (key_pos[None, :] <= query_pos[:, None])
    return allowed


def project(left, right):
    return jnp.dot(left, right, preferred_element_type=jnp.float32)


def pass_through(pieces):
    return (pieces[0].astype(jnp.bfloat16), pieces[1].astype(jnp.bfloat16))


def empty_state(tokens, head_size):
    return (
        jnp.full((HEADS, tokens), NEG, jnp.float32),
        jnp.zeros((HEADS, tokens), jnp.float32),
        jnp.zeros((HEADS, tokens, head_size), jnp.float32),
    )


def finish(state_out):
    running_max, running_sum, summed = state_out
    attended = (summed / running_sum[..., None]).transpose(1, 0, 2)
    return (attended.reshape(attended.shape[0], -1), (running_max + jnp.log(running_sum)).T)


def spread_of(grad_low, attended):
    return jnp.sum(heads_of(grad_low).astype(jnp.float32) * heads_of(attended), -1)


def forward_fold(queries, query_pos, query_doc, lengths_row, causal, prepare, carried, pieces):
    factor = queries.shape[-1] ** (-0.5)
    piece_rows = pieces[0].shape[0]
    key_pos = jnp.arange(piece_rows, dtype=jnp.int32)
    allowed = visible(query_pos, query_doc, key_pos, complex_ids(lengths_row, key_pos), causal)

    def active(state_in):
        running_max, running_sum, summed = state_in
        key_rows, value_rows = prepare(pieces)
        scores = (
            jnp.einsum(
                "qhd,khd->hqk", queries, heads_of(key_rows), preferred_element_type=jnp.float32
            )
            * factor
        )
        scores = jnp.where(allowed[None], scores, NEG)
        new_max = jnp.maximum(running_max, jnp.max(scores, -1))
        weights = jnp.where(allowed[None], jnp.exp(scores - new_max[..., None]), 0.0)
        running_sum = jnp.sum(weights, -1)
        summed = jnp.einsum(
            "hqk,khd->hqd",
            weights.astype(jnp.bfloat16),
            heads_of(value_rows),
            preferred_element_type=jnp.float32,
        )
        return (new_max, running_sum, summed)

    return lax.cond(jnp.any(allowed), active, lambda state_in: state_in, carried)


def query_fold(
    queries, grad_out, log_total, spread, query_pos, query_doc, lengths_row, causal, prepare
):
    factor = queries.shape[-1] ** (-0.5)
    log_rows = log_total.T[..., None]
    spread_rows = spread.T[..., None]

    def fold(carried, pieces, offset):
        piece_rows = pieces[0].shape[0]
        key_pos = jnp.arange(piece_rows, dtype=jnp.int32)
        allowed = visible(query_pos, query_doc, key_pos, complex_ids(lengths_row, key_pos), causal)

        def active(accum):
            key_rows, value_rows = prepare(pieces)
            key_heads = heads_of(key_rows)
            scores = (
                jnp.einsum("qhd,khd->hqk", queries, key_heads, preferred_element_type=jnp.float32)
                * factor
            )
            scores = jnp.where(allowed[None], scores, NEG)
            weights = jnp.where(allowed[None], jnp.exp(scores - log_rows), 0.0)
            slopes = jnp.einsum(
                "qhd,khd->hqk", grad_out, heads_of(value_rows), preferred_element_type=jnp.float32
            )
            tilted = (weights * (slopes - spread_rows)).astype(jnp.bfloat16)
            return (
                jnp.einsum("hqk,khd->qhd", tilted, key_heads, preferred_element_type=jnp.float32)
                * factor
            )

        return lax.cond(jnp.any(allowed), active, lambda accum: accum, carried)

    return fold


def key_fold(key_heads, value_heads, key_pos, key_doc, lengths_row, causal):
    factor = key_heads.shape[-1] ** (-0.5)

    def fold(carried, pieces, offset):
        queries, grad_out, log_total, spread = pieces
        piece_rows = queries.shape[0]
        query_pos = jnp.arange(piece_rows, dtype=jnp.int32)
        allowed = visible(query_pos, complex_ids(lengths_row, query_pos), key_pos, key_doc, causal)

        def active(sums_in):
            query_heads = heads_of(queries.astype(jnp.bfloat16))
            grad_heads = heads_of(grad_out.astype(jnp.bfloat16))
            scores = (
                jnp.einsum(
                    "qhd,khd->hqk", query_heads, key_heads, preferred_element_type=jnp.float32
                )
                * factor
            )
            scores = jnp.where(allowed[None], scores, NEG)
            weights = jnp.where(allowed[None], jnp.exp(scores - log_total.T[..., None]), 0.0)
            grad_values = jnp.einsum(
                "hqk,qhd->khd",
                weights.astype(jnp.bfloat16),
                grad_heads,
                preferred_element_type=jnp.float32,
            )
            slopes = jnp.einsum(
                "qhd,khd->hqk", grad_heads, value_heads, preferred_element_type=jnp.float32
            )
            tilted = (weights * (slopes - spread.T[..., None])).astype(jnp.bfloat16)
            grad_keys = (
                jnp.einsum("hqk,qhd->khd", tilted, query_heads, preferred_element_type=jnp.float32)
                * factor
            )
            return (grad_keys, grad_values)

        return lax.cond(jnp.any(allowed), active, lambda sums_in: sums_in, carried)

    return fold


def mutual_fold(
    queries,
    grad_out,
    log_total,
    spread,
    key_heads,
    value_heads,
    positions,
    docs,
    lengths_row,
    carried,
    pieces,
    offset,
):
    toward_queries = query_fold(
        queries, grad_out, log_total, spread, positions, docs, lengths_row, True, pass_through
    )
    toward_keys = key_fold(key_heads, value_heads, positions, docs, lengths_row, True)
    grad_query_acc, grad_keys, grad_values = carried
    remote_q, remote_grad, remote_log, remote_spread, remote_k, remote_v = pieces
    grad_query_acc = toward_queries(grad_query_acc, (remote_k, remote_v), offset)
    grad_keys, grad_values = toward_keys(
        (grad_keys, grad_values), (remote_q, remote_grad, remote_log, remote_spread), offset
    )
    return (grad_query_acc, grad_keys, grad_values)


def local(
    residues,
    memory,
    lengths,
    cotangent,
    self_norm_gain,
    self_norm_bias,
    self_query,
    self_query_bias,
    self_key,
    self_value,
    self_value_bias,
    self_output,
    self_output_bias,
    cross_norm_gain,
    cross_norm_bias,
    cross_query,
    cross_query_bias,
    cross_key,
    cross_value,
    cross_value_bias,
    cross_output,
    cross_output_bias,
    feed_norm_gain,
    feed_norm_bias,
    feed_in,
    feed_in_bias,
    feed_out,
    feed_out_bias,
):
    tokens = residues.shape[1]
    model_width = residues.shape[2]
    head_size = model_width // HEADS
    device_rank = lax.axis_index("blk")
    positions = device_rank * tokens + jnp.arange(tokens, dtype=jnp.int32)
    lengths_row = lengths[0]
    complexes = complex_ids(lengths_row, positions)
    inputs = residues[0].astype(jnp.float32)
    encoded = memory[0]
    upstream = cotangent[0].astype(jnp.float32)
    normed_one, unit_one, factor_one = layer_norm(inputs, self_norm_gain, self_norm_bias)
    normed_one = normed_one.astype(jnp.bfloat16)
    self_q = (project(normed_one, self_query) + self_query_bias).astype(jnp.bfloat16)
    self_k = project(normed_one, self_key).astype(jnp.bfloat16)
    self_v = (project(normed_one, self_value) + self_value_bias).astype(jnp.bfloat16)
    state_out = forward_fold(
        heads_of(self_q),
        positions,
        complexes,
        lengths_row,
        True,
        pass_through,
        empty_state(tokens, head_size),
        (
            lax.all_gather(self_k, "blk", axis=0, tiled=True),
            lax.all_gather(self_v, "blk", axis=0, tiled=True),
        ),
    )
    self_attended, self_log = finish(state_out)
    self_low = self_attended.astype(jnp.bfloat16)
    after_self = inputs + project(self_low, self_output) + self_output_bias
    normed_two, unit_two, factor_two = layer_norm(after_self, cross_norm_gain, cross_norm_bias)
    normed_two = normed_two.astype(jnp.bfloat16)
    cross_q = (project(normed_two, cross_query) + cross_query_bias).astype(jnp.bfloat16)
    cross_k = project(encoded, cross_key).astype(jnp.bfloat16)
    cross_v = (project(encoded, cross_value) + cross_value_bias).astype(jnp.bfloat16)
    state_out = forward_fold(
        heads_of(cross_q),
        positions,
        complexes,
        lengths_row,
        False,
        pass_through,
        empty_state(tokens, head_size),
        (
            lax.all_gather(cross_k, "blk", axis=0, tiled=True),
            lax.all_gather(cross_v, "blk", axis=0, tiled=True),
        ),
    )
    cross_attended, cross_log = finish(state_out)
    cross_low = cross_attended.astype(jnp.bfloat16)
    after_cross = after_self + project(cross_low, cross_output) + cross_output_bias
    normed_three, unit_three, factor_three = layer_norm(after_cross, feed_norm_gain, feed_norm_bias)
    normed_three = normed_three.astype(jnp.bfloat16)
    inner = project(normed_three, feed_in) + feed_in_bias
    activation = gelu_value(inner).astype(jnp.bfloat16)
    layer_out = after_cross + project(activation, feed_out) + feed_out_bias
    grad_branch = upstream.astype(jnp.bfloat16)
    grad_feed_out_bias = jnp.sum(grad_branch.astype(jnp.float32), 0)
    grad_feed_out = jnp.einsum(
        "tf,td->fd", activation, grad_branch, preferred_element_type=jnp.float32
    )
    grad_active = jnp.einsum("td,fd->tf", grad_branch, feed_out, preferred_element_type=jnp.float32)
    grad_inner = (grad_active * gelu_slope(inner)).astype(jnp.bfloat16)
    grad_feed_in_bias = jnp.sum(grad_inner.astype(jnp.float32), 0)
    grad_feed_in = jnp.einsum(
        "td,tf->df", normed_three, grad_inner, preferred_element_type=jnp.float32
    )
    grad_normed = jnp.einsum("tf,df->td", grad_inner, feed_in, preferred_element_type=jnp.float32)
    norm_grad, grad_feed_norm_gain, grad_feed_norm_bias = norm_back(
        grad_normed, unit_three, factor_three, feed_norm_gain
    )
    upstream_two = upstream + norm_grad
    feed_parts = (
        grad_feed_norm_gain,
        grad_feed_norm_bias,
        grad_feed_in,
        grad_feed_in_bias,
        grad_feed_out,
        grad_feed_out_bias,
    )
    grad_branch = upstream_two.astype(jnp.bfloat16)
    grad_cross_output_bias = jnp.sum(grad_branch.astype(jnp.float32), 0)
    grad_cross_output = jnp.einsum(
        "tc,te->ce", cross_low, grad_branch, preferred_element_type=jnp.float32
    )
    grad_attended = jnp.einsum(
        "te,ce->tc", grad_branch, cross_output, preferred_element_type=jnp.float32
    ).astype(jnp.bfloat16)
    spread = spread_of(grad_attended, cross_attended)
    query_start = jnp.zeros((tokens, HEADS, head_size), jnp.float32)
    grad_query_acc = query_fold(
        heads_of(cross_q),
        heads_of(grad_attended),
        cross_log,
        spread,
        positions,
        complexes,
        lengths_row,
        False,
        pass_through,
    )(
        query_start,
        (
            lax.all_gather(cross_k, "blk", axis=0, tiled=True),
            lax.all_gather(cross_v, "blk", axis=0, tiled=True),
        ),
        jnp.int32(0),
    )
    grad_keys_acc, grad_values_acc = key_fold(
        heads_of(cross_k), heads_of(cross_v), positions, complexes, lengths_row, False
    )(
        (query_start, query_start),
        (
            lax.all_gather(cross_q.astype(jnp.float32), "blk", axis=0, tiled=True),
            lax.all_gather(grad_attended.astype(jnp.float32), "blk", axis=0, tiled=True),
            lax.all_gather(cross_log, "blk", axis=0, tiled=True),
            lax.all_gather(spread, "blk", axis=0, tiled=True),
        ),
        jnp.int32(0),
    )
    grad_cq = grad_query_acc.reshape(tokens, model_width).astype(jnp.bfloat16)
    grad_ck = grad_keys_acc.reshape(tokens, model_width).astype(jnp.bfloat16)
    grad_cv = grad_values_acc.reshape(tokens, model_width).astype(jnp.bfloat16)
    grad_cross_query = jnp.einsum(
        "tc,te->ce", normed_two, grad_cq, preferred_element_type=jnp.float32
    )
    grad_cross_query_bias = jnp.sum(grad_cq.astype(jnp.float32), 0)
    grad_cross_key = jnp.einsum("tc,te->ce", encoded, grad_ck, preferred_element_type=jnp.float32)
    grad_cross_value = jnp.einsum("tc,te->ce", encoded, grad_cv, preferred_element_type=jnp.float32)
    grad_cross_value_bias = jnp.sum(grad_cv.astype(jnp.float32), 0)
    memory_grad = jnp.einsum(
        "te,ce->tc", grad_ck, cross_key, preferred_element_type=jnp.float32
    ) + jnp.einsum("te,ce->tc", grad_cv, cross_value, preferred_element_type=jnp.float32)
    grad_normed = jnp.einsum("te,ce->tc", grad_cq, cross_query, preferred_element_type=jnp.float32)
    norm_grad, grad_cross_norm_gain, grad_cross_norm_bias = norm_back(
        grad_normed, unit_two, factor_two, cross_norm_gain
    )
    upstream_one = upstream_two + norm_grad
    cross_parts = (
        grad_cross_norm_gain,
        grad_cross_norm_bias,
        grad_cross_query,
        grad_cross_query_bias,
        grad_cross_key,
        grad_cross_value,
        grad_cross_value_bias,
        grad_cross_output,
        grad_cross_output_bias,
    )
    grad_branch = upstream_one.astype(jnp.bfloat16)
    grad_self_output_bias = jnp.sum(grad_branch.astype(jnp.float32), 0)
    grad_self_output = jnp.einsum(
        "tc,te->ce", self_low, grad_branch, preferred_element_type=jnp.float32
    )
    grad_attended = jnp.einsum(
        "te,ce->tc", grad_branch, self_output, preferred_element_type=jnp.float32
    ).astype(jnp.bfloat16)
    spread = spread_of(grad_attended, self_attended)
    grad_query_acc, grad_keys_acc, grad_values_acc = mutual_fold(
        heads_of(self_q),
        heads_of(grad_attended),
        self_log,
        spread,
        heads_of(self_k),
        heads_of(self_v),
        positions,
        complexes,
        lengths_row,
        (query_start, query_start, query_start),
        (
            lax.all_gather(self_q.astype(jnp.float32), "blk", axis=0, tiled=True),
            lax.all_gather(grad_attended.astype(jnp.float32), "blk", axis=0, tiled=True),
            lax.all_gather(self_log, "blk", axis=0, tiled=True),
            lax.all_gather(spread, "blk", axis=0, tiled=True),
            lax.all_gather(self_k.astype(jnp.float32), "blk", axis=0, tiled=True),
            lax.all_gather(self_v.astype(jnp.float32), "blk", axis=0, tiled=True),
        ),
        jnp.int32(0),
    )
    grad_sq = grad_query_acc.reshape(tokens, model_width).astype(jnp.bfloat16)
    grad_sk = grad_keys_acc.reshape(tokens, model_width).astype(jnp.bfloat16)
    grad_sv = grad_values_acc.reshape(tokens, model_width).astype(jnp.bfloat16)
    grad_self_query = jnp.einsum(
        "tc,te->ce", normed_one, grad_sq, preferred_element_type=jnp.float32
    )
    grad_self_query_bias = jnp.sum(grad_sq.astype(jnp.float32), 0)
    grad_self_key = jnp.einsum("tc,te->ce", normed_one, grad_sk, preferred_element_type=jnp.float32)
    grad_self_value = jnp.einsum(
        "tc,te->ce", normed_one, grad_sv, preferred_element_type=jnp.float32
    )
    grad_self_value_bias = jnp.sum(grad_sv.astype(jnp.float32), 0)
    grad_normed = (
        jnp.einsum("te,ce->tc", grad_sq, self_query, preferred_element_type=jnp.float32)
        + jnp.einsum("te,ce->tc", grad_sk, self_key, preferred_element_type=jnp.float32)
        + jnp.einsum("te,ce->tc", grad_sv, self_value, preferred_element_type=jnp.float32)
    )
    norm_grad, grad_self_norm_gain, grad_self_norm_bias = norm_back(
        grad_normed, unit_one, factor_one, self_norm_gain
    )
    residues_grad = upstream_one + norm_grad
    self_parts = (
        grad_self_norm_gain,
        grad_self_norm_bias,
        grad_self_query,
        grad_self_query_bias,
        grad_self_key,
        grad_self_value,
        grad_self_value_bias,
        grad_self_output,
        grad_self_output_bias,
    )
    ordered = (
        lax.psum_scatter(self_parts[0], "blk", scatter_dimension=0, tiled=True),
        lax.psum_scatter(self_parts[1], "blk", scatter_dimension=0, tiled=True),
        lax.psum_scatter(self_parts[2], "blk", scatter_dimension=0, tiled=True),
        lax.psum_scatter(self_parts[3], "blk", scatter_dimension=0, tiled=True),
        lax.psum_scatter(self_parts[4], "blk", scatter_dimension=0, tiled=True),
        lax.psum_scatter(self_parts[5], "blk", scatter_dimension=0, tiled=True),
        lax.psum_scatter(self_parts[6], "blk", scatter_dimension=0, tiled=True),
        lax.psum_scatter(self_parts[7], "blk", scatter_dimension=0, tiled=True),
        lax.psum_scatter(self_parts[8], "blk", scatter_dimension=0, tiled=True),
        lax.psum_scatter(cross_parts[0], "blk", scatter_dimension=0, tiled=True),
        lax.psum_scatter(cross_parts[1], "blk", scatter_dimension=0, tiled=True),
        lax.psum_scatter(cross_parts[2], "blk", scatter_dimension=0, tiled=True),
        lax.psum_scatter(cross_parts[3], "blk", scatter_dimension=0, tiled=True),
        lax.psum_scatter(cross_parts[4], "blk", scatter_dimension=0, tiled=True),
        lax.psum_scatter(cross_parts[5], "blk", scatter_dimension=0, tiled=True),
        lax.psum_scatter(cross_parts[6], "blk", scatter_dimension=0, tiled=True),
        lax.psum_scatter(cross_parts[7], "blk", scatter_dimension=0, tiled=True),
        lax.psum_scatter(cross_parts[8], "blk", scatter_dimension=0, tiled=True),
        lax.psum_scatter(feed_parts[0], "blk", scatter_dimension=0, tiled=True),
        lax.psum_scatter(feed_parts[1], "blk", scatter_dimension=0, tiled=True),
        lax.psum_scatter(feed_parts[2], "blk", scatter_dimension=0, tiled=True),
        lax.psum_scatter(feed_parts[3], "blk", scatter_dimension=0, tiled=True),
        lax.psum_scatter(feed_parts[4], "blk", scatter_dimension=0, tiled=True),
        lax.psum_scatter(feed_parts[5], "blk", scatter_dimension=0, tiled=True),
    )
    totals = lax.psum(
        (
            ordered[0],
            ordered[1],
            ordered[2],
            ordered[3],
            ordered[4],
            ordered[5],
            ordered[6],
            ordered[7],
            ordered[8],
            ordered[9],
            ordered[10],
            ordered[11],
            ordered[12],
            ordered[13],
            ordered[14],
            ordered[15],
            ordered[16],
            ordered[17],
            ordered[18],
            ordered[19],
            ordered[20],
            ordered[21],
            ordered[22],
            ordered[23],
        ),
        "batch",
    )
    return (layer_out[None], residues_grad[None], memory_grad[None]) + tuple(totals)


BLOCK = 128
HALF = 64
CHIPS = 8
HEAD = 64
WIDE = 512
HIDDEN = 2048
ROUND = 16
MASKED = -1e30
ONES_LANE = 5
SELF, CROSS = 0, 1
MESH = pl.DeviceIdType.MESH
VMEM = pl.BlockSpec(memory_space=pltpu.VMEM)
SMEM = pl.BlockSpec(memory_space=pltpu.SMEM)
PLACED = pl.BlockSpec(memory_space=pl.ANY)
BF16, F32 = jnp.bfloat16, jnp.float32

SQ, SK, SV, SO, CQ, CK, CV, CO = range(8)
(
    ROW_SELF_GAIN, ROW_SELF_SHIFT, ROW_SQ, ROW_SV, ROW_SO, ROW_CROSS_GAIN, ROW_CROSS_SHIFT, ROW_CQ, ROW_CV, ROW_CO,
    ROW_FEED_GAIN, ROW_FEED_SHIFT, ROW_OUT, ROW_IN,
) = range(14)
VECTOR_ROWS = 24
UNIT_OUT, UNIT_IN = 0, 4
UNIT_OF = {CO: 8, CQ: 9, CK: 10, CV: 11, SO: 12, SQ: 13, SK: 14, SV: 15}
UNITS = 16
SPANS = ((0, 9), (9, 13), (13, 16))
X_SQ, X_SO, X_CQ, X_CO, X_CDO, X_CDQ, X_SDO, X_SDQ = range(8)


class Operands(typing.NamedTuple):
    residues: VMEM
    memory: VMEM
    lengths: SMEM
    cotangent: VMEM
    self_norm_gain: VMEM
    self_norm_bias: VMEM
    self_query: PLACED
    self_query_bias: VMEM
    self_key: PLACED
    self_value: PLACED
    self_value_bias: VMEM
    self_output: PLACED
    self_output_bias: VMEM
    cross_norm_gain: VMEM
    cross_norm_bias: VMEM
    cross_query: PLACED
    cross_query_bias: VMEM
    cross_key: PLACED
    cross_value: PLACED
    cross_value_bias: VMEM
    cross_output: PLACED
    cross_output_bias: VMEM
    feed_norm_gain: VMEM
    feed_norm_bias: VMEM
    feed_in: PLACED
    feed_in_bias: VMEM
    feed_out: PLACED
    feed_out_bias: VMEM


AT_LAYER, AT_RESIDUES, AT_MEMORY, AT_SQUARE, AT_IN, AT_OUT, AT_VECTORS = 0, 128, 256, 384, 640, 768, 896
RESULT_ROWS = AT_VECTORS + VECTOR_ROWS


class Scratch(typing.NamedTuple):
    final: pltpu.VMEM((RESULT_ROWS, WIDE), F32)
    w_square: pltpu.VMEM((8, WIDE, WIDE), BF16)
    w_in: pltpu.VMEM((WIDE, HIDDEN), BF16)
    w_out: pltpu.VMEM((HIDDEN, WIDE), BF16)
    kv_out: pltpu.VMEM((2, CHIPS, BLOCK, BLOCK), BF16)
    kv: pltpu.VMEM((2, 2 * CHIPS, BLOCK, BLOCK), BF16)
    narrow_out: pltpu.VMEM((8, CHIPS, HALF, BLOCK), BF16)
    narrow: pltpu.VMEM((8, CHIPS, HALF, BLOCK), BF16)
    dkv_out: pltpu.VMEM((2, CHIPS, BLOCK, BLOCK), BF16)
    dkv: pltpu.VMEM((2, CHIPS, BLOCK, BLOCK), BF16)
    dkv_part: pltpu.VMEM((2, CHIPS, 2, BLOCK, BLOCK), BF16)
    dkv_other: pltpu.VMEM((2, CHIPS, BLOCK, BLOCK), BF16)
    dkv_sum: pltpu.VMEM((2048, BLOCK), F32)
    q_rows: pltpu.VMEM((2, 1024, BLOCK), BF16)
    q_features: pltpu.VMEM((2, 1024, BLOCK), BF16)
    do_rows: pltpu.VMEM((2, 1024, BLOCK), BF16)
    o_rows: pltpu.VMEM((2, 1024, BLOCK), F32)
    do_features: pltpu.VMEM((1024, BLOCK), BF16)
    query_features: pltpu.VMEM((1024, BLOCK), BF16)
    key_features: pltpu.VMEM((2048, BLOCK), BF16)
    causal: pltpu.VMEM((256, 512), F32)
    causal_turned: pltpu.VMEM((512, 256), F32)
    scores: pltpu.VMEM((256, 2048), F32)
    units: pltpu.VMEM((3, BLOCK, WIDE), F32)
    factors: pltpu.VMEM((3, BLOCK, BLOCK), F32)
    normed: pltpu.VMEM((3, BLOCK, WIDE), BF16)
    attended: pltpu.VMEM((2, BLOCK, WIDE), BF16)
    upstream: pltpu.VMEM((BLOCK, WIDE), F32)
    grad_active: pltpu.VMEM((BLOCK, HIDDEN), F32)
    active: pltpu.VMEM((BLOCK, HIDDEN), BF16)
    grad_inner: pltpu.VMEM((BLOCK, HIDDEN), BF16)
    parts: pltpu.VMEM((UNITS, 4, 2, 2, 2, ROUND, WIDE), BF16)
    by_core: pltpu.VMEM((UNITS, 4, 2, 2, ROUND, WIDE), BF16)
    by_side: pltpu.VMEM((UNITS, 4, 2, ROUND, WIDE), BF16)
    by_column: pltpu.VMEM((UNITS, 4, ROUND, WIDE), BF16)
    by_plane: pltpu.VMEM((3, UNITS, ROUND, WIDE), BF16)
    halves: pltpu.VMEM((2, UNITS, ROUND, WIDE), BF16)
    vectors: pltpu.VMEM((VECTOR_ROWS, WIDE), F32)
    vec_in: pltpu.VMEM((3, VECTOR_ROWS, WIDE), F32)
    vec_sum: pltpu.VMEM((2, VECTOR_ROWS, WIDE), F32)
    vec_planes: pltpu.VMEM((4, VECTOR_ROWS, WIDE), F32)
    load_sems: pltpu.SemaphoreType.DMA((10,))
    narrow_sems: pltpu.SemaphoreType.DMA((2, 8, CHIPS))
    kv_sems: pltpu.SemaphoreType.DMA((2, 2, CHIPS))
    dkv_sems: pltpu.SemaphoreType.DMA((2, 2, CHIPS))
    pass_sems: pltpu.SemaphoreType.DMA((2, 2, CHIPS))
    share_sems: pltpu.SemaphoreType.DMA((2, 2))
    reduce_sems: pltpu.SemaphoreType.DMA((2, 3, 7))
    vec_sems: pltpu.SemaphoreType.DMA((2, 6))
    final_sems: pltpu.SemaphoreType.DMA((16,))


def specs_of(kind):
    return tuple(kind.__annotations__.values())


def dot_nn(left, right):
    return lax.dot_general(left, right, (((1,), (0,)), ((), ())), preferred_element_type=F32)


def dot_nt(left, right):
    return lax.dot_general(left, right, (((1,), (1,)), ((), ())), preferred_element_type=F32)


def dot_tn(left, right):
    return lax.dot_general(left, right, (((0,), (0,)), ((), ())), preferred_element_type=F32)


def low_lanes(shape):
    return lax.broadcasted_iota(jnp.int32, shape, len(shape) - 1) < HEAD


def turn(block):
    return pltpu.roll(block, HEAD, 1)


def swap(first, second):
    keep = low_lanes(first.shape)
    return jnp.where(keep, first, turn(second)), jnp.where(keep, turn(first), second)


def column_sum(low):
    return jnp.sum(low.astype(F32), 0, keepdims=True)


def flat(ref):
    return ref[...].reshape(1, -1)


def fused_kernel(*refs):
    count = len(specs_of(Operands))
    a, result, s = Operands(*refs[:count]), refs[count], Scratch(*refs[count + 1 :])

    rank = lax.axis_index("blk")
    side = lax.axis_index("batch")
    chip, core = lax.div(rank, 2), lax.rem(rank, 2)
    plane, column = lax.div(chip, 2), lax.rem(chip, 2)

    def around(shift):
        return lax.rem(chip + (CHIPS + shift), CHIPS)

    def at_rank(index):
        return {"blk": index}

    partner = at_rank(2 * chip + 1 - core)
    beside = at_rank(2 * (2 * plane + 1 - column) + core)
    across = {"batch": 1 - side}

    def remote(src, dst, sems, device):
        return pltpu.make_async_remote_copy(
            src_ref=src, dst_ref=dst, send_sem=sems[0], recv_sem=sems[1], device_id=device, device_id_type=MESH
        )

    sent = []

    def send(make, *which):
        make(*which).start()
        sent.append(functools.partial(make, *which))

    finished = []

    def final_put(at, values):
        s.final[pl.ds(at, values.shape[0]), : values.shape[1]] = values

    def final_start(at, rows):
        span = pl.ds(at, rows)
        finished.append(pltpu.make_async_copy(s.final.at[span], result.at[span], s.final_sems.at[len(finished)]))
        finished[-1].start()

    loads = {}
    for at, (source, target) in enumerate(
        (
            (a.self_key, s.w_square.at[SK]), (a.self_value, s.w_square.at[SV]), (a.self_query, s.w_square.at[SQ]),
            (a.cross_key, s.w_square.at[CK]), (a.cross_value, s.w_square.at[CV]), (a.feed_out, s.w_out),
            (a.self_output, s.w_square.at[SO]), (a.cross_query, s.w_square.at[CQ]),
            (a.cross_output, s.w_square.at[CO]), (a.feed_in, s.w_in),
        )
    ):
        copy = pltpu.make_async_copy(source, target, s.load_sems.at[at])
        copy.start()
        loads[(SK, SV, SQ, CK, CV, 8, SO, CQ, CO, 9)[at]] = copy

    def weight(which):
        if which in loads:
            loads.pop(which).wait()
        return s.w_square[which] if which < 8 else (s.w_out, s.w_in)[which - 8]

    barrier = pltpu.get_barrier_semaphore()
    for shift in range(1, CHIPS):
        pl.semaphore_signal(barrier, inc=1, device_id=at_rank(2 * around(shift) + core), device_id_type=MESH)
    pl.semaphore_signal(barrier, inc=1, device_id=partner, device_id_type=MESH)
    pl.semaphore_signal(barrier, inc=1, device_id=across, device_id_type=MESH)

    class Exchange:
        def __init__(self, outgoing, incoming, sems, which, by_token=False):
            self.outgoing, self.incoming, self.by_token = outgoing.at[which], incoming.at[which], by_token
            self.sems = lambda shift: (sems.at[0, which, shift], sems.at[1, which, shift])

        def slot(self, source):
            return self.incoming.at[2 * source + core if self.by_token else source]

        def copy(self, shift):
            to = around(shift)
            return remote(self.outgoing.at[to], self.slot(chip), self.sems(shift), at_rank(2 * to + core))

        def start(self):
            for shift in range(1, CHIPS):
                send(self.copy, shift)
            self.slot(chip)[...] = self.outgoing[chip]

        def wait(self, shift):
            source = around(-shift)
            remote(
                self.outgoing.at[source], self.slot(source), self.sems(shift), at_rank(2 * source + core)
            ).wait_recv()

        def wait_all(self):
            for shift in range(1, CHIPS):
                self.wait(shift)

    narrow = [Exchange(s.narrow_out, s.narrow, s.narrow_sems, which) for which in range(8)]
    keys_values = [Exchange(s.kv_out, s.kv, s.kv_sems, which, True) for which in (SELF, CROSS)]
    key_grads = [Exchange(s.dkv_out, s.dkv, s.dkv_sems, which) for which in (SELF, CROSS)]

    def pass_copy(kind, shift, which_core):
        slot = s.kv.at[kind, 2 * around(-shift) + which_core]
        return remote(slot, slot, (s.pass_sems.at[0, kind, shift], s.pass_sems.at[1, kind, shift]), partner)

    def pass_on(kind):
        for shift in range(CHIPS):
            if shift > 0:
                keys_values[kind].wait(shift)
            send(pass_copy, kind, shift, core)

    def pass_wait(kind):
        for shift in range(CHIPS):
            pass_copy(kind, shift, 1 - core).wait_recv()

    def pack_groups(matrix, which):
        for pair in range(CHIPS // 2):
            group = matrix[:, BLOCK * pair : BLOCK * (pair + 1)]
            one, two = swap(group[:HALF], group[HALF:])
            s.narrow_out[which, 2 * pair] = one.astype(BF16)
            s.narrow_out[which, 2 * pair + 1] = two.astype(BF16)

    def unpack_groups(which):
        groups = []
        for pair in range(CHIPS // 2):
            groups.append(
                jnp.concatenate(
                    swap(s.narrow[which, 2 * pair].astype(F32), s.narrow[which, 2 * pair + 1].astype(F32)), 0
                )
            )
        return jnp.concatenate(groups, 1).astype(BF16)

    def pack_pairs(keys, values, kind):
        for pair in range(CHIPS // 2):
            lanes = slice(BLOCK * pair, BLOCK * (pair + 1))
            one, two = swap(keys[:, lanes], values[:, lanes])
            s.kv_out[kind, 2 * pair] = one.astype(BF16)
            s.kv_out[kind, 2 * pair + 1] = two.astype(BF16)

    def unpack_pairs(kind):
        pairs = [
            swap(s.dkv[kind, 2 * pair].astype(F32), s.dkv[kind, 2 * pair + 1].astype(F32)) for pair in range(CHIPS // 2)
        ]
        return tuple(jnp.concatenate(each, 1).astype(BF16) for each in zip(*pairs, strict=True))

    def reduce_copy(stage, group):
        first, last = SPANS[group]
        span = pl.ds(first, last - first)
        sems = (s.reduce_sems.at[0, group, stage], s.reduce_sems.at[1, group, stage])
        if stage == 0:
            return remote(s.parts.at[span, :, :, 1 - core], s.by_core.at[span], sems, partner)
        if stage == 1:
            return remote(s.by_core.at[span, :, :, 1 - side], s.by_side.at[span], sems, across)
        if stage == 2:
            return remote(s.by_side.at[span, :, 1 - column], s.by_column.at[span], sems, beside)
        if stage < 6:
            to = lax.rem(plane + (stage - 2), 4)
            return remote(
                s.by_column.at[span, to], s.by_plane.at[stage - 3, span], sems, at_rank(2 * (2 * to + column) + core)
            )
        return remote(s.halves.at[side, span], s.halves.at[side, span], sems, across)

    def reduce_start(stage, group):
        for each in (3, 4, 5) if stage == 3 else (stage,):
            send(reduce_copy, each, group)

    def reduce_finish(stage, group):
        first, last = SPANS[group]
        for each in (3, 4, 5) if stage == 3 else (stage,):
            if each == 6:
                half = s.halves.at[1 - side, pl.ds(first, last - first)]
                remote(half, half, (s.reduce_sems.at[0, group, 6], s.reduce_sems.at[1, group, 6]), across).wait_recv()
            else:
                reduce_copy(each, group).wait_recv()

        def add(unit, nothing):
            if stage == 0:
                s.by_core[unit] = s.by_core[unit] + s.parts[unit, :, :, core]
            if stage == 1:
                s.by_side[unit] = s.by_side[unit] + s.by_core[unit, :, :, side]
            if stage == 2:
                s.by_column[unit] = s.by_column[unit] + s.by_side[unit, :, column]
            if stage == 3:
                total = s.by_column[unit, plane].astype(F32)
                for each in range(3):
                    total = total + s.by_plane[each, unit].astype(F32)
                s.halves[side, unit] = total.astype(BF16)
            return nothing

        if stage < 6:
            lax.fori_loop(first, last, add, 0)

    def reduce_step(stage, group):
        reduce_finish(stage, group)
        reduce_start(stage + 1 if stage < 3 else 6, group)

    def put_unit(unit, value):
        s.parts[unit] = value.astype(BF16).reshape(4, 2, 2, 2, ROUND, WIDE)

    def put_vector(row, values):
        for piece in range(values.shape[1] // WIDE):
            s.vectors[pl.ds(row + piece, 1), :] = values[:, piece * WIDE : (piece + 1) * WIDE]

    def norm(values, which, gain, shift):
        average = jnp.mean(values, -1, keepdims=True)
        centred = values - average
        factor = lax.rsqrt(jnp.mean(centred * centred, -1, keepdims=True) + EPS)
        normal = centred * factor
        s.units[which] = normal
        s.factors[which] = jnp.broadcast_to(factor, (BLOCK, BLOCK))
        low = (normal * flat(gain) + flat(shift)).astype(BF16)
        s.normed[which] = low
        return low

    def norm_gradient(gradient, which, gain, row):
        normal = s.units[which]
        weighted = gradient * flat(gain)
        one = jnp.mean(weighted, -1, keepdims=True)
        two = jnp.mean(weighted * normal, -1, keepdims=True)
        put_vector(row, jnp.sum(gradient * normal, 0, keepdims=True))
        put_vector(row + 1, jnp.sum(gradient, 0, keepdims=True))
        return s.factors[which][:, :1] * (weighted - one - normal * two)

    def query_rows(which, target, low_half):
        keep = low_lanes((HALF, BLOCK))

        def one(block, nothing):
            piece = s.narrow[which, block].astype(F32)
            rolled = turn(piece)
            if low_half:
                top, bottom = jnp.where(keep, piece, 0.0), jnp.where(keep, rolled, 0.0)
            else:
                top, bottom = jnp.where(keep, 0.0, rolled), jnp.where(keep, 0.0, piece)
            target[pl.ds(block * BLOCK, BLOCK), :] = jnp.concatenate([top, bottom], 0).astype(BF16)
            return nothing

        lax.fori_loop(0, CHIPS, one, 0)

    def key_block(kind, chunk):
        rows = s.kv[kind, pl.ds(4 * chunk, 4)].reshape(512, BLOCK)
        return jnp.concatenate([rows, s.key_features[pl.ds(512 * chunk, 512), :]], 1)

    def with_column(features, column_values):
        lane = lax.broadcasted_iota(jnp.int32, features.shape, 1)
        full = jnp.broadcast_to(column_values, features.shape)
        high = full.astype(BF16).astype(F32)
        middle = (full - high).astype(BF16).astype(F32)
        low = full - high - middle
        for at, piece in enumerate((high, middle, low)):
            features = jnp.where(lane == ONES_LANE + at, piece, features)
        return features.astype(BF16)

    def attend(kind, causal, which):
        def part_of(part, pieces):
            rows = pl.ds(part * 256, 256)
            queries = jnp.concatenate([s.q_rows[kind, rows, :], s.query_features[rows, :]], 1)
            highest = None
            for chunk in range(pieces):
                scores = dot_nt(queries, key_block(kind, chunk))
                if causal and chunk == pieces - 1:
                    scores = scores + s.causal[...]
                s.scores[:, 512 * chunk : 512 * (chunk + 1)] = scores
                for at in range(4):
                    piece = scores[:, BLOCK * at : BLOCK * (at + 1)]
                    highest = piece if highest is None else jnp.maximum(highest, piece)
            highest = jnp.max(highest, 1, keepdims=True)
            summed = None
            for chunk in range(pieces):
                weights = jnp.exp(s.scores[:, 512 * chunk : 512 * (chunk + 1)] - highest).astype(BF16)
                piece = dot_nn(weights, key_block(kind, chunk))
                summed = piece if summed is None else summed + piece
            total = summed[:, BLOCK + ONES_LANE : BLOCK + ONES_LANE + 1]
            result = summed[:, :BLOCK] / total
            s.o_rows[kind, rows, :] = result
            s.q_features[kind, rows, :] = with_column(
                s.query_features[rows, :].astype(F32), -(highest + jnp.log(total))
            )
            keep = low_lanes((HALF, BLOCK))
            for half in range(2):
                block = result[BLOCK * half : BLOCK * (half + 1)]
                s.narrow_out[which, 2 * part + half] = jnp.where(keep, turn(block[:HALF]), block[HALF:]).astype(BF16)

        if causal:
            for part in range(4):
                part_of(part, part + 1)
        else:

            def loop(part, nothing):
                part_of(part, 4)
                return nothing

            lax.fori_loop(0, 4, loop, 0)

    def attend_back(kind, causal, which_in, which_out):
        query_rows(which_in, s.do_rows.at[kind], False)

        def spreads(part, nothing):
            rows = pl.ds(part * 256, 256)
            spread = jnp.sum(s.do_rows[kind, rows, :].astype(F32) * s.o_rows[kind, rows, :], 1, keepdims=True)
            s.do_features[rows, :] = with_column(jnp.zeros((256, BLOCK), F32), -spread)
            return nothing

        lax.fori_loop(0, 4, spreads, 0)

        def one(part, chunk, diagonal):
            rows = pl.ds(part * 256, 256)
            keys = key_block(kind, chunk)
            queries, grads = s.q_rows[kind, rows, :], s.do_rows[kind, rows, :]
            scores = dot_nt(keys, jnp.concatenate([queries, s.q_features[kind, rows, :]], 1))
            if diagonal:
                scores = scores + s.causal_turned[...]
            weights = jnp.exp(scores)
            slopes = dot_nt(keys, jnp.concatenate([grads, s.do_features[rows, :]], 1))
            tilted = (weights * slopes).astype(BF16)
            shares = dot_nn(tilted, queries) + dot_nn(weights.astype(BF16), grads)
            return shares, dot_tn(tilted, keys[:, :BLOCK])

        def part_of(part, pieces):
            total = None
            for chunk in range(pieces):
                shares, toward = one(part, chunk, causal and chunk == pieces - 1)
                where = pl.ds(512 * chunk, 512)
                if causal and part == chunk:
                    s.dkv_sum[where, :] = shares
                else:
                    s.dkv_sum[where, :] = s.dkv_sum[where, :] + shares
                total = toward if total is None else total + toward
            total = total * (HEAD**-0.5)
            keep = low_lanes((HALF, BLOCK))
            for half in range(2):
                block = total[BLOCK * half : BLOCK * (half + 1)]
                s.narrow_out[which_out, 2 * part + half] = jnp.where(keep, block[:HALF], turn(block[HALF:])).astype(
                    BF16
                )

        if causal:
            for part in range(4):
                part_of(part, part + 1)
        else:
            s.dkv_sum[...] = jnp.zeros(s.dkv_sum.shape, F32)

            def loop(part, nothing):
                part_of(part, 4)
                return nothing

            lax.fori_loop(0, 4, loop, 0)
        s.dkv_part[kind] = s.dkv_sum[...].astype(BF16).reshape(CHIPS, 2, BLOCK, BLOCK)

    def share_copy(kind):
        return remote(
            s.dkv_part.at[kind, :, 1 - core], s.dkv_other.at[kind], (s.share_sems.at[0, kind], s.share_sems.at[1, kind]),
            partner,
        )

    def share_finish(kind):
        share_copy(kind).wait_recv()
        s.dkv_out[kind] = s.dkv_part[kind, :, core] + s.dkv_other[kind]

    inputs = a.residues[...].astype(F32)
    normed = norm(inputs, 0, a.self_norm_gain, a.self_norm_bias)
    keys = dot_nn(normed, weight(SK))
    values = dot_nn(normed, weight(SV)) + flat(a.self_value_bias)
    pack_pairs(keys, values, SELF)
    pl.semaphore_wait(barrier, CHIPS + 1)
    keys_values[SELF].start()
    queries = (dot_nn(normed, weight(SQ)) + flat(a.self_query_bias)) * (HEAD**-0.5)
    pack_groups(queries, X_SQ)
    narrow[X_SQ].start()

    encoded = a.memory[...]
    keys = dot_nn(encoded, weight(CK))
    values = dot_nn(encoded, weight(CV)) + flat(a.cross_value_bias)
    pack_pairs(keys, values, CROSS)

    bounds, reach = [], 0
    for at in range(4):
        reach = reach + a.lengths[0, at]
        bounds.append(reach)
    lane = lax.broadcasted_iota(jnp.int32, (BLOCK, BLOCK), 1)
    row = lax.broadcasted_iota(jnp.int32, (BLOCK, BLOCK), 0)

    def documents(position):
        found = jnp.zeros((BLOCK, BLOCK), jnp.int32)
        for bound in bounds:
            found = found + (position >= bound).astype(jnp.int32)
        return found

    ones = jnp.where((lane >= ONES_LANE) & (lane < ONES_LANE + 3), 1.0, 0.0)

    def key_features(block, nothing):
        other = documents(row + block * BLOCK) != lane
        s.key_features[pl.ds(block * BLOCK, BLOCK), :] = jnp.where((lane < ONES_LANE) & other, MASKED, ones).astype(
            BF16
        )
        return nothing

    lax.fori_loop(0, 2 * CHIPS, key_features, 0)

    def query_features(block, nothing):
        same = documents(row + (2 * block + core) * BLOCK) == lane
        s.query_features[pl.ds(block * BLOCK, BLOCK), :] = jnp.where((lane < ONES_LANE) & same, 1.0, 0.0).astype(BF16)
        return nothing

    lax.fori_loop(0, CHIPS, query_features, 0)

    def query_place(at):
        return at + core * BLOCK + jnp.where(at >= BLOCK, BLOCK, 0)

    at_row = lax.broadcasted_iota(jnp.int32, (256, 512), 0)
    at_key = lax.broadcasted_iota(jnp.int32, (256, 512), 1)
    s.causal[...] = jnp.where(at_key <= query_place(at_row), 0.0, MASKED)
    at_key = lax.broadcasted_iota(jnp.int32, (512, 256), 0)
    at_row = lax.broadcasted_iota(jnp.int32, (512, 256), 1)
    s.causal_turned[...] = jnp.where(at_key <= query_place(at_row), 0.0, MASKED)
    pass_on(SELF)
    keys_values[CROSS].start()
    narrow[X_SQ].wait_all()
    query_rows(X_SQ, s.q_rows.at[SELF], True)
    pass_wait(SELF)
    attend(SELF, True, X_SO)
    narrow[X_SO].start()
    grads = a.cotangent[...]
    weight(8)
    for piece in range(4):
        lanes = slice(512 * piece, 512 * (piece + 1))
        s.grad_active[:, lanes] = dot_nt(grads, s.w_out[lanes, :])
    pass_on(CROSS)
    narrow[X_SO].wait_all()
    self_low = unpack_groups(X_SO)
    s.attended[SELF] = self_low
    after_self = inputs + dot_nn(self_low, weight(SO)) + flat(a.self_output_bias)

    normed = norm(after_self, 1, a.cross_norm_gain, a.cross_norm_bias)
    queries = (dot_nn(normed, weight(CQ)) + flat(a.cross_query_bias)) * (HEAD**-0.5)
    pack_groups(queries, X_CQ)
    narrow[X_CQ].start()
    pass_wait(CROSS)
    narrow[X_CQ].wait_all()
    query_rows(X_CQ, s.q_rows.at[CROSS], True)
    attend(CROSS, False, X_CO)
    narrow[X_CO].start()
    weight(9)
    narrow[X_CO].wait_all()
    cross_low = unpack_groups(X_CO)
    s.attended[CROSS] = cross_low
    after_cross = after_self + dot_nn(cross_low, weight(CO)) + flat(a.cross_output_bias)

    normed = norm(after_cross, 2, a.feed_norm_gain, a.feed_norm_bias)
    layer_out, back = after_cross + flat(a.feed_out_bias), None
    for piece in range(4):
        lanes = slice(512 * piece, 512 * (piece + 1))
        inner = dot_nn(normed, s.w_in[:, lanes]) + flat(a.feed_in_bias)[:, lanes]
        bell = 0.5 * (1.0 + lax.erf(inner * SQRT_HALF))
        active = (inner * bell).astype(BF16)
        slope = bell + inner * jnp.exp(-0.5 * inner * inner) * INV_ROOT_TAU
        grad_inner = (s.grad_active[:, lanes] * slope).astype(BF16)
        s.active[:, lanes] = active
        s.grad_inner[:, lanes] = grad_inner
        layer_out = layer_out + dot_nn(active, s.w_out[lanes, :])
        toward = dot_nt(grad_inner, s.w_in[:, lanes])
        back = toward if back is None else back + toward
    final_put(AT_LAYER, layer_out)
    final_start(AT_LAYER, BLOCK)
    upstream = a.cotangent[...].astype(F32)
    upstream = upstream + norm_gradient(back, 2, a.feed_norm_gain, ROW_FEED_GAIN)

    branch = upstream.astype(BF16)
    pack_groups(dot_nt(branch, weight(CO)), X_CDO)
    narrow[X_CDO].start()
    s.upstream[...] = upstream
    put_vector(ROW_OUT, column_sum(a.cotangent[...]))
    put_vector(ROW_IN, column_sum(s.grad_inner[...]))
    put_vector(ROW_CO, column_sum(branch))
    for piece in range(4):
        lanes = slice(512 * piece, 512 * (piece + 1))
        part = dot_tn(s.active[:, lanes], a.cotangent[...]).astype(BF16).reshape(2, 2, 4, 2, ROUND, WIDE)
        for each in range(4):
            s.parts[UNIT_OUT + each, piece] = part[:, :, each]
        put_unit(UNIT_IN + piece, dot_tn(s.normed[2], s.grad_inner[:, lanes]))
    put_unit(UNIT_OF[CO], dot_tn(s.attended[CROSS], branch))
    reduce_start(0, 0)
    narrow[X_CDO].wait_all()
    attend_back(CROSS, False, X_CDO, X_CDQ)
    narrow[X_CDQ].start()
    send(share_copy, CROSS)
    reduce_step(0, 0)
    share_finish(CROSS)
    key_grads[CROSS].start()
    narrow[X_CDQ].wait_all()
    grad_query = unpack_groups(X_CDQ)
    gradient = dot_nt(grad_query, weight(CQ))
    upstream = s.upstream[...] + norm_gradient(gradient, 1, a.cross_norm_gain, ROW_CROSS_GAIN)

    branch = upstream.astype(BF16)
    pack_groups(dot_nt(branch, weight(SO)), X_SDO)
    narrow[X_SDO].start()
    s.upstream[...] = upstream
    put_vector(ROW_SO, column_sum(branch))
    put_vector(ROW_CQ, column_sum(grad_query))
    put_unit(UNIT_OF[SO], dot_tn(s.attended[SELF], branch))
    put_unit(UNIT_OF[CQ], dot_tn(s.normed[1], grad_query))
    key_grads[CROSS].wait_all()
    grad_key, grad_value = unpack_pairs(CROSS)
    put_vector(ROW_CV, column_sum(grad_value))
    put_unit(UNIT_OF[CK], dot_tn(a.memory[...], grad_key))
    put_unit(UNIT_OF[CV], dot_tn(a.memory[...], grad_value))
    reduce_start(0, 1)
    final_put(AT_MEMORY, dot_nt(grad_key, weight(CK)) + dot_nt(grad_value, weight(CV)))
    final_start(AT_MEMORY, BLOCK)
    narrow[X_SDO].wait_all()
    attend_back(SELF, True, X_SDO, X_SDQ)
    narrow[X_SDQ].start()
    send(share_copy, SELF)
    reduce_step(1, 0)
    reduce_step(0, 1)
    share_finish(SELF)
    key_grads[SELF].start()
    narrow[X_SDQ].wait_all()
    grad_query = unpack_groups(X_SDQ)
    key_grads[SELF].wait_all()
    grad_key, grad_value = unpack_pairs(SELF)
    normed = s.normed[0]
    put_unit(UNIT_OF[SQ], dot_tn(normed, grad_query))
    put_unit(UNIT_OF[SK], dot_tn(normed, grad_key))
    put_unit(UNIT_OF[SV], dot_tn(normed, grad_value))
    reduce_start(0, 2)
    put_vector(ROW_SQ, column_sum(grad_query))
    put_vector(ROW_SV, column_sum(grad_value))
    gradient = dot_nt(grad_query, weight(SQ)) + dot_nt(grad_key, weight(SK)) + dot_nt(grad_value, weight(SV))
    final_put(AT_RESIDUES, s.upstream[...] + norm_gradient(gradient, 0, a.self_norm_gain, ROW_SELF_GAIN))
    final_start(AT_RESIDUES, BLOCK)

    def vector_copy(stage):
        sems = (s.vec_sems.at[0, stage], s.vec_sems.at[1, stage])
        if stage == 0:
            return remote(s.vectors, s.vec_in.at[0], sems, partner)
        if stage == 1:
            return remote(s.vec_sum.at[0], s.vec_in.at[1], sems, across)
        if stage == 2:
            return remote(s.vec_sum.at[1], s.vec_in.at[2], sems, beside)
        to = lax.rem(plane + (stage - 2), 4)
        return remote(s.vec_planes.at[plane], s.vec_planes.at[plane], sems, at_rank(2 * (2 * to + column) + core))

    s.vectors[pl.ds(17, VECTOR_ROWS - 17), :] = jnp.zeros((VECTOR_ROWS - 17, WIDE), F32)
    send(vector_copy, 0)
    reduce_step(2, 0)
    reduce_step(1, 1)
    vector_copy(0).wait_recv()
    s.vec_sum[0] = s.vectors[...] + s.vec_in[0]
    send(vector_copy, 1)
    reduce_step(0, 2)
    reduce_step(3, 0)
    reduce_step(2, 1)
    vector_copy(1).wait_recv()
    s.vec_sum[1] = s.vec_sum[0] + s.vec_in[1]
    send(vector_copy, 2)
    reduce_step(1, 2)
    vector_copy(2).wait_recv()
    s.vec_planes[plane] = s.vec_sum[1] + s.vec_in[2]
    for stage in (3, 4, 5):
        send(vector_copy, stage)
    reduce_step(3, 1)
    reduce_step(2, 2)
    reduce_finish(6, 0)
    for stage in (3, 4, 5):
        source = lax.rem(plane + 4 - (stage - 2), 4)
        remote(
            s.vec_planes.at[plane], s.vec_planes.at[source], (s.vec_sems.at[0, stage], s.vec_sems.at[1, stage]), beside
        ).wait_recv()
    total = s.vec_planes[0]
    for each in range(1, 4):
        total = total + s.vec_planes[each]
    shares = pltpu.roll(total, lax.rem(WIDE - 32 * rank, WIDE), 1)[:, :BLOCK]
    turned = pltpu.roll(total, lax.rem(WIDE - BLOCK * lax.rem(rank, 4), WIDE), 1)[:, :BLOCK]
    own = jnp.zeros((1, BLOCK), F32)
    for each in range(4):
        own = own + jnp.where(lax.div(rank, 4) == each, turned[ROW_IN + each : ROW_IN + each + 1], 0.0)
    s.final[pl.ds(AT_VECTORS, VECTOR_ROWS), :BLOCK] = shares
    s.final[pl.ds(AT_VECTORS + ROW_IN, 1), :BLOCK] = own
    final_start(AT_VECTORS, VECTOR_ROWS)

    def unit_value(unit):
        return jnp.concatenate([s.halves[0, unit], s.halves[1, unit]], 0).astype(F32)

    def put_final_unit(at, unit):
        final_put(at, unit_value(unit))

    for piece in range(4):
        put_final_unit(AT_OUT + 32 * piece, UNIT_OUT + piece)
        put_final_unit(AT_IN + 32 * piece, UNIT_IN + piece)
    final_start(AT_IN, 2 * BLOCK)
    reduce_step(3, 2)
    reduce_finish(6, 1)
    for which in (CO, CQ, CK, CV, SO):
        put_final_unit(AT_SQUARE + 32 * which, UNIT_OF[which])
    reduce_finish(6, 2)
    for which in (SQ, SK, SV):
        put_final_unit(AT_SQUARE + 32 * which, UNIT_OF[which])
    final_start(AT_SQUARE, 256)
    for copy in finished:
        copy.wait()
    for make in sent:
        make().wait_send()


def place_kernel(packed, *refs):
    results, vectors, sems = refs[:-2], refs[-2], refs[-1]
    copies = []

    def place(at, target):
        source = packed.at[pl.ds(at, target.shape[0]), pl.ds(0, target.shape[1])]
        copies.append(pltpu.make_async_copy(source, target, sems.at[len(copies)]))
        copies[-1].start()

    place(AT_VECTORS, vectors)
    for at, target in zip((AT_LAYER, AT_RESIDUES, AT_MEMORY), results[:3], strict=True):
        place(at, target)
    for which, at in SQUARE_RESULTS.items():
        place(AT_SQUARE + 32 * which, results[at])
    for piece in range(4):
        place(AT_IN + 32 * piece, results[23].at[:, pl.ds(512 * piece, 512)])
    place(AT_OUT, results[25])
    copies[0].wait()
    rows = vectors[...]
    for row, at in VECTOR_RESULTS.items():
        results[at][...] = rows[row, : results[at].shape[0]]
    for copy in copies[1:]:
        copy.wait()


SQUARE_RESULTS = {SQ: 5, SK: 7, SV: 8, SO: 10, CQ: 14, CK: 16, CV: 17, CO: 19}
VECTOR_RESULTS = {
    ROW_SELF_GAIN: 3, ROW_SELF_SHIFT: 4, ROW_SQ: 6, ROW_SV: 9, ROW_SO: 11, ROW_CROSS_GAIN: 12, ROW_CROSS_SHIFT: 13,
    ROW_CQ: 15, ROW_CV: 18, ROW_CO: 20, ROW_FEED_GAIN: 21, ROW_FEED_SHIFT: 22, ROW_OUT: 26, ROW_IN: 24,
}


def fused(residues, memory, lengths, cotangent, *parameters):
    packed = pl.pallas_call(
        fused_kernel,
        out_shape=jax.ShapeDtypeStruct((RESULT_ROWS, WIDE), F32),
        in_specs=specs_of(Operands),
        out_specs=PLACED,
        scratch_shapes=specs_of(Scratch),
        compiler_params=pltpu.CompilerParams(
            collective_id=0, has_side_effects=True, vmem_limit_bytes=60 * 1024 * 1024
        ),
    )(residues[0], memory[0], lengths, cotangent[0], *parameters)
    shapes = [jax.ShapeDtypeStruct((BLOCK, WIDE), F32)] * 3
    for parameter in parameters:
        shapes.append(jax.ShapeDtypeStruct((parameter.shape[0] // (2 * CHIPS),) + parameter.shape[1:], F32))
    results = pl.pallas_call(
        place_kernel,
        out_shape=shapes,
        in_specs=(PLACED,),
        out_specs=(VMEM,) * len(shapes),
        scratch_shapes=(pltpu.VMEM((VECTOR_ROWS, BLOCK), F32), pltpu.SemaphoreType.DMA((17,))),
        compiler_params=pltpu.CompilerParams(vmem_limit_bytes=60 * 1024 * 1024),
    )(packed)
    return tuple(each[None] for each in results[:3]) + tuple(results[3:])


def solution(mesh):
    fits = mesh.shape["blk"] == 2 * CHIPS and mesh.shape["batch"] == 2
    return jax.shard_map(
        fused if fits else local,
        mesh=mesh,
        in_specs=(
            P("batch", "blk", None),
            P("batch", "blk", None),
            P("batch", None),
            P("batch", "blk", None),
            P(),
            P(),
            P(),
            P(),
            P(),
            P(),
            P(),
            P(),
            P(),
            P(),
            P(),
            P(),
            P(),
            P(),
            P(),
            P(),
            P(),
            P(),
            P(),
            P(),
            P(),
            P(),
            P(),
            P(),
        ),
        out_specs=(
            P("batch", "blk", None),
            P("batch", "blk", None),
            P("batch", "blk", None),
            P("blk"),
            P("blk"),
            P("blk", None),
            P("blk"),
            P("blk", None),
            P("blk", None),
            P("blk"),
            P("blk", None),
            P("blk"),
            P("blk"),
            P("blk"),
            P("blk", None),
            P("blk"),
            P("blk", None),
            P("blk", None),
            P("blk"),
            P("blk", None),
            P("blk"),
            P("blk"),
            P("blk"),
            P("blk", None),
            P("blk"),
            P("blk", None),
            P("blk"),
        ),
        check_vma=False,
    )
```

```python
import typing

import jax
import jax.numpy as jnp
from jax import lax
from jax.experimental import pallas as pl
from jax.experimental.pallas import tpu as pltpu
from jax.sharding import PartitionSpec as P

HEADS = 8


NEG = -1e30
EPS = 1e-05
SQRT_HALF = 0.7071067811865476
INV_ROOT_TAU = 0.3989422804014327


def layer_norm(values, gain, shift):
    average = jnp.mean(values, -1, keepdims=True)
    centred = values - average
    factor = lax.rsqrt(jnp.mean(centred * centred, -1, keepdims=True) + EPS)
    normal = centred * factor
    return (normal * gain + shift, normal, factor)


def norm_back(gradient, normal, factor, gain):
    weighted = gradient * gain
    average_one = jnp.mean(weighted, -1, keepdims=True)
    average_two = jnp.mean(weighted * normal, -1, keepdims=True)
    return (
        factor * (weighted - average_one - normal * average_two),
        jnp.sum(gradient * normal, 0),
        jnp.sum(gradient, 0),
    )


def gelu_value(values):
    return 0.5 * values * (1.0 + lax.erf(values * SQRT_HALF))


def gelu_slope(values):
    return (
        0.5 * (1.0 + lax.erf(values * SQRT_HALF))
        + values * jnp.exp(-0.5 * values * values) * INV_ROOT_TAU
    )


def heads_of(matrix):
    return matrix.reshape(matrix.shape[0], HEADS, -1)


def complex_ids(lengths_row, positions):
    bounds = jnp.cumsum(lengths_row)
    return jnp.sum((positions[:, None] >= bounds[None, :]).astype(jnp.int32), 1)


def visible(query_pos, query_doc, key_pos, key_doc, causal):
    allowed = query_doc[:, None] == key_doc[None, :]
    if causal:
        allowed = allowed & (key_pos[None, :] <= query_pos[:, None])
    return allowed


def project(left, right):
    return jnp.dot(left, right, preferred_element_type=jnp.float32)


def pass_through(pieces):
    return (pieces[0].astype(jnp.bfloat16), pieces[1].astype(jnp.bfloat16))


def empty_state(tokens, head_size):
    return (
        jnp.full((HEADS, tokens), NEG, jnp.float32),
        jnp.zeros((HEADS, tokens), jnp.float32),
        jnp.zeros((HEADS, tokens, head_size), jnp.float32),
    )


def finish(state_out):
    running_max, running_sum, summed = state_out
    attended = (summed / running_sum[..., None]).transpose(1, 0, 2)
    return (attended.reshape(attended.shape[0], -1), (running_max + jnp.log(running_sum)).T)


def spread_of(grad_low, attended):
    return jnp.sum(heads_of(grad_low).astype(jnp.float32) * heads_of(attended), -1)


def forward_fold(queries, query_pos, query_doc, lengths_row, causal, prepare, carried, pieces):
    factor = queries.shape[-1] ** (-0.5)
    piece_rows = pieces[0].shape[0]
    key_pos = jnp.arange(piece_rows, dtype=jnp.int32)
    allowed = visible(query_pos, query_doc, key_pos, complex_ids(lengths_row, key_pos), causal)

    def active(state_in):
        running_max, running_sum, summed = state_in
        key_rows, value_rows = prepare(pieces)
        scores = (
            jnp.einsum(
                "qhd,khd->hqk", queries, heads_of(key_rows), preferred_element_type=jnp.float32
            )
            * factor
        )
        scores = jnp.where(allowed[None], scores, NEG)
        new_max = jnp.maximum(running_max, jnp.max(scores, -1))
        weights = jnp.where(allowed[None], jnp.exp(scores - new_max[..., None]), 0.0)
        running_sum = jnp.sum(weights, -1)
        summed = jnp.einsum(
            "hqk,khd->hqd",
            weights.astype(jnp.bfloat16),
            heads_of(value_rows),
            preferred_element_type=jnp.float32,
        )
        return (new_max, running_sum, summed)

    return lax.cond(jnp.any(allowed), active, lambda state_in: state_in, carried)


def query_fold(
    queries, grad_out, log_total, spread, query_pos, query_doc, lengths_row, causal, prepare
):
    factor = queries.shape[-1] ** (-0.5)
    log_rows = log_total.T[..., None]
    spread_rows = spread.T[..., None]

    def fold(carried, pieces, offset):
        piece_rows = pieces[0].shape[0]
        key_pos = jnp.arange(piece_rows, dtype=jnp.int32)
        allowed = visible(query_pos, query_doc, key_pos, complex_ids(lengths_row, key_pos), causal)

        def active(accum):
            key_rows, value_rows = prepare(pieces)
            key_heads = heads_of(key_rows)
            scores = (
                jnp.einsum("qhd,khd->hqk", queries, key_heads, preferred_element_type=jnp.float32)
                * factor
            )
            scores = jnp.where(allowed[None], scores, NEG)
            weights = jnp.where(allowed[None], jnp.exp(scores - log_rows), 0.0)
            slopes = jnp.einsum(
                "qhd,khd->hqk", grad_out, heads_of(value_rows), preferred_element_type=jnp.float32
            )
            tilted = (weights * (slopes - spread_rows)).astype(jnp.bfloat16)
            return (
                jnp.einsum("hqk,khd->qhd", tilted, key_heads, preferred_element_type=jnp.float32)
                * factor
            )

        return lax.cond(jnp.any(allowed), active, lambda accum: accum, carried)

    return fold


def key_fold(key_heads, value_heads, key_pos, key_doc, lengths_row, causal):
    factor = key_heads.shape[-1] ** (-0.5)

    def fold(carried, pieces, offset):
        queries, grad_out, log_total, spread = pieces
        piece_rows = queries.shape[0]
        query_pos = jnp.arange(piece_rows, dtype=jnp.int32)
        allowed = visible(query_pos, complex_ids(lengths_row, query_pos), key_pos, key_doc, causal)

        def active(sums_in):
            query_heads = heads_of(queries.astype(jnp.bfloat16))
            grad_heads = heads_of(grad_out.astype(jnp.bfloat16))
            scores = (
                jnp.einsum(
                    "qhd,khd->hqk", query_heads, key_heads, preferred_element_type=jnp.float32
                )
                * factor
            )
            scores = jnp.where(allowed[None], scores, NEG)
            weights = jnp.where(allowed[None], jnp.exp(scores - log_total.T[..., None]), 0.0)
            grad_values = jnp.einsum(
                "hqk,qhd->khd",
                weights.astype(jnp.bfloat16),
                grad_heads,
                preferred_element_type=jnp.float32,
            )
            slopes = jnp.einsum(
                "qhd,khd->hqk", grad_heads, value_heads, preferred_element_type=jnp.float32
            )
            tilted = (weights * (slopes - spread.T[..., None])).astype(jnp.bfloat16)
            grad_keys = (
                jnp.einsum("hqk,qhd->khd", tilted, query_heads, preferred_element_type=jnp.float32)
                * factor
            )
            return (grad_keys, grad_values)

        return lax.cond(jnp.any(allowed), active, lambda sums_in: sums_in, carried)

    return fold


def mutual_fold(
    queries,
    grad_out,
    log_total,
    spread,
    key_heads,
    value_heads,
    positions,
    docs,
    lengths_row,
    carried,
    pieces,
    offset,
):
    toward_queries = query_fold(
        queries, grad_out, log_total, spread, positions, docs, lengths_row, True, pass_through
    )
    toward_keys = key_fold(key_heads, value_heads, positions, docs, lengths_row, True)
    grad_query_acc, grad_keys, grad_values = carried
    remote_q, remote_grad, remote_log, remote_spread, remote_k, remote_v = pieces
    grad_query_acc = toward_queries(grad_query_acc, (remote_k, remote_v), offset)
    grad_keys, grad_values = toward_keys(
        (grad_keys, grad_values), (remote_q, remote_grad, remote_log, remote_spread), offset
    )
    return (grad_query_acc, grad_keys, grad_values)


def local(
    residues,
    memory,
    lengths,
    cotangent,
    self_norm_gain,
    self_norm_bias,
    self_query,
    self_query_bias,
    self_key,
    self_value,
    self_value_bias,
    self_output,
    self_output_bias,
    cross_norm_gain,
    cross_norm_bias,
    cross_query,
    cross_query_bias,
    cross_key,
    cross_value,
    cross_value_bias,
    cross_output,
    cross_output_bias,
    feed_norm_gain,
    feed_norm_bias,
    feed_in,
    feed_in_bias,
    feed_out,
    feed_out_bias,
):
    tokens = residues.shape[1]
    model_width = residues.shape[2]
    head_size = model_width // HEADS
    device_rank = lax.axis_index("blk")
    positions = device_rank * tokens + jnp.arange(tokens, dtype=jnp.int32)
    lengths_row = lengths[0]
    complexes = complex_ids(lengths_row, positions)
    inputs = residues[0].astype(jnp.float32)
    encoded = memory[0]
    upstream = cotangent[0].astype(jnp.float32)
    normed_one, unit_one, factor_one = layer_norm(inputs, self_norm_gain, self_norm_bias)
    normed_one = normed_one.astype(jnp.bfloat16)
    self_q = (project(normed_one, self_query) + self_query_bias).astype(jnp.bfloat16)
    self_k = project(normed_one, self_key).astype(jnp.bfloat16)
    self_v = (project(normed_one, self_value) + self_value_bias).astype(jnp.bfloat16)
    state_out = forward_fold(
        heads_of(self_q),
        positions,
        complexes,
        lengths_row,
        True,
        pass_through,
        empty_state(tokens, head_size),
        (
            lax.all_gather(self_k, "blk", axis=0, tiled=True),
            lax.all_gather(self_v, "blk", axis=0, tiled=True),
        ),
    )
    self_attended, self_log = finish(state_out)
    self_low = self_attended.astype(jnp.bfloat16)
    after_self = inputs + project(self_low, self_output) + self_output_bias
    normed_two, unit_two, factor_two = layer_norm(after_self, cross_norm_gain, cross_norm_bias)
    normed_two = normed_two.astype(jnp.bfloat16)
    cross_q = (project(normed_two, cross_query) + cross_query_bias).astype(jnp.bfloat16)
    cross_k = project(encoded, cross_key).astype(jnp.bfloat16)
    cross_v = (project(encoded, cross_value) + cross_value_bias).astype(jnp.bfloat16)
    state_out = forward_fold(
        heads_of(cross_q),
        positions,
        complexes,
        lengths_row,
        False,
        pass_through,
        empty_state(tokens, head_size),
        (
            lax.all_gather(cross_k, "blk", axis=0, tiled=True),
            lax.all_gather(cross_v, "blk", axis=0, tiled=True),
        ),
    )
    cross_attended, cross_log = finish(state_out)
    cross_low = cross_attended.astype(jnp.bfloat16)
    after_cross = after_self + project(cross_low, cross_output) + cross_output_bias
    normed_three, unit_three, factor_three = layer_norm(after_cross, feed_norm_gain, feed_norm_bias)
    normed_three = normed_three.astype(jnp.bfloat16)
    inner = project(normed_three, feed_in) + feed_in_bias
    activation = gelu_value(inner).astype(jnp.bfloat16)
    layer_out = after_cross + project(activation, feed_out) + feed_out_bias
    grad_branch = upstream.astype(jnp.bfloat16)
    grad_feed_out_bias = jnp.sum(grad_branch.astype(jnp.float32), 0)
    grad_feed_out = jnp.einsum(
        "tf,td->fd", activation, grad_branch, preferred_element_type=jnp.float32
    )
    grad_active = jnp.einsum("td,fd->tf", grad_branch, feed_out, preferred_element_type=jnp.float32)
    grad_inner = (grad_active * gelu_slope(inner)).astype(jnp.bfloat16)
    grad_feed_in_bias = jnp.sum(grad_inner.astype(jnp.float32), 0)
    grad_feed_in = jnp.einsum(
        "td,tf->df", normed_three, grad_inner, preferred_element_type=jnp.float32
    )
    grad_normed = jnp.einsum("tf,df->td", grad_inner, feed_in, preferred_element_type=jnp.float32)
    norm_grad, grad_feed_norm_gain, grad_feed_norm_bias = norm_back(
        grad_normed, unit_three, factor_three, feed_norm_gain
    )
    upstream_two = upstream + norm_grad
    feed_parts = (
        grad_feed_norm_gain,
        grad_feed_norm_bias,
        grad_feed_in,
        grad_feed_in_bias,
        grad_feed_out,
        grad_feed_out_bias,
    )
    grad_branch = upstream_two.astype(jnp.bfloat16)
    grad_cross_output_bias = jnp.sum(grad_branch.astype(jnp.float32), 0)
    grad_cross_output = jnp.einsum(
        "tc,te->ce", cross_low, grad_branch, preferred_element_type=jnp.float32
    )
    grad_attended = jnp.einsum(
        "te,ce->tc", grad_branch, cross_output, preferred_element_type=jnp.float32
    ).astype(jnp.bfloat16)
    spread = spread_of(grad_attended, cross_attended)
    query_start = jnp.zeros((tokens, HEADS, head_size), jnp.float32)
    grad_query_acc = query_fold(
        heads_of(cross_q),
        heads_of(grad_attended),
        cross_log,
        spread,
        positions,
        complexes,
        lengths_row,
        False,
        pass_through,
    )(
        query_start,
        (
            lax.all_gather(cross_k, "blk", axis=0, tiled=True),
            lax.all_gather(cross_v, "blk", axis=0, tiled=True),
        ),
        jnp.int32(0),
    )
    grad_keys_acc, grad_values_acc = key_fold(
        heads_of(cross_k), heads_of(cross_v), positions, complexes, lengths_row, False
    )(
        (query_start, query_start),
        (
            lax.all_gather(cross_q.astype(jnp.float32), "blk", axis=0, tiled=True),
            lax.all_gather(grad_attended.astype(jnp.float32), "blk", axis=0, tiled=True),
            lax.all_gather(cross_log, "blk", axis=0, tiled=True),
            lax.all_gather(spread, "blk", axis=0, tiled=True),
        ),
        jnp.int32(0),
    )
    grad_cq = grad_query_acc.reshape(tokens, model_width).astype(jnp.bfloat16)
    grad_ck = grad_keys_acc.reshape(tokens, model_width).astype(jnp.bfloat16)
    grad_cv = grad_values_acc.reshape(tokens, model_width).astype(jnp.bfloat16)
    grad_cross_query = jnp.einsum(
        "tc,te->ce", normed_two, grad_cq, preferred_element_type=jnp.float32
    )
    grad_cross_query_bias = jnp.sum(grad_cq.astype(jnp.float32), 0)
    grad_cross_key = jnp.einsum("tc,te->ce", encoded, grad_ck, preferred_element_type=jnp.float32)
    grad_cross_value = jnp.einsum("tc,te->ce", encoded, grad_cv, preferred_element_type=jnp.float32)
    grad_cross_value_bias = jnp.sum(grad_cv.astype(jnp.float32), 0)
    memory_grad = jnp.einsum(
        "te,ce->tc", grad_ck, cross_key, preferred_element_type=jnp.float32
    ) + jnp.einsum("te,ce->tc", grad_cv, cross_value, preferred_element_type=jnp.float32)
    grad_normed = jnp.einsum("te,ce->tc", grad_cq, cross_query, preferred_element_type=jnp.float32)
    norm_grad, grad_cross_norm_gain, grad_cross_norm_bias = norm_back(
        grad_normed, unit_two, factor_two, cross_norm_gain
    )
    upstream_one = upstream_two + norm_grad
    cross_parts = (
        grad_cross_norm_gain,
        grad_cross_norm_bias,
        grad_cross_query,
        grad_cross_query_bias,
        grad_cross_key,
        grad_cross_value,
        grad_cross_value_bias,
        grad_cross_output,
        grad_cross_output_bias,
    )
    grad_branch = upstream_one.astype(jnp.bfloat16)
    grad_self_output_bias = jnp.sum(grad_branch.astype(jnp.float32), 0)
    grad_self_output = jnp.einsum(
        "tc,te->ce", self_low, grad_branch, preferred_element_type=jnp.float32
    )
    grad_attended = jnp.einsum(
        "te,ce->tc", grad_branch, self_output, preferred_element_type=jnp.float32
    ).astype(jnp.bfloat16)
    spread = spread_of(grad_attended, self_attended)
    grad_query_acc, grad_keys_acc, grad_values_acc = mutual_fold(
        heads_of(self_q),
        heads_of(grad_attended),
        self_log,
        spread,
        heads_of(self_k),
        heads_of(self_v),
        positions,
        complexes,
        lengths_row,
        (query_start, query_start, query_start),
        (
            lax.all_gather(self_q.astype(jnp.float32), "blk", axis=0, tiled=True),
            lax.all_gather(grad_attended.astype(jnp.float32), "blk", axis=0, tiled=True),
            lax.all_gather(self_log, "blk", axis=0, tiled=True),
            lax.all_gather(spread, "blk", axis=0, tiled=True),
            lax.all_gather(self_k.astype(jnp.float32), "blk", axis=0, tiled=True),
            lax.all_gather(self_v.astype(jnp.float32), "blk", axis=0, tiled=True),
        ),
        jnp.int32(0),
    )
    grad_sq = grad_query_acc.reshape(tokens, model_width).astype(jnp.bfloat16)
    grad_sk = grad_keys_acc.reshape(tokens, model_width).astype(jnp.bfloat16)
    grad_sv = grad_values_acc.reshape(tokens, model_width).astype(jnp.bfloat16)
    grad_self_query = jnp.einsum(
        "tc,te->ce", normed_one, grad_sq, preferred_element_type=jnp.float32
    )
    grad_self_query_bias = jnp.sum(grad_sq.astype(jnp.float32), 0)
    grad_self_key = jnp.einsum("tc,te->ce", normed_one, grad_sk, preferred_element_type=jnp.float32)
    grad_self_value = jnp.einsum(
        "tc,te->ce", normed_one, grad_sv, preferred_element_type=jnp.float32
    )
    grad_self_value_bias = jnp.sum(grad_sv.astype(jnp.float32), 0)
    grad_normed = (
        jnp.einsum("te,ce->tc", grad_sq, self_query, preferred_element_type=jnp.float32)
        + jnp.einsum("te,ce->tc", grad_sk, self_key, preferred_element_type=jnp.float32)
        + jnp.einsum("te,ce->tc", grad_sv, self_value, preferred_element_type=jnp.float32)
    )
    norm_grad, grad_self_norm_gain, grad_self_norm_bias = norm_back(
        grad_normed, unit_one, factor_one, self_norm_gain
    )
    residues_grad = upstream_one + norm_grad
    self_parts = (
        grad_self_norm_gain,
        grad_self_norm_bias,
        grad_self_query,
        grad_self_query_bias,
        grad_self_key,
        grad_self_value,
        grad_self_value_bias,
        grad_self_output,
        grad_self_output_bias,
    )
    ordered = (
        lax.psum_scatter(self_parts[0], "blk", scatter_dimension=0, tiled=True),
        lax.psum_scatter(self_parts[1], "blk", scatter_dimension=0, tiled=True),
        lax.psum_scatter(self_parts[2], "blk", scatter_dimension=0, tiled=True),
        lax.psum_scatter(self_parts[3], "blk", scatter_dimension=0, tiled=True),
        lax.psum_scatter(self_parts[4], "blk", scatter_dimension=0, tiled=True),
        lax.psum_scatter(self_parts[5], "blk", scatter_dimension=0, tiled=True),
        lax.psum_scatter(self_parts[6], "blk", scatter_dimension=0, tiled=True),
        lax.psum_scatter(self_parts[7], "blk", scatter_dimension=0, tiled=True),
        lax.psum_scatter(self_parts[8], "blk", scatter_dimension=0, tiled=True),
        lax.psum_scatter(cross_parts[0], "blk", scatter_dimension=0, tiled=True),
        lax.psum_scatter(cross_parts[1], "blk", scatter_dimension=0, tiled=True),
        lax.psum_scatter(cross_parts[2], "blk", scatter_dimension=0, tiled=True),
        lax.psum_scatter(cross_parts[3], "blk", scatter_dimension=0, tiled=True),
        lax.psum_scatter(cross_parts[4], "blk", scatter_dimension=0, tiled=True),
        lax.psum_scatter(cross_parts[5], "blk", scatter_dimension=0, tiled=True),
        lax.psum_scatter(cross_parts[6], "blk", scatter_dimension=0, tiled=True),
        lax.psum_scatter(cross_parts[7], "blk", scatter_dimension=0, tiled=True),
        lax.psum_scatter(cross_parts[8], "blk", scatter_dimension=0, tiled=True),
        lax.psum_scatter(feed_parts[0], "blk", scatter_dimension=0, tiled=True),
        lax.psum_scatter(feed_parts[1], "blk", scatter_dimension=0, tiled=True),
        lax.psum_scatter(feed_parts[2], "blk", scatter_dimension=0, tiled=True),
        lax.psum_scatter(feed_parts[3], "blk", scatter_dimension=0, tiled=True),
        lax.psum_scatter(feed_parts[4], "blk", scatter_dimension=0, tiled=True),
        lax.psum_scatter(feed_parts[5], "blk", scatter_dimension=0, tiled=True),
    )
    totals = lax.psum(
        (
            ordered[0],
            ordered[1],
            ordered[2],
            ordered[3],
            ordered[4],
            ordered[5],
            ordered[6],
            ordered[7],
            ordered[8],
            ordered[9],
            ordered[10],
            ordered[11],
            ordered[12],
            ordered[13],
            ordered[14],
            ordered[15],
            ordered[16],
            ordered[17],
            ordered[18],
            ordered[19],
            ordered[20],
            ordered[21],
            ordered[22],
            ordered[23],
        ),
        "batch",
    )
    return (layer_out[None], residues_grad[None], memory_grad[None]) + tuple(totals)


BLOCK = 128
HALF = 64
CHIPS = 8
HEAD = 64
WIDE = 512
HIDDEN = 2048
ROUND = 16
MASKED = -1e30
ONES_LANE = 5
SELF, CROSS = 0, 1
MESH = pl.DeviceIdType.MESH
VMEM = pl.BlockSpec(memory_space=pltpu.VMEM)
SMEM = pl.BlockSpec(memory_space=pltpu.SMEM)
PLACED = pl.BlockSpec(memory_space=pl.ANY)
BF16, F32 = jnp.bfloat16, jnp.float32

SQ, SK, SV, SO, CQ, CK, CV, CO = range(8)
(
    ROW_SELF_GAIN, ROW_SELF_SHIFT, ROW_SQ, ROW_SV, ROW_SO, ROW_CROSS_GAIN, ROW_CROSS_SHIFT, ROW_CQ, ROW_CV, ROW_CO,
    ROW_FEED_GAIN, ROW_FEED_SHIFT, ROW_OUT, ROW_IN,
) = range(14)
VECTOR_ROWS = 24
UNIT_OUT, UNIT_IN = 0, 4
UNIT_OF = {CO: 8, SO: 9, CQ: 10, CK: 11, CV: 12, SQ: 13, SV: 14, SK: 15}
UNITS = 16
G_OUT, G_MORE, G_IN, G_REST, G_EARLY, G_CROSS, G_SELF, G_LAST = range(8)
SPANS = ((0, 2), (2, 4), (4, 6), (6, 9), (9, 11), (11, 13), (13, 15), (15, 16))
COLUMN_FIRST = (G_OUT, G_LAST)
X_SQ, X_SO, X_CQ, X_CO, X_CDO, X_CDQ, X_SDO, X_SDQ = range(8)


class Operands(typing.NamedTuple):
    residues: VMEM
    memory: VMEM
    lengths: SMEM
    cotangent: VMEM
    self_norm_gain: VMEM
    self_norm_bias: VMEM
    self_query: PLACED
    self_query_bias: VMEM
    self_key: PLACED
    self_value: PLACED
    self_value_bias: VMEM
    self_output: PLACED
    self_output_bias: VMEM
    cross_norm_gain: VMEM
    cross_norm_bias: VMEM
    cross_query: PLACED
    cross_query_bias: VMEM
    cross_key: PLACED
    cross_value: PLACED
    cross_value_bias: VMEM
    cross_output: PLACED
    cross_output_bias: VMEM
    feed_norm_gain: VMEM
    feed_norm_bias: VMEM
    feed_in: PLACED
    feed_in_bias: VMEM
    feed_out: PLACED
    feed_out_bias: VMEM


AT_LAYER, AT_RESIDUES, AT_MEMORY, AT_SQUARE, AT_IN, AT_OUT, AT_VECTORS = 0, 128, 256, 384, 640, 768, 896
RESULT_ROWS = AT_VECTORS + VECTOR_ROWS


class Scratch(typing.NamedTuple):
    final: pltpu.VMEM((RESULT_ROWS, WIDE), F32)
    w_square: pltpu.VMEM((8, WIDE, WIDE), BF16)
    w_in: pltpu.VMEM((WIDE, HIDDEN), BF16)
    w_out: pltpu.VMEM((HIDDEN, WIDE), BF16)
    kv_out: pltpu.VMEM((2, CHIPS, BLOCK, BLOCK), BF16)
    kv: pltpu.VMEM((2, 2 * CHIPS, BLOCK, BLOCK), BF16)
    narrow_out: pltpu.VMEM((8, CHIPS, HALF, BLOCK), BF16)
    narrow: pltpu.VMEM((8, CHIPS, HALF, BLOCK), BF16)
    dkv_out: pltpu.VMEM((2, CHIPS, BLOCK, BLOCK), BF16)
    dkv: pltpu.VMEM((2, CHIPS, BLOCK, BLOCK), BF16)
    dkv_part: pltpu.VMEM((2, CHIPS, 2, BLOCK, BLOCK), BF16)
    dkv_other: pltpu.VMEM((2, CHIPS, BLOCK, BLOCK), BF16)
    dq_turned: pltpu.VMEM((BLOCK, 1024), F32)
    q_rows: pltpu.VMEM((2, 1024, BLOCK), BF16)
    q_features: pltpu.VMEM((2, 1024, BLOCK), BF16)
    do_rows: pltpu.VMEM((2, 1024, BLOCK), BF16)
    o_rows: pltpu.VMEM((2, 1024, BLOCK), F32)
    do_features: pltpu.VMEM((1024, BLOCK), BF16)
    query_features: pltpu.VMEM((1024, BLOCK), BF16)
    key_features: pltpu.VMEM((2048, BLOCK), BF16)
    causal: pltpu.VMEM((256, 512), F32)
    causal_turned: pltpu.VMEM((512, 256), F32)
    units: pltpu.VMEM((3, BLOCK, WIDE), F32)
    factors: pltpu.VMEM((3, BLOCK, BLOCK), F32)
    normed: pltpu.VMEM((3, BLOCK, WIDE), BF16)
    attended: pltpu.VMEM((2, BLOCK, WIDE), BF16)
    upstream: pltpu.VMEM((BLOCK, WIDE), F32)
    grad_active: pltpu.VMEM((BLOCK, HIDDEN), F32)
    active: pltpu.VMEM((BLOCK, HIDDEN), BF16)
    grad_inner: pltpu.VMEM((BLOCK, HIDDEN), BF16)
    parts: pltpu.VMEM((UNITS, 4, 2, 2, 2, ROUND, WIDE), BF16)
    by_core: pltpu.VMEM((UNITS, 4, 2, 2, ROUND, WIDE), BF16)
    by_side: pltpu.VMEM((UNITS, 4, 2, ROUND, WIDE), BF16)
    by_column: pltpu.VMEM((UNITS, 4, ROUND, WIDE), BF16)
    by_plane: pltpu.VMEM((3, UNITS, ROUND, WIDE), BF16)
    halves: pltpu.VMEM((2, UNITS, ROUND, WIDE), BF16)
    vectors: pltpu.VMEM((VECTOR_ROWS, WIDE), F32)
    vec_in: pltpu.VMEM((CHIPS, VECTOR_ROWS, BLOCK), F32)
    vec_four: pltpu.VMEM((4, VECTOR_ROWS, BLOCK), F32)
    load_sems: pltpu.SemaphoreType.DMA((10,))
    narrow_sems: pltpu.SemaphoreType.DMA((8,))
    kv_sems: pltpu.SemaphoreType.DMA((2, CHIPS))
    dkv_sems: pltpu.SemaphoreType.DMA((2,))
    pass_sems: pltpu.SemaphoreType.DMA((2,))
    share_sems: pltpu.SemaphoreType.DMA((2, 2))
    sent_sems: pltpu.SemaphoreType.DMA((7,))
    reduce_sems: pltpu.SemaphoreType.DMA((len(SPANS), 5))
    reduce_sent: pltpu.SemaphoreType.DMA((len(SPANS),))
    vec_sems: pltpu.SemaphoreType.DMA((2,))
    final_sems: pltpu.SemaphoreType.DMA((6,))


def specs_of(kind):
    return tuple(kind.__annotations__.values())


def dot_nn(left, right):
    return lax.dot_general(left, right, (((1,), (0,)), ((), ())), preferred_element_type=F32)


def dot_nt(left, right):
    return lax.dot_general(left, right, (((1,), (1,)), ((), ())), preferred_element_type=F32)


def dot_tn(left, right):
    return lax.dot_general(left, right, (((0,), (0,)), ((), ())), preferred_element_type=F32)


def low_lanes(shape):
    return lax.broadcasted_iota(jnp.int32, shape, len(shape) - 1) < HEAD


def turn(block):
    return pltpu.roll(block, HEAD, 1)


def swap(first, second):
    keep = low_lanes(first.shape)
    return jnp.where(keep, first, turn(second)), jnp.where(keep, turn(first), second)


def column_sum(low):
    return jnp.sum(low.astype(F32), 0, keepdims=True)


def flat(ref):
    return ref[...].reshape(1, -1)


def fused_kernel(*refs):
    count = len(specs_of(Operands))
    a, result, s = Operands(*refs[:count]), refs[count], Scratch(*refs[count + 1 :])

    rank = lax.axis_index("blk")
    side = lax.axis_index("batch")
    chip, core = lax.div(rank, 2), lax.rem(rank, 2)
    plane, column = lax.div(chip, 2), lax.rem(chip, 2)

    def around(shift):
        return lax.rem(chip + (CHIPS + shift), CHIPS)

    def at_rank(index):
        return {"blk": index}

    partner = at_rank(2 * chip + 1 - core)
    beside = at_rank(2 * (2 * plane + 1 - column) + core)
    across = {"batch": 1 - side}
    opposite = {"blk": 2 * chip + 1 - core, "batch": 1 - side}

    def remote(src, dst, sems, device):
        return pltpu.make_async_remote_copy(
            src_ref=src, dst_ref=dst, send_sem=sems[0], recv_sem=sems[1], device_id=device, device_id_type=MESH
        )

    SENT_NARROW, SENT_KV, SENT_PASS, SENT_DKV, SENT_SHARE, SENT_VECTOR, SENT_FOUR = (
        s.sent_sems.at[which] for which in range(7)
    )

    finished = []

    def final_put(at, values):
        s.final[pl.ds(at, values.shape[0]), : values.shape[1]] = values

    def final_start(at, rows):
        span = pl.ds(at, rows)
        finished.append(pltpu.make_async_copy(s.final.at[span], result.at[span], s.final_sems.at[len(finished)]))
        finished[-1].start()

    loads = {}

    def load(*pairs):
        for which, source in pairs:
            target = s.w_square.at[which] if which < 8 else (s.w_out, s.w_in)[which - 8]
            loads[which] = pltpu.make_async_copy(source, target, s.load_sems.at[which])
            loads[which].start()

    load((SK, a.self_key), (SV, a.self_value), (SQ, a.self_query))

    def weight(which):
        if which in loads:
            loads.pop(which).wait()
        return s.w_square[which] if which < 8 else (s.w_out, s.w_in)[which - 8]

    barrier = pltpu.get_barrier_semaphore()
    for shift in range(1, CHIPS):
        pl.semaphore_signal(barrier, inc=1, device_id=at_rank(2 * around(shift) + core), device_id_type=MESH)
    for other in (partner, across, opposite):
        pl.semaphore_signal(barrier, inc=1, device_id=other, device_id_type=MESH)

    class Exchange:
        def __init__(self, outgoing, incoming, sems, sent, which, by_source=False):
            self.outgoing, self.incoming, self.by_source = outgoing.at[which], incoming.at[which], by_source
            self.sems, self.sent = sems.at[which], sent

        def slot(self, source):
            return self.incoming.at[2 * source + core if self.by_source else source]

        def pair(self, source):
            return (self.sent, self.sems.at[source] if self.by_source else self.sems)

        def start(self):
            for shift in range(1, CHIPS):
                to = around(shift)
                remote(self.outgoing.at[to], self.slot(chip), self.pair(chip), at_rank(2 * to + core)).start()
            self.slot(chip)[...] = self.outgoing[chip]

        def wait(self, shift):
            source = around(-shift)
            remote(
                self.outgoing.at[source], self.slot(source), self.pair(source), at_rank(2 * source + core)
            ).wait_recv()

        def wait_all(self):
            seven = pl.ds(0, CHIPS - 1)
            remote(self.outgoing.at[seven], self.incoming.at[seven], (self.sent, self.sems), partner).wait_recv()

    narrow = [Exchange(s.narrow_out, s.narrow, s.narrow_sems, SENT_NARROW, which) for which in range(8)]
    keys_values = [Exchange(s.kv_out, s.kv, s.kv_sems, SENT_KV, which, True) for which in (SELF, CROSS)]
    key_grads = [Exchange(s.dkv_out, s.dkv, s.dkv_sems, SENT_DKV, which) for which in (SELF, CROSS)]

    def pass_on(kind):
        for shift in range(CHIPS):
            if shift > 0:
                keys_values[kind].wait(shift)
            slot = s.kv.at[kind, 2 * around(-shift) + core]
            remote(slot, slot, (SENT_PASS, s.pass_sems.at[kind]), partner).start()

    def pass_wait(kind):
        eight = s.kv.at[kind, pl.ds(0, CHIPS)]
        remote(eight, eight, (SENT_PASS, s.pass_sems.at[kind]), partner).wait_recv()

    def pack_groups(matrix, which):
        for pair in range(CHIPS // 2):
            group = matrix[:, BLOCK * pair : BLOCK * (pair + 1)]
            one, two = swap(group[:HALF], group[HALF:])
            s.narrow_out[which, 2 * pair] = one.astype(BF16)
            s.narrow_out[which, 2 * pair + 1] = two.astype(BF16)

    def unpack_groups(which):
        groups = []
        for pair in range(CHIPS // 2):
            groups.append(
                jnp.concatenate(
                    swap(s.narrow[which, 2 * pair].astype(F32), s.narrow[which, 2 * pair + 1].astype(F32)), 0
                )
            )
        return jnp.concatenate(groups, 1).astype(BF16)

    def pack_pairs(keys, values, kind):
        for pair in range(CHIPS // 2):
            lanes = slice(BLOCK * pair, BLOCK * (pair + 1))
            one, two = swap(keys[:, lanes], values[:, lanes])
            s.kv_out[kind, 2 * pair] = one.astype(BF16)
            s.kv_out[kind, 2 * pair + 1] = two.astype(BF16)

    def unpack_pairs(kind):
        pairs = [
            swap(s.dkv[kind, 2 * pair].astype(F32), s.dkv[kind, 2 * pair + 1].astype(F32)) for pair in range(CHIPS // 2)
        ]
        return tuple(jnp.concatenate(each, 1).astype(BF16) for each in zip(*pairs, strict=True))

    def reduce_copy(stage, group):
        first, last = SPANS[group]
        span = pl.ds(first, last - first)
        sems = (s.reduce_sent.at[group], s.reduce_sems.at[group, {0: 0, 1: 1, 2: 2, 6: 4}.get(stage, 3)])
        if stage == 0:
            return remote(s.parts.at[span, :, :, 1 - core], s.by_core.at[span], sems, partner)
        columns = (stage == 1) == (group in COLUMN_FIRST)
        if stage == 1:
            source = s.by_core.at[span, :, 1 - column] if columns else s.by_core.at[span, :, :, 1 - side]
            return remote(source, s.by_side.at[span], sems, beside if columns else across)
        if stage == 2:
            source = s.by_side.at[span, :, 1 - column if columns else 1 - side]
            return remote(source, s.by_column.at[span], sems, beside if columns else across)
        if stage < 6:
            to = lax.rem(plane + (stage - 2), 4)
            return remote(
                s.by_column.at[span, to], s.by_plane.at[stage - 3, span], sems, at_rank(2 * (2 * to + column) + core)
            )
        return remote(s.halves.at[side, span], s.halves.at[side, span], sems, across)

    def planes_copy(group):
        span = s.by_plane.at[:, pl.ds(SPANS[group][0], SPANS[group][1] - SPANS[group][0])]
        return remote(span, span, (s.reduce_sent.at[group], s.reduce_sems.at[group, 3]), partner)

    def reduce_sent(stage, group):
        (planes_copy(group) if stage == 3 else reduce_copy(stage, group)).wait_send()

    def reduce_start(stage, group):
        if stage > 0:
            reduce_sent(3 if stage == 6 else stage - 1, group)
        for each in (3, 4, 5) if stage == 3 else (stage,):
            reduce_copy(each, group).start()

    def reduce_finish(stage, group):
        first, last = SPANS[group]
        if stage == 3:
            planes_copy(group).wait_recv()
        elif stage == 6:
            half = s.halves.at[1 - side, pl.ds(first, last - first)]
            remote(half, half, (s.reduce_sent.at[group], s.reduce_sems.at[group, 4]), across).wait_recv()
        else:
            reduce_copy(stage, group).wait_recv()

        def add(unit, nothing):
            if stage == 0:
                s.by_core[unit] = s.by_core[unit] + s.parts[unit, :, :, core]
            columns = (stage == 1) == (group in COLUMN_FIRST)
            if stage == 1:
                own = s.by_core[unit, :, column] if columns else s.by_core[unit, :, :, side]
                s.by_side[unit] = s.by_side[unit] + own
            if stage == 2:
                s.by_column[unit] = s.by_column[unit] + s.by_side[unit, :, column if columns else side]
            if stage == 3:
                total = s.by_column[unit, plane].astype(F32)
                for each in range(3):
                    total = total + s.by_plane[each, unit].astype(F32)
                s.halves[side, unit] = total.astype(BF16)
            return nothing

        if stage < 6:
            lax.fori_loop(first, last, add, 0)

    def reduce_step(stage, group):
        reduce_finish(stage, group)
        reduce_start(stage + 1 if stage < 3 else 6, group)

    def put_unit(unit, value):
        s.parts[unit] = value.astype(BF16).reshape(4, 2, 2, 2, ROUND, WIDE)

    def put_vector(row, values):
        if values.shape[1] == WIDE:
            s.vectors[pl.ds(row, 1), :] = values
            return
        for at in range(HIDDEN // BLOCK):
            group, piece = divmod(at, 4)
            s.vectors[pl.ds(row + piece, 1), BLOCK * group : BLOCK * (group + 1)] = values[
                :, BLOCK * at : BLOCK * (at + 1)
            ]

    def norm(values, which, gain, shift):
        average = jnp.mean(values, -1, keepdims=True)
        centred = values - average
        factor = lax.rsqrt(jnp.mean(centred * centred, -1, keepdims=True) + EPS)
        normal = centred * factor
        s.units[which] = normal
        s.factors[which] = jnp.broadcast_to(factor, (BLOCK, BLOCK))
        low = (normal * flat(gain) + flat(shift)).astype(BF16)
        s.normed[which] = low
        return low

    def norm_gradient(gradient, which, gain, row):
        normal = s.units[which]
        weighted = gradient * flat(gain)
        one = jnp.mean(weighted, -1, keepdims=True)
        two = jnp.mean(weighted * normal, -1, keepdims=True)
        put_vector(row, jnp.sum(gradient * normal, 0, keepdims=True))
        put_vector(row + 1, jnp.sum(gradient, 0, keepdims=True))
        return s.factors[which][:, :1] * (weighted - one - normal * two)

    def query_rows(kind, which):
        keep = low_lanes((HALF, BLOCK))
        for block in range(CHIPS):
            piece = s.narrow[which, block].astype(F32)
            both = jnp.concatenate([jnp.where(keep, piece, 0.0), jnp.where(keep, turn(piece), 0.0)], 0)
            s.q_rows[kind, pl.ds(block * BLOCK, BLOCK), :] = both.astype(BF16)

    def key_block(kind, chunk):
        rows = s.kv[kind, pl.ds(4 * chunk, 4)].reshape(512, BLOCK)
        return jnp.concatenate([rows, s.key_features[pl.ds(512 * chunk, 512), :]], 1)

    def with_column(features, column_values):
        lane = lax.broadcasted_iota(jnp.int32, features.shape, 1)
        full = jnp.broadcast_to(column_values, features.shape)
        high = full.astype(BF16).astype(F32)
        middle = (full - high).astype(BF16).astype(F32)
        low = full - high - middle
        for at, piece in enumerate((high, middle, low)):
            features = jnp.where(lane == ONES_LANE + at, piece, features)
        return features.astype(BF16)

    def attend(kind, causal, which):
        for part in range(4):
            rows = pl.ds(part * 256, 256)
            queries = jnp.concatenate([s.q_rows[kind, rows, :], s.query_features[rows, :]], 1)
            highest, summed = None, None
            chunks = range(part, -1, -1) if causal else range(4)
            for chunk in chunks:
                keys = key_block(kind, chunk)
                scores = dot_nt(queries, keys)
                if causal and chunk == part:
                    scores = scores + s.causal[...]
                reach = scores[:, :BLOCK]
                for at in range(1, 4):
                    reach = jnp.maximum(reach, scores[:, BLOCK * at : BLOCK * (at + 1)])
                reach = jnp.max(reach, 1, keepdims=True)
                if summed is None:
                    summed = dot_nn(jnp.exp(scores - reach).astype(BF16), keys)
                else:
                    reach = jnp.maximum(highest, reach)
                    summed = summed * jnp.exp(highest - reach) + dot_nn(jnp.exp(scores - reach).astype(BF16), keys)
                highest = reach
            total = summed[:, BLOCK + ONES_LANE : BLOCK + ONES_LANE + 1]
            result = summed[:, :BLOCK] / total
            s.o_rows[kind, rows, :] = result
            s.q_features[kind, rows, :] = with_column(
                s.query_features[rows, :].astype(F32), -(highest + jnp.log(total))
            )
            keep = low_lanes((HALF, BLOCK))
            for half in range(2):
                block = result[BLOCK * half : BLOCK * (half + 1)]
                s.narrow_out[which, 2 * part + half] = jnp.where(keep, turn(block[:HALF]), block[HALF:]).astype(BF16)

    def attend_back(kind, causal, which_in, which_out, between):
        keep = low_lanes((HALF, BLOCK))
        for block in range(CHIPS):
            rows = pl.ds(block * BLOCK, BLOCK)
            piece = s.narrow[which_in, block].astype(F32)
            gradient = jnp.concatenate([jnp.where(keep, 0.0, turn(piece)), jnp.where(keep, 0.0, piece)], 0)
            s.do_rows[kind, rows, :] = gradient.astype(BF16)
            spread = jnp.sum(gradient * s.o_rows[kind, rows, :], 1, keepdims=True)
            s.do_features[rows, :] = with_column(jnp.zeros((BLOCK, BLOCK), F32), -spread)
        for chunk in range(4):
            keys = key_block(kind, chunk)
            total = None
            for part in range(chunk if causal else 0, 4):
                rows = pl.ds(part * 256, 256)
                queries, grads = s.q_rows[kind, rows, :], s.do_rows[kind, rows, :]
                scores = dot_nt(keys, jnp.concatenate([queries, s.q_features[kind, rows, :]], 1))
                if causal and part == chunk:
                    scores = scores + s.causal_turned[...]
                weights = jnp.exp(scores)
                slopes = dot_nt(keys, jnp.concatenate([grads, s.do_features[rows, :]], 1))
                tilted = (weights * slopes).astype(BF16)
                shares = dot_nn(
                    jnp.concatenate([tilted, weights.astype(BF16)], 1), jnp.concatenate([queries, grads], 0)
                )
                total = shares if total is None else total + shares
                toward = dot_tn(keys[:, :BLOCK], tilted)
                s.dq_turned[:, rows] = toward if chunk == 0 else s.dq_turned[:, rows] + toward
            s.dkv_part[kind, 2 * chunk : 2 * chunk + 2] = total.astype(BF16).reshape(2, 2, BLOCK, BLOCK)
            between(chunk)
        for block in range(CHIPS):
            s.narrow_out[which_out, block] = (
                s.dq_turned[:HEAD, BLOCK * block : BLOCK * (block + 1)] * (HEAD**-0.5)
            ).astype(BF16)

    def turned_rows(which):
        return s.narrow[which].reshape(WIDE, BLOCK).astype(F32).T.astype(BF16)

    def share_copy(kind, part):
        chips = pl.ds(4 * part, 4)
        return remote(
            s.dkv_part.at[kind, chips, 1 - core], s.dkv_other.at[kind, chips], (SENT_SHARE, s.share_sems.at[kind, part]),
            partner,
        )

    def share_finish(kind):
        for part in range(2):
            share_copy(kind, part).wait_recv()
            chips = slice(4 * part, 4 * part + 4)
            s.dkv_out[kind, chips] = s.dkv_part[kind, chips, core] + s.dkv_other[kind, chips]

    inputs = a.residues[...].astype(F32)
    normed = norm(inputs, 0, a.self_norm_gain, a.self_norm_bias)
    keys = dot_nn(normed, weight(SK))
    values = dot_nn(normed, weight(SV)) + flat(a.self_value_bias)
    pack_pairs(keys, values, SELF)
    pl.semaphore_wait(barrier, CHIPS + 2)
    keys_values[SELF].start()
    load((CK, a.cross_key), (CV, a.cross_value), (8, a.feed_out), (SO, a.self_output))
    load((CQ, a.cross_query), (CO, a.cross_output), (9, a.feed_in))
    queries = (dot_nn(normed, weight(SQ)) + flat(a.self_query_bias)) * (HEAD**-0.5)
    pack_groups(queries, X_SQ)
    narrow[X_SQ].start()

    encoded = a.memory[...]
    keys = dot_nn(encoded, weight(CK))
    values = dot_nn(encoded, weight(CV)) + flat(a.cross_value_bias)
    pack_pairs(keys, values, CROSS)

    bounds, reach = [], 0
    for at in range(4):
        reach = reach + a.lengths[0, at]
        bounds.append(reach)
    lane = lax.broadcasted_iota(jnp.int32, (BLOCK, BLOCK), 1)
    row = lax.broadcasted_iota(jnp.int32, (BLOCK, BLOCK), 0)

    def documents(position):
        found = jnp.zeros((BLOCK, BLOCK), jnp.int32)
        for bound in bounds:
            found = found + (position >= bound).astype(jnp.int32)
        return found

    ones = jnp.where((lane >= ONES_LANE) & (lane < ONES_LANE + 3), 1.0, 0.0)

    def key_features(block, nothing):
        other = documents(row + block * BLOCK) != lane
        s.key_features[pl.ds(block * BLOCK, BLOCK), :] = jnp.where((lane < ONES_LANE) & other, MASKED, ones).astype(
            BF16
        )
        return nothing

    lax.fori_loop(0, 2 * CHIPS, key_features, 0)

    def query_features(block, nothing):
        same = documents(row + (2 * block + core) * BLOCK) == lane
        s.query_features[pl.ds(block * BLOCK, BLOCK), :] = jnp.where((lane < ONES_LANE) & same, 1.0, 0.0).astype(BF16)
        return nothing

    lax.fori_loop(0, CHIPS, query_features, 0)

    def query_place(at):
        return at + core * BLOCK + jnp.where(at >= BLOCK, BLOCK, 0)

    at_row = lax.broadcasted_iota(jnp.int32, (256, 512), 0)
    at_key = lax.broadcasted_iota(jnp.int32, (256, 512), 1)
    s.causal[...] = jnp.where(at_key <= query_place(at_row), 0.0, MASKED)
    at_key = lax.broadcasted_iota(jnp.int32, (512, 256), 0)
    at_row = lax.broadcasted_iota(jnp.int32, (512, 256), 1)
    s.causal_turned[...] = jnp.where(at_key <= query_place(at_row), 0.0, MASKED)
    pass_on(SELF)
    keys_values[CROSS].start()
    narrow[X_SQ].wait_all()
    query_rows(SELF, X_SQ)
    pass_wait(SELF)
    attend(SELF, True, X_SO)
    narrow[X_SO].start()
    grads = a.cotangent[...]
    weight(8)
    for piece in range(4):
        lanes = slice(512 * piece, 512 * (piece + 1))
        s.grad_active[:, lanes] = dot_nt(grads, s.w_out[lanes, :])
    pass_on(CROSS)
    narrow[X_SO].wait_all()
    self_low = unpack_groups(X_SO)
    s.attended[SELF] = self_low
    after_self = inputs + dot_nn(self_low, weight(SO)) + flat(a.self_output_bias)

    normed = norm(after_self, 1, a.cross_norm_gain, a.cross_norm_bias)
    queries = (dot_nn(normed, weight(CQ)) + flat(a.cross_query_bias)) * (HEAD**-0.5)
    pack_groups(queries, X_CQ)
    narrow[X_CQ].start()
    pass_wait(CROSS)
    narrow[X_CQ].wait_all()
    query_rows(CROSS, X_CQ)
    attend(CROSS, False, X_CO)
    narrow[X_CO].start()
    weight(9)
    narrow[X_CO].wait_all()
    cross_low = unpack_groups(X_CO)
    s.attended[CROSS] = cross_low
    after_cross = after_self + dot_nn(cross_low, weight(CO)) + flat(a.cross_output_bias)

    normed = norm(after_cross, 2, a.feed_norm_gain, a.feed_norm_bias)
    layer_out, back = after_cross + flat(a.feed_out_bias), None
    for piece in range(4):
        lanes = slice(512 * piece, 512 * (piece + 1))
        inner = dot_nn(normed, s.w_in[:, lanes]) + flat(a.feed_in_bias)[:, lanes]
        bell = 0.5 * (1.0 + lax.erf(inner * SQRT_HALF))
        active = (inner * bell).astype(BF16)
        slope = bell + inner * jnp.exp(-0.5 * inner * inner) * INV_ROOT_TAU
        grad_inner = (s.grad_active[:, lanes] * slope).astype(BF16)
        s.active[:, lanes] = active
        s.grad_inner[:, lanes] = grad_inner
        layer_out = layer_out + dot_nn(active, s.w_out[lanes, :])
        toward = dot_nt(grad_inner, s.w_in[:, lanes])
        back = toward if back is None else back + toward
    final_put(AT_LAYER, layer_out)
    final_start(AT_LAYER, BLOCK)
    upstream = a.cotangent[...].astype(F32)
    upstream = upstream + norm_gradient(back, 2, a.feed_norm_gain, ROW_FEED_GAIN)

    branch = upstream.astype(BF16)
    pack_groups(dot_nt(branch, weight(CO)), X_CDO)
    narrow[X_CDO].start()
    s.upstream[...] = upstream
    put_vector(ROW_OUT, column_sum(a.cotangent[...]))
    put_vector(ROW_IN, column_sum(s.grad_inner[...]))
    put_vector(ROW_CO, column_sum(branch))
    for piece in range(4):
        lanes = slice(512 * piece, 512 * (piece + 1))
        part = dot_tn(s.active[:, lanes], a.cotangent[...]).astype(BF16).reshape(2, 2, 4, 2, ROUND, WIDE)
        for each in range(4):
            s.parts[UNIT_OUT + each, piece] = part[:, :, each]
    reduce_start(0, G_OUT)
    reduce_start(0, G_MORE)
    for piece in range(4):
        lanes = slice(512 * piece, 512 * (piece + 1))
        put_unit(UNIT_IN + piece, dot_tn(s.normed[2], s.grad_inner[:, lanes]))
        if piece == 1:
            reduce_start(0, G_IN)
    put_unit(UNIT_OF[CO], dot_tn(s.attended[CROSS], branch))
    reduce_start(0, G_REST)
    reduce_step(0, G_MORE)
    narrow[X_CDO].wait_all()
    reduce_step(0, G_OUT)

    def between_cross(chunk):
        if chunk == 0:
            reduce_step(0, G_IN)
        if chunk in (1, 3):
            share_copy(CROSS, chunk // 2).start()

    attend_back(CROSS, False, X_CDO, X_CDQ, between_cross)
    narrow[X_CDQ].start()
    share_finish(CROSS)
    key_grads[CROSS].start()
    reduce_step(1, G_OUT)
    reduce_step(0, G_REST)
    reduce_step(1, G_MORE)
    narrow[X_CDQ].wait_all()
    grad_query = turned_rows(X_CDQ)
    gradient = dot_nt(grad_query, weight(CQ))
    upstream = s.upstream[...] + norm_gradient(gradient, 1, a.cross_norm_gain, ROW_CROSS_GAIN)

    branch = upstream.astype(BF16)
    pack_groups(dot_nt(branch, weight(SO)), X_SDO)
    narrow[X_SDO].start()
    reduce_step(2, G_OUT)
    reduce_step(1, G_IN)
    s.upstream[...] = upstream
    put_vector(ROW_SO, column_sum(branch))
    put_vector(ROW_CQ, column_sum(grad_query))
    put_unit(UNIT_OF[SO], dot_tn(s.attended[SELF], branch))
    put_unit(UNIT_OF[CQ], dot_tn(s.normed[1], grad_query))
    reduce_start(0, G_EARLY)
    key_grads[CROSS].wait_all()
    grad_key, grad_value = unpack_pairs(CROSS)
    put_vector(ROW_CV, column_sum(grad_value))
    put_unit(UNIT_OF[CK], dot_tn(a.memory[...], grad_key))
    put_unit(UNIT_OF[CV], dot_tn(a.memory[...], grad_value))
    reduce_start(0, G_CROSS)
    reduce_step(0, G_EARLY)
    final_put(AT_MEMORY, dot_nt(grad_key, weight(CK)) + dot_nt(grad_value, weight(CV)))
    final_start(AT_MEMORY, BLOCK)
    narrow[X_SDO].wait_all()
    reduce_step(2, G_MORE)
    reduce_step(1, G_REST)

    def between_self(chunk):
        if chunk == 0:
            reduce_step(0, G_CROSS)
        if chunk in (1, 3):
            share_copy(SELF, chunk // 2).start()

    attend_back(SELF, True, X_SDO, X_SDQ, between_self)
    narrow[X_SDQ].start()
    share_finish(SELF)
    key_grads[SELF].start()
    reduce_step(3, G_OUT)
    narrow[X_SDQ].wait_all()
    grad_query = turned_rows(X_SDQ)
    put_unit(UNIT_OF[SQ], dot_tn(s.normed[0], grad_query))
    reduce_step(1, G_EARLY)
    key_grads[SELF].wait_all()
    grad_key, grad_value = unpack_pairs(SELF)
    normed = s.normed[0]
    put_unit(UNIT_OF[SV], dot_tn(normed, grad_value))
    reduce_start(0, G_SELF)
    put_unit(UNIT_OF[SK], dot_tn(normed, grad_key))
    reduce_start(0, G_LAST)
    put_vector(ROW_SQ, column_sum(grad_query))
    put_vector(ROW_SV, column_sum(grad_value))
    gradient = dot_nt(grad_query, weight(SQ)) + dot_nt(grad_key, weight(SK)) + dot_nt(grad_value, weight(SV))
    final_put(AT_RESIDUES, s.upstream[...] + norm_gradient(gradient, 0, a.self_norm_gain, ROW_SELF_GAIN))
    final_start(AT_RESIDUES, BLOCK)

    def vector_copy(shift):
        if shift < CHIPS:
            to = around(shift)
            lanes = pl.ds(pl.multiple_of(lax.div(to, 2) * BLOCK, BLOCK), BLOCK)
            sems = (SENT_VECTOR, s.vec_sems.at[0])
            return remote(s.vectors.at[:, lanes], s.vec_in.at[shift], sems, at_rank(2 * to + core))
        other = (partner, across, opposite)[shift - CHIPS]
        return remote(s.vec_four.at[0], s.vec_four.at[shift - CHIPS + 1], (SENT_FOUR, s.vec_sems.at[1]), other)

    def vector_all(step):
        rows = s.vec_in.at[pl.ds(1, 7)] if step == 0 else s.vec_four.at[pl.ds(1, 3)]
        return remote(rows, rows, ((SENT_VECTOR, SENT_FOUR)[step], s.vec_sems.at[step]), partner)

    s.vectors[pl.ds(17, VECTOR_ROWS - 17), :] = jnp.zeros((VECTOR_ROWS - 17, WIDE), F32)
    for shift in range(1, CHIPS):
        vector_copy(shift).start()
    reduce_step(0, G_SELF)
    reduce_step(0, G_LAST)
    reduce_step(2, G_IN)
    reduce_step(1, G_CROSS)
    reduce_step(2, G_REST)
    reduce_step(3, G_MORE)
    lanes = pl.ds(pl.multiple_of(lax.div(chip, 2) * BLOCK, BLOCK), BLOCK)
    total = s.vectors[:, lanes]
    vector_all(0).wait_recv()
    for shift in range(1, CHIPS):
        total = total + s.vec_in[shift]
    s.vec_four[0] = total
    for other in range(3):
        vector_copy(CHIPS + other).start()
    reduce_step(2, G_EARLY)
    reduce_step(1, G_LAST)
    reduce_step(1, G_SELF)
    reduce_step(3, G_IN)
    reduce_step(2, G_CROSS)
    reduce_step(3, G_REST)
    vector_all(1).wait_recv()
    total = (s.vec_four[0] + s.vec_four[2]) + (s.vec_four[1] + s.vec_four[3])
    place_in_group = lax.rem(rank, 4)
    s.final[pl.ds(AT_VECTORS, VECTOR_ROWS), :BLOCK] = pltpu.roll(total, lax.rem(BLOCK - 32 * place_in_group, BLOCK), 1)
    own = jnp.zeros((1, BLOCK), F32)
    for each in range(4):
        own = own + jnp.where(place_in_group == each, total[ROW_IN + each : ROW_IN + each + 1], 0.0)
    s.final[pl.ds(AT_VECTORS + ROW_IN, 1), :BLOCK] = own
    final_start(AT_VECTORS, VECTOR_ROWS)

    def unit_value(unit):
        return jnp.concatenate([s.halves[0, unit], s.halves[1, unit]], 0).astype(F32)

    def put_final_unit(at, unit):
        final_put(at, unit_value(unit))

    reduce_step(2, G_LAST)
    reduce_step(2, G_SELF)
    reduce_step(3, G_EARLY)
    reduce_step(3, G_CROSS)
    reduce_finish(6, G_OUT)
    reduce_finish(6, G_MORE)
    reduce_finish(6, G_IN)
    reduce_finish(6, G_REST)
    for piece in range(4):
        put_final_unit(AT_OUT + 32 * piece, UNIT_OUT + piece)
        put_final_unit(AT_IN + 32 * piece, UNIT_IN + piece)
    final_start(AT_IN, 2 * BLOCK)
    reduce_finish(6, G_EARLY)
    reduce_finish(6, G_CROSS)
    for which in (CO, CQ, CK, CV, SO):
        put_final_unit(AT_SQUARE + 32 * which, UNIT_OF[which])
    reduce_step(3, G_SELF)
    reduce_step(3, G_LAST)
    reduce_finish(6, G_SELF)
    reduce_finish(6, G_LAST)
    for which in (SQ, SK, SV):
        put_final_unit(AT_SQUARE + 32 * which, UNIT_OF[which])
    final_start(AT_SQUARE, 256)
    for copy in finished:
        copy.wait()
    for group in range(len(SPANS)):
        reduce_sent(6, group)
    seven = pl.ds(0, CHIPS - 1)
    for sent, blocks in (
        (SENT_NARROW, s.narrow_out.at[:, seven]), (SENT_KV, s.kv_out.at[:, seven]), (SENT_DKV, s.dkv_out.at[:, seven]),
        (SENT_PASS, s.kv.at[:, pl.ds(0, CHIPS)]), (SENT_SHARE, s.dkv_other),
    ):
        remote(blocks, blocks, (sent, s.vec_sems.at[0]), partner).wait_send()
    vector_all(0).wait_send()
    vector_all(1).wait_send()


def place_kernel(packed, *refs):
    results, vectors, sems = refs[:-2], refs[-2], refs[-1]
    copies = []

    def place(at, target):
        source = packed.at[pl.ds(at, target.shape[0]), pl.ds(0, target.shape[1])]
        copies.append(pltpu.make_async_copy(source, target, sems.at[len(copies)]))
        copies[-1].start()

    place(AT_VECTORS, vectors)
    for at, target in zip((AT_LAYER, AT_RESIDUES, AT_MEMORY), results[:3], strict=True):
        place(at, target)
    for which, at in SQUARE_RESULTS.items():
        place(AT_SQUARE + 32 * which, results[at])
    for piece in range(4):
        place(AT_IN + 32 * piece, results[23].at[:, pl.ds(512 * piece, 512)])
    place(AT_OUT, results[25])
    copies[0].wait()
    rows = vectors[...]
    for row, at in VECTOR_RESULTS.items():
        results[at][...] = rows[row, : results[at].shape[0]]
    for copy in copies[1:]:
        copy.wait()


SQUARE_RESULTS = {SQ: 5, SK: 7, SV: 8, SO: 10, CQ: 14, CK: 16, CV: 17, CO: 19}
VECTOR_RESULTS = {
    ROW_SELF_GAIN: 3, ROW_SELF_SHIFT: 4, ROW_SQ: 6, ROW_SV: 9, ROW_SO: 11, ROW_CROSS_GAIN: 12, ROW_CROSS_SHIFT: 13,
    ROW_CQ: 15, ROW_CV: 18, ROW_CO: 20, ROW_FEED_GAIN: 21, ROW_FEED_SHIFT: 22, ROW_OUT: 26, ROW_IN: 24,
}


def fused(residues, memory, lengths, cotangent, *parameters):
    packed = pl.pallas_call(
        fused_kernel,
        out_shape=jax.ShapeDtypeStruct((RESULT_ROWS, WIDE), F32),
        in_specs=specs_of(Operands),
        out_specs=PLACED,
        scratch_shapes=specs_of(Scratch),
        compiler_params=pltpu.CompilerParams(
            collective_id=0, has_side_effects=True, vmem_limit_bytes=60 * 1024 * 1024
        ),
    )(residues[0], memory[0], lengths, cotangent[0], *parameters)
    shapes = [jax.ShapeDtypeStruct((BLOCK, WIDE), F32)] * 3
    for parameter in parameters:
        shapes.append(jax.ShapeDtypeStruct((parameter.shape[0] // (2 * CHIPS),) + parameter.shape[1:], F32))
    results = pl.pallas_call(
        place_kernel,
        out_shape=shapes,
        in_specs=(PLACED,),
        out_specs=(VMEM,) * len(shapes),
        scratch_shapes=(pltpu.VMEM((VECTOR_ROWS, BLOCK), F32), pltpu.SemaphoreType.DMA((17,))),
        compiler_params=pltpu.CompilerParams(vmem_limit_bytes=60 * 1024 * 1024),
    )(packed)
    return tuple(each[None] for each in results[:3]) + tuple(results[3:])


def solution(mesh):
    fits = mesh.shape["blk"] == 2 * CHIPS and mesh.shape["batch"] == 2
    return jax.shard_map(
        fused if fits else local,
        mesh=mesh,
        in_specs=(
            P("batch", "blk", None),
            P("batch", "blk", None),
            P("batch", None),
            P("batch", "blk", None),
            P(),
            P(),
            P(),
            P(),
            P(),
            P(),
            P(),
            P(),
            P(),
            P(),
            P(),
            P(),
            P(),
            P(),
            P(),
            P(),
            P(),
            P(),
            P(),
            P(),
            P(),
            P(),
            P(),
            P(),
        ),
        out_specs=(
            P("batch", "blk", None),
            P("batch", "blk", None),
            P("batch", "blk", None),
            P("blk"),
            P("blk"),
            P("blk", None),
            P("blk"),
            P("blk", None),
            P("blk", None),
            P("blk"),
            P("blk", None),
            P("blk"),
            P("blk"),
            P("blk"),
            P("blk", None),
            P("blk"),
            P("blk", None),
            P("blk", None),
            P("blk"),
            P("blk", None),
            P("blk"),
            P("blk"),
            P("blk"),
            P("blk", None),
            P("blk"),
            P("blk", None),
            P("blk"),
        ),
        check_vma=False,
    )
```

```python
import typing

import jax
import jax.numpy as jnp
from jax import lax
from jax.experimental import pallas as pl
from jax.experimental.pallas import tpu as pltpu
from jax.sharding import PartitionSpec as P

HEADS = 8


NEG = -1e30
EPS = 1e-05
SQRT_HALF = 0.7071067811865476
INV_ROOT_TAU = 0.3989422804014327


def layer_norm(values, gain, shift):
    average = jnp.mean(values, -1, keepdims=True)
    centred = values - average
    factor = lax.rsqrt(jnp.mean(centred * centred, -1, keepdims=True) + EPS)
    normal = centred * factor
    return (normal * gain + shift, normal, factor)


def norm_back(gradient, normal, factor, gain):
    weighted = gradient * gain
    average_one = jnp.mean(weighted, -1, keepdims=True)
    average_two = jnp.mean(weighted * normal, -1, keepdims=True)
    return (
        factor * (weighted - average_one - normal * average_two),
        jnp.sum(gradient * normal, 0),
        jnp.sum(gradient, 0),
    )


def gelu_value(values):
    return 0.5 * values * (1.0 + lax.erf(values * SQRT_HALF))


def gelu_slope(values):
    return (
        0.5 * (1.0 + lax.erf(values * SQRT_HALF))
        + values * jnp.exp(-0.5 * values * values) * INV_ROOT_TAU
    )


def heads_of(matrix):
    return matrix.reshape(matrix.shape[0], HEADS, -1)


def complex_ids(lengths_row, positions):
    bounds = jnp.cumsum(lengths_row)
    return jnp.sum((positions[:, None] >= bounds[None, :]).astype(jnp.int32), 1)


def visible(query_pos, query_doc, key_pos, key_doc, causal):
    allowed = query_doc[:, None] == key_doc[None, :]
    if causal:
        allowed = allowed & (key_pos[None, :] <= query_pos[:, None])
    return allowed


def project(left, right):
    return jnp.dot(left, right, preferred_element_type=jnp.float32)


def pass_through(pieces):
    return (pieces[0].astype(jnp.bfloat16), pieces[1].astype(jnp.bfloat16))


def empty_state(tokens, head_size):
    return (
        jnp.full((HEADS, tokens), NEG, jnp.float32),
        jnp.zeros((HEADS, tokens), jnp.float32),
        jnp.zeros((HEADS, tokens, head_size), jnp.float32),
    )


def finish(state_out):
    running_max, running_sum, summed = state_out
    attended = (summed / running_sum[..., None]).transpose(1, 0, 2)
    return (attended.reshape(attended.shape[0], -1), (running_max + jnp.log(running_sum)).T)


def spread_of(grad_low, attended):
    return jnp.sum(heads_of(grad_low).astype(jnp.float32) * heads_of(attended), -1)


def forward_fold(queries, query_pos, query_doc, lengths_row, causal, prepare, carried, pieces):
    factor = queries.shape[-1] ** (-0.5)
    piece_rows = pieces[0].shape[0]
    key_pos = jnp.arange(piece_rows, dtype=jnp.int32)
    allowed = visible(query_pos, query_doc, key_pos, complex_ids(lengths_row, key_pos), causal)

    def active(state_in):
        running_max, running_sum, summed = state_in
        key_rows, value_rows = prepare(pieces)
        scores = (
            jnp.einsum(
                "qhd,khd->hqk", queries, heads_of(key_rows), preferred_element_type=jnp.float32
            )
            * factor
        )
        scores = jnp.where(allowed[None], scores, NEG)
        new_max = jnp.maximum(running_max, jnp.max(scores, -1))
        weights = jnp.where(allowed[None], jnp.exp(scores - new_max[..., None]), 0.0)
        running_sum = jnp.sum(weights, -1)
        summed = jnp.einsum(
            "hqk,khd->hqd",
            weights.astype(jnp.bfloat16),
            heads_of(value_rows),
            preferred_element_type=jnp.float32,
        )
        return (new_max, running_sum, summed)

    return lax.cond(jnp.any(allowed), active, lambda state_in: state_in, carried)


def query_fold(
    queries, grad_out, log_total, spread, query_pos, query_doc, lengths_row, causal, prepare
):
    factor = queries.shape[-1] ** (-0.5)
    log_rows = log_total.T[..., None]
    spread_rows = spread.T[..., None]

    def fold(carried, pieces, offset):
        piece_rows = pieces[0].shape[0]
        key_pos = jnp.arange(piece_rows, dtype=jnp.int32)
        allowed = visible(query_pos, query_doc, key_pos, complex_ids(lengths_row, key_pos), causal)

        def active(accum):
            key_rows, value_rows = prepare(pieces)
            key_heads = heads_of(key_rows)
            scores = (
                jnp.einsum("qhd,khd->hqk", queries, key_heads, preferred_element_type=jnp.float32)
                * factor
            )
            scores = jnp.where(allowed[None], scores, NEG)
            weights = jnp.where(allowed[None], jnp.exp(scores - log_rows), 0.0)
            slopes = jnp.einsum(
                "qhd,khd->hqk", grad_out, heads_of(value_rows), preferred_element_type=jnp.float32
            )
            tilted = (weights * (slopes - spread_rows)).astype(jnp.bfloat16)
            return (
                jnp.einsum("hqk,khd->qhd", tilted, key_heads, preferred_element_type=jnp.float32)
                * factor
            )

        return lax.cond(jnp.any(allowed), active, lambda accum: accum, carried)

    return fold


def key_fold(key_heads, value_heads, key_pos, key_doc, lengths_row, causal):
    factor = key_heads.shape[-1] ** (-0.5)

    def fold(carried, pieces, offset):
        queries, grad_out, log_total, spread = pieces
        piece_rows = queries.shape[0]
        query_pos = jnp.arange(piece_rows, dtype=jnp.int32)
        allowed = visible(query_pos, complex_ids(lengths_row, query_pos), key_pos, key_doc, causal)

        def active(sums_in):
            query_heads = heads_of(queries.astype(jnp.bfloat16))
            grad_heads = heads_of(grad_out.astype(jnp.bfloat16))
            scores = (
                jnp.einsum(
                    "qhd,khd->hqk", query_heads, key_heads, preferred_element_type=jnp.float32
                )
                * factor
            )
            scores = jnp.where(allowed[None], scores, NEG)
            weights = jnp.where(allowed[None], jnp.exp(scores - log_total.T[..., None]), 0.0)
            grad_values = jnp.einsum(
                "hqk,qhd->khd",
                weights.astype(jnp.bfloat16),
                grad_heads,
                preferred_element_type=jnp.float32,
            )
            slopes = jnp.einsum(
                "qhd,khd->hqk", grad_heads, value_heads, preferred_element_type=jnp.float32
            )
            tilted = (weights * (slopes - spread.T[..., None])).astype(jnp.bfloat16)
            grad_keys = (
                jnp.einsum("hqk,qhd->khd", tilted, query_heads, preferred_element_type=jnp.float32)
                * factor
            )
            return (grad_keys, grad_values)

        return lax.cond(jnp.any(allowed), active, lambda sums_in: sums_in, carried)

    return fold


def mutual_fold(
    queries,
    grad_out,
    log_total,
    spread,
    key_heads,
    value_heads,
    positions,
    docs,
    lengths_row,
    carried,
    pieces,
    offset,
):
    toward_queries = query_fold(
        queries, grad_out, log_total, spread, positions, docs, lengths_row, True, pass_through
    )
    toward_keys = key_fold(key_heads, value_heads, positions, docs, lengths_row, True)
    grad_query_acc, grad_keys, grad_values = carried
    remote_q, remote_grad, remote_log, remote_spread, remote_k, remote_v = pieces
    grad_query_acc = toward_queries(grad_query_acc, (remote_k, remote_v), offset)
    grad_keys, grad_values = toward_keys(
        (grad_keys, grad_values), (remote_q, remote_grad, remote_log, remote_spread), offset
    )
    return (grad_query_acc, grad_keys, grad_values)


def local(
    residues,
    memory,
    lengths,
    cotangent,
    self_norm_gain,
    self_norm_bias,
    self_query,
    self_query_bias,
    self_key,
    self_value,
    self_value_bias,
    self_output,
    self_output_bias,
    cross_norm_gain,
    cross_norm_bias,
    cross_query,
    cross_query_bias,
    cross_key,
    cross_value,
    cross_value_bias,
    cross_output,
    cross_output_bias,
    feed_norm_gain,
    feed_norm_bias,
    feed_in,
    feed_in_bias,
    feed_out,
    feed_out_bias,
):
    tokens = residues.shape[1]
    model_width = residues.shape[2]
    head_size = model_width // HEADS
    device_rank = lax.axis_index("blk")
    positions = device_rank * tokens + jnp.arange(tokens, dtype=jnp.int32)
    lengths_row = lengths[0]
    complexes = complex_ids(lengths_row, positions)
    inputs = residues[0].astype(jnp.float32)
    encoded = memory[0]
    upstream = cotangent[0].astype(jnp.float32)
    normed_one, unit_one, factor_one = layer_norm(inputs, self_norm_gain, self_norm_bias)
    normed_one = normed_one.astype(jnp.bfloat16)
    self_q = (project(normed_one, self_query) + self_query_bias).astype(jnp.bfloat16)
    self_k = project(normed_one, self_key).astype(jnp.bfloat16)
    self_v = (project(normed_one, self_value) + self_value_bias).astype(jnp.bfloat16)
    state_out = forward_fold(
        heads_of(self_q),
        positions,
        complexes,
        lengths_row,
        True,
        pass_through,
        empty_state(tokens, head_size),
        (
            lax.all_gather(self_k, "blk", axis=0, tiled=True),
            lax.all_gather(self_v, "blk", axis=0, tiled=True),
        ),
    )
    self_attended, self_log = finish(state_out)
    self_low = self_attended.astype(jnp.bfloat16)
    after_self = inputs + project(self_low, self_output) + self_output_bias
    normed_two, unit_two, factor_two = layer_norm(after_self, cross_norm_gain, cross_norm_bias)
    normed_two = normed_two.astype(jnp.bfloat16)
    cross_q = (project(normed_two, cross_query) + cross_query_bias).astype(jnp.bfloat16)
    cross_k = project(encoded, cross_key).astype(jnp.bfloat16)
    cross_v = (project(encoded, cross_value) + cross_value_bias).astype(jnp.bfloat16)
    state_out = forward_fold(
        heads_of(cross_q),
        positions,
        complexes,
        lengths_row,
        False,
        pass_through,
        empty_state(tokens, head_size),
        (
            lax.all_gather(cross_k, "blk", axis=0, tiled=True),
            lax.all_gather(cross_v, "blk", axis=0, tiled=True),
        ),
    )
    cross_attended, cross_log = finish(state_out)
    cross_low = cross_attended.astype(jnp.bfloat16)
    after_cross = after_self + project(cross_low, cross_output) + cross_output_bias
    normed_three, unit_three, factor_three = layer_norm(after_cross, feed_norm_gain, feed_norm_bias)
    normed_three = normed_three.astype(jnp.bfloat16)
    inner = project(normed_three, feed_in) + feed_in_bias
    activation = gelu_value(inner).astype(jnp.bfloat16)
    layer_out = after_cross + project(activation, feed_out) + feed_out_bias
    grad_branch = upstream.astype(jnp.bfloat16)
    grad_feed_out_bias = jnp.sum(grad_branch.astype(jnp.float32), 0)
    grad_feed_out = jnp.einsum(
        "tf,td->fd", activation, grad_branch, preferred_element_type=jnp.float32
    )
    grad_active = jnp.einsum("td,fd->tf", grad_branch, feed_out, preferred_element_type=jnp.float32)
    grad_inner = (grad_active * gelu_slope(inner)).astype(jnp.bfloat16)
    grad_feed_in_bias = jnp.sum(grad_inner.astype(jnp.float32), 0)
    grad_feed_in = jnp.einsum(
        "td,tf->df", normed_three, grad_inner, preferred_element_type=jnp.float32
    )
    grad_normed = jnp.einsum("tf,df->td", grad_inner, feed_in, preferred_element_type=jnp.float32)
    norm_grad, grad_feed_norm_gain, grad_feed_norm_bias = norm_back(
        grad_normed, unit_three, factor_three, feed_norm_gain
    )
    upstream_two = upstream + norm_grad
    feed_parts = (
        grad_feed_norm_gain,
        grad_feed_norm_bias,
        grad_feed_in,
        grad_feed_in_bias,
        grad_feed_out,
        grad_feed_out_bias,
    )
    grad_branch = upstream_two.astype(jnp.bfloat16)
    grad_cross_output_bias = jnp.sum(grad_branch.astype(jnp.float32), 0)
    grad_cross_output = jnp.einsum(
        "tc,te->ce", cross_low, grad_branch, preferred_element_type=jnp.float32
    )
    grad_attended = jnp.einsum(
        "te,ce->tc", grad_branch, cross_output, preferred_element_type=jnp.float32
    ).astype(jnp.bfloat16)
    spread = spread_of(grad_attended, cross_attended)
    query_start = jnp.zeros((tokens, HEADS, head_size), jnp.float32)
    grad_query_acc = query_fold(
        heads_of(cross_q),
        heads_of(grad_attended),
        cross_log,
        spread,
        positions,
        complexes,
        lengths_row,
        False,
        pass_through,
    )(
        query_start,
        (
            lax.all_gather(cross_k, "blk", axis=0, tiled=True),
            lax.all_gather(cross_v, "blk", axis=0, tiled=True),
        ),
        jnp.int32(0),
    )
    grad_keys_acc, grad_values_acc = key_fold(
        heads_of(cross_k), heads_of(cross_v), positions, complexes, lengths_row, False
    )(
        (query_start, query_start),
        (
            lax.all_gather(cross_q.astype(jnp.float32), "blk", axis=0, tiled=True),
            lax.all_gather(grad_attended.astype(jnp.float32), "blk", axis=0, tiled=True),
            lax.all_gather(cross_log, "blk", axis=0, tiled=True),
            lax.all_gather(spread, "blk", axis=0, tiled=True),
        ),
        jnp.int32(0),
    )
    grad_cq = grad_query_acc.reshape(tokens, model_width).astype(jnp.bfloat16)
    grad_ck = grad_keys_acc.reshape(tokens, model_width).astype(jnp.bfloat16)
    grad_cv = grad_values_acc.reshape(tokens, model_width).astype(jnp.bfloat16)
    grad_cross_query = jnp.einsum(
        "tc,te->ce", normed_two, grad_cq, preferred_element_type=jnp.float32
    )
    grad_cross_query_bias = jnp.sum(grad_cq.astype(jnp.float32), 0)
    grad_cross_key = jnp.einsum("tc,te->ce", encoded, grad_ck, preferred_element_type=jnp.float32)
    grad_cross_value = jnp.einsum("tc,te->ce", encoded, grad_cv, preferred_element_type=jnp.float32)
    grad_cross_value_bias = jnp.sum(grad_cv.astype(jnp.float32), 0)
    memory_grad = jnp.einsum(
        "te,ce->tc", grad_ck, cross_key, preferred_element_type=jnp.float32
    ) + jnp.einsum("te,ce->tc", grad_cv, cross_value, preferred_element_type=jnp.float32)
    grad_normed = jnp.einsum("te,ce->tc", grad_cq, cross_query, preferred_element_type=jnp.float32)
    norm_grad, grad_cross_norm_gain, grad_cross_norm_bias = norm_back(
        grad_normed, unit_two, factor_two, cross_norm_gain
    )
    upstream_one = upstream_two + norm_grad
    cross_parts = (
        grad_cross_norm_gain,
        grad_cross_norm_bias,
        grad_cross_query,
        grad_cross_query_bias,
        grad_cross_key,
        grad_cross_value,
        grad_cross_value_bias,
        grad_cross_output,
        grad_cross_output_bias,
    )
    grad_branch = upstream_one.astype(jnp.bfloat16)
    grad_self_output_bias = jnp.sum(grad_branch.astype(jnp.float32), 0)
    grad_self_output = jnp.einsum(
        "tc,te->ce", self_low, grad_branch, preferred_element_type=jnp.float32
    )
    grad_attended = jnp.einsum(
        "te,ce->tc", grad_branch, self_output, preferred_element_type=jnp.float32
    ).astype(jnp.bfloat16)
    spread = spread_of(grad_attended, self_attended)
    grad_query_acc, grad_keys_acc, grad_values_acc = mutual_fold(
        heads_of(self_q),
        heads_of(grad_attended),
        self_log,
        spread,
        heads_of(self_k),
        heads_of(self_v),
        positions,
        complexes,
        lengths_row,
        (query_start, query_start, query_start),
        (
            lax.all_gather(self_q.astype(jnp.float32), "blk", axis=0, tiled=True),
            lax.all_gather(grad_attended.astype(jnp.float32), "blk", axis=0, tiled=True),
            lax.all_gather(self_log, "blk", axis=0, tiled=True),
            lax.all_gather(spread, "blk", axis=0, tiled=True),
            lax.all_gather(self_k.astype(jnp.float32), "blk", axis=0, tiled=True),
            lax.all_gather(self_v.astype(jnp.float32), "blk", axis=0, tiled=True),
        ),
        jnp.int32(0),
    )
    grad_sq = grad_query_acc.reshape(tokens, model_width).astype(jnp.bfloat16)
    grad_sk = grad_keys_acc.reshape(tokens, model_width).astype(jnp.bfloat16)
    grad_sv = grad_values_acc.reshape(tokens, model_width).astype(jnp.bfloat16)
    grad_self_query = jnp.einsum(
        "tc,te->ce", normed_one, grad_sq, preferred_element_type=jnp.float32
    )
    grad_self_query_bias = jnp.sum(grad_sq.astype(jnp.float32), 0)
    grad_self_key = jnp.einsum("tc,te->ce", normed_one, grad_sk, preferred_element_type=jnp.float32)
    grad_self_value = jnp.einsum(
        "tc,te->ce", normed_one, grad_sv, preferred_element_type=jnp.float32
    )
    grad_self_value_bias = jnp.sum(grad_sv.astype(jnp.float32), 0)
    grad_normed = (
        jnp.einsum("te,ce->tc", grad_sq, self_query, preferred_element_type=jnp.float32)
        + jnp.einsum("te,ce->tc", grad_sk, self_key, preferred_element_type=jnp.float32)
        + jnp.einsum("te,ce->tc", grad_sv, self_value, preferred_element_type=jnp.float32)
    )
    norm_grad, grad_self_norm_gain, grad_self_norm_bias = norm_back(
        grad_normed, unit_one, factor_one, self_norm_gain
    )
    residues_grad = upstream_one + norm_grad
    self_parts = (
        grad_self_norm_gain,
        grad_self_norm_bias,
        grad_self_query,
        grad_self_query_bias,
        grad_self_key,
        grad_self_value,
        grad_self_value_bias,
        grad_self_output,
        grad_self_output_bias,
    )
    ordered = (
        lax.psum_scatter(self_parts[0], "blk", scatter_dimension=0, tiled=True),
        lax.psum_scatter(self_parts[1], "blk", scatter_dimension=0, tiled=True),
        lax.psum_scatter(self_parts[2], "blk", scatter_dimension=0, tiled=True),
        lax.psum_scatter(self_parts[3], "blk", scatter_dimension=0, tiled=True),
        lax.psum_scatter(self_parts[4], "blk", scatter_dimension=0, tiled=True),
        lax.psum_scatter(self_parts[5], "blk", scatter_dimension=0, tiled=True),
        lax.psum_scatter(self_parts[6], "blk", scatter_dimension=0, tiled=True),
        lax.psum_scatter(self_parts[7], "blk", scatter_dimension=0, tiled=True),
        lax.psum_scatter(self_parts[8], "blk", scatter_dimension=0, tiled=True),
        lax.psum_scatter(cross_parts[0], "blk", scatter_dimension=0, tiled=True),
        lax.psum_scatter(cross_parts[1], "blk", scatter_dimension=0, tiled=True),
        lax.psum_scatter(cross_parts[2], "blk", scatter_dimension=0, tiled=True),
        lax.psum_scatter(cross_parts[3], "blk", scatter_dimension=0, tiled=True),
        lax.psum_scatter(cross_parts[4], "blk", scatter_dimension=0, tiled=True),
        lax.psum_scatter(cross_parts[5], "blk", scatter_dimension=0, tiled=True),
        lax.psum_scatter(cross_parts[6], "blk", scatter_dimension=0, tiled=True),
        lax.psum_scatter(cross_parts[7], "blk", scatter_dimension=0, tiled=True),
        lax.psum_scatter(cross_parts[8], "blk", scatter_dimension=0, tiled=True),
        lax.psum_scatter(feed_parts[0], "blk", scatter_dimension=0, tiled=True),
        lax.psum_scatter(feed_parts[1], "blk", scatter_dimension=0, tiled=True),
        lax.psum_scatter(feed_parts[2], "blk", scatter_dimension=0, tiled=True),
        lax.psum_scatter(feed_parts[3], "blk", scatter_dimension=0, tiled=True),
        lax.psum_scatter(feed_parts[4], "blk", scatter_dimension=0, tiled=True),
        lax.psum_scatter(feed_parts[5], "blk", scatter_dimension=0, tiled=True),
    )
    totals = lax.psum(
        (
            ordered[0],
            ordered[1],
            ordered[2],
            ordered[3],
            ordered[4],
            ordered[5],
            ordered[6],
            ordered[7],
            ordered[8],
            ordered[9],
            ordered[10],
            ordered[11],
            ordered[12],
            ordered[13],
            ordered[14],
            ordered[15],
            ordered[16],
            ordered[17],
            ordered[18],
            ordered[19],
            ordered[20],
            ordered[21],
            ordered[22],
            ordered[23],
        ),
        "batch",
    )
    return (layer_out[None], residues_grad[None], memory_grad[None]) + tuple(totals)


BLOCK = 128
HALF = 64
CHIPS = 8
HEAD = 64
WIDE = 512
HIDDEN = 2048
ROUND = 16
MASKED = -1e30
ONES_LANE = 5
SELF, CROSS = 0, 1
FAR_FIRST = (7, 6, 5, 4, 3, 2, 1)
MESH = pl.DeviceIdType.MESH
VMEM = pl.BlockSpec(memory_space=pltpu.VMEM)
SMEM = pl.BlockSpec(memory_space=pltpu.SMEM)
PLACED = pl.BlockSpec(memory_space=pl.ANY)
BF16, F32 = jnp.bfloat16, jnp.float32

SQ, SK, SV, SO, CQ, CK, CV, CO = range(8)
(
    ROW_SELF_GAIN, ROW_SELF_SHIFT, ROW_SQ, ROW_SV, ROW_SO, ROW_CROSS_GAIN, ROW_CROSS_SHIFT, ROW_CQ, ROW_CV, ROW_CO,
    ROW_FEED_GAIN, ROW_FEED_SHIFT, ROW_OUT, ROW_IN,
) = range(14)
VECTOR_ROWS = 24
UNIT_OUT, UNIT_IN = 0, 4
UNIT_OF = {CO: 8, SO: 9, CQ: 10, CK: 11, CV: 12, SQ: 13, SV: 14, SK: 15}
UNITS = 16
G_OUT, G_MORE, G_IN, G_REST, G_EARLY, G_CROSS, G_SQ, G_SV, G_SK = range(9)
SPANS = ((0, 2), (2, 4), (4, 6), (6, 9), (9, 11), (11, 13), (13, 14), (14, 15), (15, 16))
COLUMN_FIRST = (G_OUT, G_EARLY, G_SK)
BY_CORE, BY_FIRST, BY_SECOND, BY_PLANES, BY_NEAR, BY_FAR, BY_HALVES = range(7)
PLANES_IN_PAIRS = (G_OUT, G_MORE, G_IN, G_REST)
X_SQ, X_SO, X_CQ, X_CO, X_CDO, X_CDQ, X_SDO, X_SDQ = range(8)


class Operands(typing.NamedTuple):
    residues: VMEM
    memory: VMEM
    lengths: SMEM
    cotangent: VMEM
    self_norm_gain: VMEM
    self_norm_bias: VMEM
    self_query: PLACED
    self_query_bias: VMEM
    self_key: PLACED
    self_value: PLACED
    self_value_bias: VMEM
    self_output: PLACED
    self_output_bias: VMEM
    cross_norm_gain: VMEM
    cross_norm_bias: VMEM
    cross_query: PLACED
    cross_query_bias: VMEM
    cross_key: PLACED
    cross_value: PLACED
    cross_value_bias: VMEM
    cross_output: PLACED
    cross_output_bias: VMEM
    feed_norm_gain: VMEM
    feed_norm_bias: VMEM
    feed_in: PLACED
    feed_in_bias: VMEM
    feed_out: PLACED
    feed_out_bias: VMEM


AT_LAYER, AT_RESIDUES, AT_MEMORY, AT_SQUARE, AT_IN, AT_OUT, AT_VECTORS = 0, 128, 256, 384, 640, 768, 896
RESULT_ROWS = AT_VECTORS + VECTOR_ROWS


class Scratch(typing.NamedTuple):
    final: pltpu.VMEM((RESULT_ROWS, WIDE), F32)
    w_square: pltpu.VMEM((8, WIDE, WIDE), BF16)
    w_in: pltpu.VMEM((WIDE, HIDDEN), BF16)
    w_out: pltpu.VMEM((HIDDEN, WIDE), BF16)
    kv_out: pltpu.VMEM((2, CHIPS, BLOCK, BLOCK), BF16)
    kv: pltpu.VMEM((2, 2 * CHIPS, BLOCK, BLOCK), BF16)
    narrow_out: pltpu.VMEM((8, CHIPS, HALF, BLOCK), BF16)
    narrow: pltpu.VMEM((8, CHIPS, HALF, BLOCK), BF16)
    dkv_out: pltpu.VMEM((2, CHIPS, BLOCK, BLOCK), BF16)
    dkv: pltpu.VMEM((2, CHIPS, BLOCK, BLOCK), BF16)
    dkv_part: pltpu.VMEM((2, CHIPS, 2, BLOCK, BLOCK), BF16)
    dkv_other: pltpu.VMEM((2, CHIPS, BLOCK, BLOCK), BF16)
    dq_turned: pltpu.VMEM((BLOCK, 1024), F32)
    q_rows: pltpu.VMEM((2, 1024, BLOCK), BF16)
    q_features: pltpu.VMEM((2, 1024, BLOCK), BF16)
    do_rows: pltpu.VMEM((2, 1024, BLOCK), BF16)
    o_rows: pltpu.VMEM((2, 1024, BLOCK), F32)
    do_features: pltpu.VMEM((1024, BLOCK), BF16)
    query_features: pltpu.VMEM((1024, BLOCK), BF16)
    key_features: pltpu.VMEM((2048, BLOCK), BF16)
    causal: pltpu.VMEM((256, 512), F32)
    causal_turned: pltpu.VMEM((512, 256), F32)
    units: pltpu.VMEM((3, BLOCK, WIDE), F32)
    factors: pltpu.VMEM((3, BLOCK, BLOCK), F32)
    normed: pltpu.VMEM((3, BLOCK, WIDE), BF16)
    attended: pltpu.VMEM((2, BLOCK, WIDE), BF16)
    upstream: pltpu.VMEM((BLOCK, WIDE), F32)
    grad_active: pltpu.VMEM((BLOCK, HIDDEN), F32)
    active: pltpu.VMEM((BLOCK, HIDDEN), BF16)
    grad_inner: pltpu.VMEM((BLOCK, HIDDEN), BF16)
    parts: pltpu.VMEM((UNITS, 2, 2, 2, 2, 2, ROUND, WIDE), BF16)
    by_core: pltpu.VMEM((UNITS, 2, 2, 2, 2, ROUND, WIDE), BF16)
    by_side: pltpu.VMEM((UNITS, 2, 2, 2, ROUND, WIDE), BF16)
    by_column: pltpu.VMEM((UNITS, 2, 2, ROUND, WIDE), BF16)
    by_plane: pltpu.VMEM((3, UNITS, ROUND, WIDE), BF16)
    by_near: pltpu.VMEM((UNITS, 2, ROUND, WIDE), BF16)
    halves: pltpu.VMEM((2, UNITS, ROUND, WIDE), BF16)
    vectors: pltpu.VMEM((VECTOR_ROWS, WIDE), F32)
    vec_in: pltpu.VMEM((CHIPS, VECTOR_ROWS, BLOCK), F32)
    vec_four: pltpu.VMEM((4, VECTOR_ROWS, BLOCK), F32)
    load_sems: pltpu.SemaphoreType.DMA((10,))
    narrow_sems: pltpu.SemaphoreType.DMA((8,))
    kv_sems: pltpu.SemaphoreType.DMA((2, CHIPS))
    dkv_sems: pltpu.SemaphoreType.DMA((2,))
    pass_sems: pltpu.SemaphoreType.DMA((2,))
    share_sems: pltpu.SemaphoreType.DMA((2, 4))
    sent_sems: pltpu.SemaphoreType.DMA((7,))
    reduce_sems: pltpu.SemaphoreType.DMA((len(SPANS), 7))
    reduce_sent: pltpu.SemaphoreType.DMA((len(SPANS),))
    vec_sems: pltpu.SemaphoreType.DMA((2,))
    final_sems: pltpu.SemaphoreType.DMA((6,))


def specs_of(kind):
    return tuple(kind.__annotations__.values())


def dot_nn(left, right):
    return lax.dot_general(left, right, (((1,), (0,)), ((), ())), preferred_element_type=F32)


def dot_nt(left, right):
    return lax.dot_general(left, right, (((1,), (1,)), ((), ())), preferred_element_type=F32)


def dot_tn(left, right):
    return lax.dot_general(left, right, (((0,), (0,)), ((), ())), preferred_element_type=F32)


def low_lanes(shape):
    return lax.broadcasted_iota(jnp.int32, shape, len(shape) - 1) < HEAD


def turn(block):
    return pltpu.roll(block, HEAD, 1)


def swap(first, second):
    keep = low_lanes(first.shape)
    return jnp.where(keep, first, turn(second)), jnp.where(keep, turn(first), second)


def column_sum(low):
    return jnp.sum(low.astype(F32), 0, keepdims=True)


def flat(ref):
    return ref[...].reshape(1, -1)


def fused_kernel(*refs):
    count = len(specs_of(Operands))
    a, result, s = Operands(*refs[:count]), refs[count], Scratch(*refs[count + 1 :])

    rank = lax.axis_index("blk")
    side = lax.axis_index("batch")
    chip, core = lax.div(rank, 2), lax.rem(rank, 2)
    plane, column = lax.div(chip, 2), lax.rem(chip, 2)

    plane_high, plane_low = lax.div(plane, 2), lax.rem(plane, 2)

    def peer(turned):
        high, low, side_by = (
            1 - bit if turned >> at & 1 else bit for at, bit in ((2, plane_high), (1, plane_low), (0, column))
        )
        return 4 * high + 2 * low + side_by

    def at_rank(index):
        return {"blk": index}

    partner = at_rank(2 * chip + 1 - core)
    beside = at_rank(2 * (2 * plane + 1 - column) + core)
    across = {"batch": 1 - side}
    opposite = {"blk": 2 * chip + 1 - core, "batch": 1 - side}

    def remote(src, dst, sems, device):
        return pltpu.make_async_remote_copy(
            src_ref=src, dst_ref=dst, send_sem=sems[0], recv_sem=sems[1], device_id=device, device_id_type=MESH
        )

    SENT_NARROW, SENT_KV, SENT_PASS, SENT_DKV, SENT_SHARE, SENT_VECTOR, SENT_FOUR = (
        s.sent_sems.at[which] for which in range(7)
    )

    finished = []

    def final_put(at, values):
        s.final[pl.ds(at, values.shape[0]), : values.shape[1]] = values

    def final_start(at, rows):
        span = pl.ds(at, rows)
        finished.append(pltpu.make_async_copy(s.final.at[span], result.at[span], s.final_sems.at[len(finished)]))
        finished[-1].start()

    loads = {}

    def load(*pairs):
        for which, source in pairs:
            target = s.w_square.at[which] if which < 8 else (s.w_out, s.w_in)[which - 8]
            loads[which] = pltpu.make_async_copy(source, target, s.load_sems.at[which])
            loads[which].start()

    load((SK, a.self_key), (SV, a.self_value), (SQ, a.self_query))

    def weight(which):
        if which in loads:
            loads.pop(which).wait()
        return s.w_square[which] if which < 8 else (s.w_out, s.w_in)[which - 8]

    barrier = pltpu.get_barrier_semaphore()
    for shift in range(1, CHIPS):
        pl.semaphore_signal(barrier, inc=1, device_id=at_rank(2 * peer(shift) + core), device_id_type=MESH)
    for other in (partner, across, opposite):
        pl.semaphore_signal(barrier, inc=1, device_id=other, device_id_type=MESH)

    class Exchange:
        def __init__(self, outgoing, incoming, sems, sent, which, by_source=False):
            self.outgoing, self.incoming, self.by_source = outgoing.at[which], incoming.at[which], by_source
            self.sems, self.sent = sems.at[which], sent

        def slot(self, source):
            return self.incoming.at[2 * source + core if self.by_source else source]

        def pair(self, source):
            return (self.sent, self.sems.at[source] if self.by_source else self.sems)

        def start(self):
            for shift in FAR_FIRST:
                to = peer(shift)
                remote(self.outgoing.at[to], self.slot(chip), self.pair(chip), at_rank(2 * to + core)).start()
            self.slot(chip)[...] = self.outgoing[chip]

        def start_to(self, to):
            @pl.when(chip != to)
            def _():
                remote(self.outgoing.at[to], self.slot(chip), self.pair(chip), at_rank(2 * to + core)).start()

            @pl.when(chip == to)
            def _():
                self.slot(chip)[...] = self.outgoing[to]

        def wait(self, shift):
            source = peer(shift)
            remote(
                self.outgoing.at[source], self.slot(source), self.pair(source), at_rank(2 * source + core)
            ).wait_recv()

        def wait_all(self):
            seven = pl.ds(0, CHIPS - 1)
            remote(self.outgoing.at[seven], self.incoming.at[seven], (self.sent, self.sems), partner).wait_recv()

    narrow = [Exchange(s.narrow_out, s.narrow, s.narrow_sems, SENT_NARROW, which) for which in range(8)]
    keys_values = [Exchange(s.kv_out, s.kv, s.kv_sems, SENT_KV, which, True) for which in (SELF, CROSS)]
    key_grads = [Exchange(s.dkv_out, s.dkv, s.dkv_sems, SENT_DKV, which) for which in (SELF, CROSS)]

    def pass_on(kind):
        for shift in range(CHIPS):
            if shift > 0:
                keys_values[kind].wait(shift)
            slot = s.kv.at[kind, 2 * peer(shift) + core]
            remote(slot, slot, (SENT_PASS, s.pass_sems.at[kind]), partner).start()

    def pass_wait(kind):
        eight = s.kv.at[kind, pl.ds(0, CHIPS)]
        remote(eight, eight, (SENT_PASS, s.pass_sems.at[kind]), partner).wait_recv()

    def pack_groups(matrix, which):
        for pair in range(CHIPS // 2):
            group = matrix[:, BLOCK * pair : BLOCK * (pair + 1)]
            one, two = swap(group[:HALF], group[HALF:])
            s.narrow_out[which, 2 * pair] = one.astype(BF16)
            s.narrow_out[which, 2 * pair + 1] = two.astype(BF16)

    def unpack_groups(which):
        groups = []
        for pair in range(CHIPS // 2):
            groups.append(
                jnp.concatenate(
                    swap(s.narrow[which, 2 * pair].astype(F32), s.narrow[which, 2 * pair + 1].astype(F32)), 0
                )
            )
        return jnp.concatenate(groups, 1).astype(BF16)

    def pack_pairs(keys, values, kind):
        for pair in range(CHIPS // 2):
            lanes = slice(BLOCK * pair, BLOCK * (pair + 1))
            one, two = swap(keys[:, lanes], values[:, lanes])
            s.kv_out[kind, 2 * pair] = one.astype(BF16)
            s.kv_out[kind, 2 * pair + 1] = two.astype(BF16)

    def unpack_pairs(kind):
        pairs = [
            swap(s.dkv[kind, 2 * pair].astype(F32), s.dkv[kind, 2 * pair + 1].astype(F32)) for pair in range(CHIPS // 2)
        ]
        return tuple(jnp.concatenate(each, 1).astype(BF16) for each in zip(*pairs, strict=True))

    def plane_rank(other):
        return at_rank(2 * (2 * other + column) + core)

    def reduce_copies(stage, group):
        first, last = SPANS[group]
        span = pl.ds(first, last - first)
        sems = (s.reduce_sent.at[group], s.reduce_sems.at[group, stage])
        columns = (stage == BY_FIRST) == (group in COLUMN_FIRST)
        if stage == BY_CORE:
            return [remote(s.parts.at[span, :, :, :, 1 - core], s.by_core.at[span], sems, partner)]
        if stage == BY_FIRST:
            source = s.by_core.at[span, :, :, 1 - column] if columns else s.by_core.at[span, :, :, :, 1 - side]
            return [remote(source, s.by_side.at[span], sems, beside if columns else across)]
        if stage == BY_SECOND:
            source = s.by_side.at[span, :, :, 1 - column if columns else 1 - side]
            return [remote(source, s.by_column.at[span], sems, beside if columns else across)]
        if stage == BY_PLANES:
            others = [lax.rem(plane + shift, 4) for shift in range(1, 4)]
            return [
                remote(
                    s.by_column.at[span, lax.div(to, 2), lax.rem(to, 2)], s.by_plane.at[at, span], sems, plane_rank(to)
                )
                for at, to in enumerate(others)
            ]
        if stage == BY_NEAR:
            to = plane_rank(2 * plane_high + 1 - plane_low)
            return [remote(s.by_column.at[span, :, 1 - plane_low], s.by_near.at[span], sems, to)]
        if stage == BY_FAR:
            to = plane_rank(2 * (1 - plane_high) + plane_low)
            return [remote(s.by_near.at[span, 1 - plane_high], s.by_plane.at[0, span], sems, to)]
        return [remote(s.halves.at[side, span], s.halves.at[side, span], sems, across)]

    def reduce_whole(stage, group):
        if stage != BY_PLANES:
            return reduce_copies(stage, group)[0]
        blocks = s.by_plane.at[:, pl.ds(SPANS[group][0], SPANS[group][1] - SPANS[group][0])]
        return remote(blocks, blocks, (s.reduce_sent.at[group], s.reduce_sems.at[group, stage]), partner)

    def reduce_next(stage, group):
        if stage == BY_SECOND:
            return BY_NEAR if group in PLANES_IN_PAIRS else BY_PLANES
        return {BY_CORE: BY_FIRST, BY_FIRST: BY_SECOND, BY_NEAR: BY_FAR}.get(stage, BY_HALVES)

    def reduce_start(stage, group):
        for copy in reduce_copies(stage, group):
            copy.start()

    def reduce_finish(stage, group):
        first, last = SPANS[group]
        if stage == BY_HALVES:
            half = s.halves.at[1 - side, pl.ds(first, last - first)]
            remote(half, half, (s.reduce_sent.at[group], s.reduce_sems.at[group, stage]), across).wait_recv()
            return
        reduce_whole(stage, group).wait_recv()
        columns = (stage == BY_FIRST) == (group in COLUMN_FIRST)

        def add(unit, nothing):
            if stage == BY_CORE:
                s.by_core[unit] = s.by_core[unit] + s.parts[unit, :, :, :, core]
            if stage == BY_FIRST:
                own = s.by_core[unit, :, :, column] if columns else s.by_core[unit, :, :, :, side]
                s.by_side[unit] = s.by_side[unit] + own
            if stage == BY_SECOND:
                s.by_column[unit] = s.by_column[unit] + s.by_side[unit, :, :, column if columns else side]
            if stage == BY_PLANES:
                total = s.by_column[unit, plane_high, plane_low].astype(F32)
                for each in range(3):
                    total = total + s.by_plane[each, unit].astype(F32)
                s.halves[side, unit] = total.astype(BF16)
            if stage == BY_NEAR:
                s.by_near[unit] = s.by_near[unit] + s.by_column[unit, :, plane_low]
            if stage == BY_FAR:
                s.halves[side, unit] = s.by_plane[0, unit] + s.by_near[unit, plane_high]
            return nothing

        lax.fori_loop(first, last, add, 0)

    def reduce_step(stage, group):
        reduce_finish(stage, group)
        reduce_whole(stage, group).wait_send()
        reduce_start(reduce_next(stage, group), group)

    def put_unit(unit, value):
        s.parts[unit] = value.astype(BF16).reshape(2, 2, 2, 2, 2, ROUND, WIDE)

    def put_vector(row, values):
        if values.shape[1] == WIDE:
            s.vectors[pl.ds(row, 1), :] = values
            return
        for at in range(HIDDEN // BLOCK):
            group, piece = divmod(at, 4)
            s.vectors[pl.ds(row + piece, 1), BLOCK * group : BLOCK * (group + 1)] = values[
                :, BLOCK * at : BLOCK * (at + 1)
            ]

    def norm(values, which, gain, shift):
        average = jnp.mean(values, -1, keepdims=True)
        centred = values - average
        factor = lax.rsqrt(jnp.mean(centred * centred, -1, keepdims=True) + EPS)
        normal = centred * factor
        s.units[which] = normal
        s.factors[which] = jnp.broadcast_to(factor, (BLOCK, BLOCK))
        low = (normal * flat(gain) + flat(shift)).astype(BF16)
        s.normed[which] = low
        return low

    def norm_gradient(gradient, which, gain, row):
        normal = s.units[which]
        weighted = gradient * flat(gain)
        one = jnp.mean(weighted, -1, keepdims=True)
        two = jnp.mean(weighted * normal, -1, keepdims=True)
        put_vector(row, jnp.sum(gradient * normal, 0, keepdims=True))
        put_vector(row + 1, jnp.sum(gradient, 0, keepdims=True))
        return s.factors[which][:, :1] * (weighted - one - normal * two)

    def query_rows(kind, which):
        keep = low_lanes((HALF, BLOCK))
        for block in range(CHIPS):
            piece = s.narrow[which, block].astype(F32)
            both = jnp.concatenate([jnp.where(keep, piece, 0.0), jnp.where(keep, turn(piece), 0.0)], 0)
            s.q_rows[kind, pl.ds(block * BLOCK, BLOCK), :] = both.astype(BF16)

    def key_block(kind, chunk):
        rows = s.kv[kind, pl.ds(4 * chunk, 4)].reshape(512, BLOCK)
        return jnp.concatenate([rows, s.key_features[pl.ds(512 * chunk, 512), :]], 1)

    def with_column(features, column_values):
        lane = lax.broadcasted_iota(jnp.int32, features.shape, 1)
        full = jnp.broadcast_to(column_values, features.shape)
        high = full.astype(BF16).astype(F32)
        middle = (full - high).astype(BF16).astype(F32)
        low = full - high - middle
        for at, piece in enumerate((high, middle, low)):
            features = jnp.where(lane == ONES_LANE + at, piece, features)
        return features.astype(BF16)

    def attend(kind, causal, which):
        for part in range(4):
            rows = pl.ds(part * 256, 256)
            queries = jnp.concatenate([s.q_rows[kind, rows, :], s.query_features[rows, :]], 1)
            highest, summed = None, None
            chunks = range(part, -1, -1) if causal else range(4)
            for chunk in chunks:
                keys = key_block(kind, chunk)
                scores = dot_nt(queries, keys)
                if causal and chunk == part:
                    scores = scores + s.causal[...]
                reach = scores[:, :BLOCK]
                for at in range(1, 4):
                    reach = jnp.maximum(reach, scores[:, BLOCK * at : BLOCK * (at + 1)])
                reach = jnp.max(reach, 1, keepdims=True)
                if summed is None:
                    summed = dot_nn(jnp.exp(scores - reach).astype(BF16), keys)
                else:
                    reach = jnp.maximum(highest, reach)
                    summed = summed * jnp.exp(highest - reach) + dot_nn(jnp.exp(scores - reach).astype(BF16), keys)
                highest = reach
            total = summed[:, BLOCK + ONES_LANE : BLOCK + ONES_LANE + 1]
            result = summed[:, :BLOCK] / total
            s.o_rows[kind, rows, :] = result
            s.q_features[kind, rows, :] = with_column(
                s.query_features[rows, :].astype(F32), -(highest + jnp.log(total))
            )
            keep = low_lanes((HALF, BLOCK))
            for half in range(2):
                block = result[BLOCK * half : BLOCK * (half + 1)]
                s.narrow_out[which, 2 * part + half] = jnp.where(keep, turn(block[:HALF]), block[HALF:]).astype(BF16)

    def attend_back(kind, causal, which_in, which_out, between):
        keep = low_lanes((HALF, BLOCK))
        for block in range(CHIPS):
            rows = pl.ds(block * BLOCK, BLOCK)
            piece = s.narrow[which_in, block].astype(F32)
            gradient = jnp.concatenate([jnp.where(keep, 0.0, turn(piece)), jnp.where(keep, 0.0, piece)], 0)
            s.do_rows[kind, rows, :] = gradient.astype(BF16)
            spread = jnp.sum(gradient * s.o_rows[kind, rows, :], 1, keepdims=True)
            s.do_features[rows, :] = with_column(jnp.zeros((BLOCK, BLOCK), F32), -spread)
        for chunk in range(4):
            keys = key_block(kind, chunk)
            total = None
            for part in range(chunk if causal else 0, 4):
                rows = pl.ds(part * 256, 256)
                queries, grads = s.q_rows[kind, rows, :], s.do_rows[kind, rows, :]
                scores = dot_nt(keys, jnp.concatenate([queries, s.q_features[kind, rows, :]], 1))
                if causal and part == chunk:
                    scores = scores + s.causal_turned[...]
                weights = jnp.exp(scores)
                slopes = dot_nt(keys, jnp.concatenate([grads, s.do_features[rows, :]], 1))
                tilted = (weights * slopes).astype(BF16)
                shares = dot_nn(
                    jnp.concatenate([tilted, weights.astype(BF16)], 1), jnp.concatenate([queries, grads], 0)
                )
                total = shares if total is None else total + shares
                toward = dot_tn(keys[:, :BLOCK], tilted)
                s.dq_turned[:, rows] = toward if chunk == 0 else s.dq_turned[:, rows] + toward
            s.dkv_part[kind, 2 * chunk : 2 * chunk + 2] = total.astype(BF16).reshape(2, 2, BLOCK, BLOCK)
            between(chunk)
        if not causal:
            for part in range(4):
                put_dq(which_out, part)

    def put_dq(which, part):
        for block in (2 * part, 2 * part + 1):
            s.narrow_out[which, block] = (
                s.dq_turned[:HEAD, BLOCK * block : BLOCK * (block + 1)] * (HEAD**-0.5)
            ).astype(BF16)

    def turned_rows(which):
        return s.narrow[which].reshape(WIDE, BLOCK).astype(F32).T.astype(BF16)

    def share_copy(kind, part):
        chips = pl.ds(2 * part, 2)
        return remote(
            s.dkv_part.at[kind, chips, 1 - core], s.dkv_other.at[kind, chips], (SENT_SHARE, s.share_sems.at[kind, part]),
            partner,
        )

    def share_finish(kind, part):
        share_copy(kind, part).wait_recv()
        chips = slice(2 * part, 2 * part + 2)
        s.dkv_out[kind, chips] = s.dkv_part[kind, chips, core] + s.dkv_other[kind, chips]

    inputs = a.residues[...].astype(F32)
    normed = norm(inputs, 0, a.self_norm_gain, a.self_norm_bias)
    keys = dot_nn(normed, weight(SK))
    values = dot_nn(normed, weight(SV)) + flat(a.self_value_bias)
    pack_pairs(keys, values, SELF)
    pl.semaphore_wait(barrier, CHIPS + 2)
    keys_values[SELF].start()
    load((CK, a.cross_key), (CV, a.cross_value), (8, a.feed_out), (SO, a.self_output))
    load((CQ, a.cross_query), (CO, a.cross_output), (9, a.feed_in))
    queries = (dot_nn(normed, weight(SQ)) + flat(a.self_query_bias)) * (HEAD**-0.5)
    pack_groups(queries, X_SQ)
    narrow[X_SQ].start()

    encoded = a.memory[...]
    keys = dot_nn(encoded, weight(CK))
    values = dot_nn(encoded, weight(CV)) + flat(a.cross_value_bias)
    pack_pairs(keys, values, CROSS)

    bounds, reach = [], 0
    for at in range(4):
        reach = reach + a.lengths[0, at]
        bounds.append(reach)
    lane = lax.broadcasted_iota(jnp.int32, (BLOCK, BLOCK), 1)
    row = lax.broadcasted_iota(jnp.int32, (BLOCK, BLOCK), 0)

    def documents(position):
        found = jnp.zeros((BLOCK, BLOCK), jnp.int32)
        for bound in bounds:
            found = found + (position >= bound).astype(jnp.int32)
        return found

    ones = jnp.where((lane >= ONES_LANE) & (lane < ONES_LANE + 3), 1.0, 0.0)

    def key_features(block, nothing):
        other = documents(row + block * BLOCK) != lane
        s.key_features[pl.ds(block * BLOCK, BLOCK), :] = jnp.where((lane < ONES_LANE) & other, MASKED, ones).astype(
            BF16
        )
        return nothing

    lax.fori_loop(0, 2 * CHIPS, key_features, 0)

    def query_features(block, nothing):
        same = documents(row + (2 * block + core) * BLOCK) == lane
        s.query_features[pl.ds(block * BLOCK, BLOCK), :] = jnp.where((lane < ONES_LANE) & same, 1.0, 0.0).astype(BF16)
        return nothing

    lax.fori_loop(0, CHIPS, query_features, 0)

    def query_place(at):
        return at + core * BLOCK + jnp.where(at >= BLOCK, BLOCK, 0)

    at_row = lax.broadcasted_iota(jnp.int32, (256, 512), 0)
    at_key = lax.broadcasted_iota(jnp.int32, (256, 512), 1)
    s.causal[...] = jnp.where(at_key <= query_place(at_row), 0.0, MASKED)
    at_key = lax.broadcasted_iota(jnp.int32, (512, 256), 0)
    at_row = lax.broadcasted_iota(jnp.int32, (512, 256), 1)
    s.causal_turned[...] = jnp.where(at_key <= query_place(at_row), 0.0, MASKED)
    pass_on(SELF)
    keys_values[CROSS].start()
    narrow[X_SQ].wait_all()
    query_rows(SELF, X_SQ)
    pass_wait(SELF)
    attend(SELF, True, X_SO)
    narrow[X_SO].start()
    grads = a.cotangent[...]
    weight(8)
    for piece in range(4):
        lanes = slice(512 * piece, 512 * (piece + 1))
        s.grad_active[:, lanes] = dot_nt(grads, s.w_out[lanes, :])
    pass_on(CROSS)
    narrow[X_SO].wait_all()
    self_low = unpack_groups(X_SO)
    s.attended[SELF] = self_low
    after_self = inputs + dot_nn(self_low, weight(SO)) + flat(a.self_output_bias)

    normed = norm(after_self, 1, a.cross_norm_gain, a.cross_norm_bias)
    queries = (dot_nn(normed, weight(CQ)) + flat(a.cross_query_bias)) * (HEAD**-0.5)
    pack_groups(queries, X_CQ)
    narrow[X_CQ].start()
    pass_wait(CROSS)
    narrow[X_CQ].wait_all()
    query_rows(CROSS, X_CQ)
    attend(CROSS, False, X_CO)
    narrow[X_CO].start()
    weight(9)
    narrow[X_CO].wait_all()
    cross_low = unpack_groups(X_CO)
    s.attended[CROSS] = cross_low
    after_cross = after_self + dot_nn(cross_low, weight(CO)) + flat(a.cross_output_bias)

    normed = norm(after_cross, 2, a.feed_norm_gain, a.feed_norm_bias)
    back = None
    for piece in range(4):
        lanes = slice(512 * piece, 512 * (piece + 1))
        inner = dot_nn(normed, s.w_in[:, lanes]) + flat(a.feed_in_bias)[:, lanes]
        bell = 0.5 * (1.0 + lax.erf(inner * SQRT_HALF))
        active = (inner * bell).astype(BF16)
        slope = bell + inner * jnp.exp(-0.5 * inner * inner) * INV_ROOT_TAU
        grad_inner = (s.grad_active[:, lanes] * slope).astype(BF16)
        s.active[:, lanes] = active
        s.grad_inner[:, lanes] = grad_inner
        toward = dot_nt(grad_inner, s.w_in[:, lanes])
        back = toward if back is None else back + toward
    s.final[AT_LAYER : AT_LAYER + BLOCK, :] = after_cross + flat(a.feed_out_bias)
    upstream = a.cotangent[...].astype(F32)
    upstream = upstream + norm_gradient(back, 2, a.feed_norm_gain, ROW_FEED_GAIN)

    branch = upstream.astype(BF16)
    pack_groups(dot_nt(branch, weight(CO)), X_CDO)
    narrow[X_CDO].start()
    s.upstream[...] = upstream
    put_vector(ROW_OUT, column_sum(a.cotangent[...]))
    put_vector(ROW_IN, column_sum(s.grad_inner[...]))
    put_vector(ROW_CO, column_sum(branch))
    for piece in range(4):
        lanes = slice(512 * piece, 512 * (piece + 1))
        part = dot_tn(s.active[:, lanes], a.cotangent[...]).astype(BF16).reshape(2, 2, 4, 2, ROUND, WIDE)
        for each in range(4):
            s.parts[UNIT_OUT + each, piece // 2, piece % 2] = part[:, :, each]
    reduce_start(BY_CORE, G_OUT)
    reduce_start(BY_CORE, G_MORE)
    for piece in range(4):
        lanes = slice(512 * piece, 512 * (piece + 1))
        put_unit(UNIT_IN + piece, dot_tn(s.normed[2], s.grad_inner[:, lanes]))
        if piece == 1:
            reduce_start(BY_CORE, G_IN)
            reduce_step(BY_CORE, G_MORE)
    put_unit(UNIT_OF[CO], dot_tn(s.attended[CROSS], branch))
    reduce_start(BY_CORE, G_REST)
    final_put(AT_LAYER, s.final[AT_LAYER : AT_LAYER + BLOCK, :] + dot_nn(s.active[...], s.w_out[...]))
    final_start(AT_LAYER, BLOCK)
    narrow[X_CDO].wait_all()
    reduce_step(BY_CORE, G_OUT)

    def between_cross(chunk):
        if chunk == 0:
            reduce_step(BY_CORE, G_IN)
        share_copy(CROSS, chunk).start()

    attend_back(CROSS, False, X_CDO, X_CDQ, between_cross)
    narrow[X_CDQ].start()
    for part in range(4):
        share_finish(CROSS, part)
    key_grads[CROSS].start()
    reduce_step(BY_FIRST, G_OUT)
    reduce_step(BY_CORE, G_REST)
    reduce_step(BY_FIRST, G_MORE)
    narrow[X_CDQ].wait_all()
    grad_query = turned_rows(X_CDQ)
    gradient = dot_nt(grad_query, weight(CQ))
    upstream = s.upstream[...] + norm_gradient(gradient, 1, a.cross_norm_gain, ROW_CROSS_GAIN)

    branch = upstream.astype(BF16)
    pack_groups(dot_nt(branch, weight(SO)), X_SDO)
    narrow[X_SDO].start()
    reduce_step(BY_SECOND, G_OUT)
    reduce_step(BY_FIRST, G_IN)
    s.upstream[...] = upstream
    put_vector(ROW_SO, column_sum(branch))
    put_vector(ROW_CQ, column_sum(grad_query))
    put_unit(UNIT_OF[SO], dot_tn(s.attended[SELF], branch))
    put_unit(UNIT_OF[CQ], dot_tn(s.normed[1], grad_query))
    reduce_start(BY_CORE, G_EARLY)
    key_grads[CROSS].wait_all()
    grad_key, grad_value = unpack_pairs(CROSS)
    put_vector(ROW_CV, column_sum(grad_value))
    put_unit(UNIT_OF[CK], dot_tn(a.memory[...], grad_key))
    put_unit(UNIT_OF[CV], dot_tn(a.memory[...], grad_value))
    reduce_start(BY_CORE, G_CROSS)
    reduce_step(BY_CORE, G_EARLY)
    final_put(AT_MEMORY, dot_nt(grad_key, weight(CK)) + dot_nt(grad_value, weight(CV)))
    final_start(AT_MEMORY, BLOCK)
    narrow[X_SDO].wait_all()
    reduce_step(BY_SECOND, G_MORE)
    reduce_step(BY_FIRST, G_REST)

    def between_self(chunk):
        put_dq(X_SDQ, chunk)
        share_copy(SELF, chunk).start()
        if chunk > 0:
            send_shares(chunk - 1)
        for to in (2 * chunk, 2 * chunk + 1):
            narrow[X_SDQ].start_to(to)
        if chunk == 0:
            reduce_step(BY_CORE, G_CROSS)
            reduce_step(BY_NEAR, G_OUT)
        if chunk == 1:
            reduce_step(BY_SECOND, G_IN)

    def send_shares(part):
        share_finish(SELF, part)
        for to in (2 * part, 2 * part + 1):
            key_grads[SELF].start_to(to)

    attend_back(SELF, True, X_SDO, X_SDQ, between_self)
    send_shares(3)
    reduce_step(BY_NEAR, G_MORE)
    reduce_step(BY_FAR, G_OUT)
    reduce_step(BY_FIRST, G_EARLY)
    reduce_step(BY_FIRST, G_CROSS)
    narrow[X_SDQ].wait_all()
    grad_query = turned_rows(X_SDQ)
    normed = s.normed[0]
    put_unit(UNIT_OF[SQ], dot_tn(normed, grad_query))
    reduce_start(BY_CORE, G_SQ)
    reduce_step(BY_SECOND, G_REST)
    reduce_step(BY_NEAR, G_IN)
    reduce_step(BY_CORE, G_SQ)
    key_grads[SELF].wait_all()
    grad_key, grad_value = unpack_pairs(SELF)
    put_unit(UNIT_OF[SV], dot_tn(normed, grad_value))
    reduce_start(BY_CORE, G_SV)
    put_unit(UNIT_OF[SK], dot_tn(normed, grad_key))
    reduce_start(BY_CORE, G_SK)
    put_vector(ROW_SQ, column_sum(grad_query))
    put_vector(ROW_SV, column_sum(grad_value))
    gradient = dot_nt(grad_query, weight(SQ)) + dot_nt(grad_key, weight(SK)) + dot_nt(grad_value, weight(SV))
    reduce_step(BY_CORE, G_SV)
    reduce_step(BY_CORE, G_SK)
    final_put(AT_RESIDUES, s.upstream[...] + norm_gradient(gradient, 0, a.self_norm_gain, ROW_SELF_GAIN))
    final_start(AT_RESIDUES, BLOCK)

    def vector_copy(shift):
        if shift < CHIPS:
            to = peer(shift)
            lanes = pl.ds(pl.multiple_of(lax.div(to, 2) * BLOCK, BLOCK), BLOCK)
            sems = (SENT_VECTOR, s.vec_sems.at[0])
            return remote(s.vectors.at[:, lanes], s.vec_in.at[shift], sems, at_rank(2 * to + core))
        other = (partner, across, opposite)[shift - CHIPS]
        return remote(s.vec_four.at[0], s.vec_four.at[shift - CHIPS + 1], (SENT_FOUR, s.vec_sems.at[1]), other)

    def vector_all(step):
        rows = s.vec_in.at[pl.ds(1, 7)] if step == 0 else s.vec_four.at[pl.ds(1, 3)]
        return remote(rows, rows, ((SENT_VECTOR, SENT_FOUR)[step], s.vec_sems.at[step]), partner)

    s.vectors[pl.ds(17, VECTOR_ROWS - 17), :] = jnp.zeros((VECTOR_ROWS - 17, WIDE), F32)
    for shift in FAR_FIRST:
        vector_copy(shift).start()
    reduce_step(BY_SECOND, G_EARLY)
    reduce_step(BY_SECOND, G_CROSS)
    reduce_step(BY_NEAR, G_REST)
    reduce_step(BY_FAR, G_MORE)
    reduce_step(BY_FAR, G_IN)
    reduce_step(BY_FIRST, G_SQ)
    lanes = pl.ds(pl.multiple_of(lax.div(chip, 2) * BLOCK, BLOCK), BLOCK)
    total = s.vectors[:, lanes]
    vector_all(0).wait_recv()
    for shift in range(1, CHIPS):
        total = total + s.vec_in[shift]
    s.vec_four[0] = total
    for other in range(3):
        vector_copy(CHIPS + other).start()
    reduce_step(BY_FIRST, G_SK)
    reduce_step(BY_FIRST, G_SV)
    reduce_step(BY_PLANES, G_EARLY)
    reduce_step(BY_SECOND, G_SQ)
    vector_all(1).wait_recv()
    total = (s.vec_four[0] + s.vec_four[2]) + (s.vec_four[1] + s.vec_four[3])
    place_in_group = lax.rem(rank, 4)
    s.final[pl.ds(AT_VECTORS, VECTOR_ROWS), :BLOCK] = pltpu.roll(total, lax.rem(BLOCK - 32 * place_in_group, BLOCK), 1)
    own = jnp.zeros((1, BLOCK), F32)
    for each in range(4):
        own = own + jnp.where(place_in_group == each, total[ROW_IN + each : ROW_IN + each + 1], 0.0)
    s.final[pl.ds(AT_VECTORS + ROW_IN, 1), :BLOCK] = own
    final_start(AT_VECTORS, VECTOR_ROWS)

    def unit_value(unit):
        return jnp.concatenate([s.halves[0, unit], s.halves[1, unit]], 0).astype(F32)

    def put_final_unit(at, unit):
        final_put(at, unit_value(unit))

    reduce_step(BY_SECOND, G_SK)
    reduce_step(BY_SECOND, G_SV)
    reduce_step(BY_FAR, G_REST)
    reduce_step(BY_PLANES, G_CROSS)
    reduce_step(BY_PLANES, G_SQ)
    for group in (G_OUT, G_MORE, G_IN, G_REST):
        reduce_finish(BY_HALVES, group)
    for piece in range(4):
        put_final_unit(AT_OUT + 32 * piece, UNIT_OUT + piece)
        put_final_unit(AT_IN + 32 * piece, UNIT_IN + piece)
    final_start(AT_IN, 2 * BLOCK)
    reduce_finish(BY_HALVES, G_EARLY)
    reduce_finish(BY_HALVES, G_CROSS)
    for which in (CO, CQ, CK, CV, SO):
        put_final_unit(AT_SQUARE + 32 * which, UNIT_OF[which])
    reduce_step(BY_PLANES, G_SK)
    reduce_step(BY_PLANES, G_SV)
    reduce_finish(BY_HALVES, G_SQ)
    reduce_finish(BY_HALVES, G_SK)
    reduce_finish(BY_HALVES, G_SV)
    for which in (SQ, SK, SV):
        put_final_unit(AT_SQUARE + 32 * which, UNIT_OF[which])
    final_start(AT_SQUARE, 256)
    for copy in finished:
        copy.wait()
    for group in range(len(SPANS)):
        reduce_whole(BY_HALVES, group).wait_send()
    seven = pl.ds(0, CHIPS - 1)
    for sent, blocks in (
        (SENT_NARROW, s.narrow_out.at[:, seven]), (SENT_KV, s.kv_out.at[:, seven]), (SENT_DKV, s.dkv_out.at[:, seven]),
        (SENT_PASS, s.kv.at[:, pl.ds(0, CHIPS)]), (SENT_SHARE, s.dkv_other),
    ):
        remote(blocks, blocks, (sent, s.vec_sems.at[0]), partner).wait_send()
    vector_all(0).wait_send()
    vector_all(1).wait_send()


def place_kernel(packed, *refs):
    results, vectors, sems = refs[:-2], refs[-2], refs[-1]
    copies = []

    def place(at, target):
        source = packed.at[pl.ds(at, target.shape[0]), pl.ds(0, target.shape[1])]
        copies.append(pltpu.make_async_copy(source, target, sems.at[len(copies)]))
        copies[-1].start()

    place(AT_VECTORS, vectors)
    for at, target in zip((AT_LAYER, AT_RESIDUES, AT_MEMORY), results[:3], strict=True):
        place(at, target)
    for which, at in SQUARE_RESULTS.items():
        place(AT_SQUARE + 32 * which, results[at])
    for piece in range(4):
        place(AT_IN + 32 * piece, results[23].at[:, pl.ds(512 * piece, 512)])
    place(AT_OUT, results[25])
    copies[0].wait()
    rows = vectors[...]
    for row, at in VECTOR_RESULTS.items():
        results[at][...] = rows[row, : results[at].shape[0]]
    for copy in copies[1:]:
        copy.wait()


SQUARE_RESULTS = {SQ: 5, SK: 7, SV: 8, SO: 10, CQ: 14, CK: 16, CV: 17, CO: 19}
VECTOR_RESULTS = {
    ROW_SELF_GAIN: 3, ROW_SELF_SHIFT: 4, ROW_SQ: 6, ROW_SV: 9, ROW_SO: 11, ROW_CROSS_GAIN: 12, ROW_CROSS_SHIFT: 13,
    ROW_CQ: 15, ROW_CV: 18, ROW_CO: 20, ROW_FEED_GAIN: 21, ROW_FEED_SHIFT: 22, ROW_OUT: 26, ROW_IN: 24,
}


def fused(residues, memory, lengths, cotangent, *parameters):
    packed = pl.pallas_call(
        fused_kernel,
        out_shape=jax.ShapeDtypeStruct((RESULT_ROWS, WIDE), F32),
        in_specs=specs_of(Operands),
        out_specs=PLACED,
        scratch_shapes=specs_of(Scratch),
        compiler_params=pltpu.CompilerParams(
            collective_id=0, has_side_effects=True, vmem_limit_bytes=60 * 1024 * 1024
        ),
    )(residues[0], memory[0], lengths, cotangent[0], *parameters)
    shapes = [jax.ShapeDtypeStruct((BLOCK, WIDE), F32)] * 3
    for parameter in parameters:
        shapes.append(jax.ShapeDtypeStruct((parameter.shape[0] // (2 * CHIPS),) + parameter.shape[1:], F32))
    results = pl.pallas_call(
        place_kernel,
        out_shape=shapes,
        in_specs=(PLACED,),
        out_specs=(VMEM,) * len(shapes),
        scratch_shapes=(pltpu.VMEM((VECTOR_ROWS, BLOCK), F32), pltpu.SemaphoreType.DMA((17,))),
        compiler_params=pltpu.CompilerParams(vmem_limit_bytes=60 * 1024 * 1024),
    )(packed)
    return tuple(each[None] for each in results[:3]) + tuple(results[3:])


def solution(mesh):
    fits = mesh.shape["blk"] == 2 * CHIPS and mesh.shape["batch"] == 2
    return jax.shard_map(
        fused if fits else local,
        mesh=mesh,
        in_specs=(
            P("batch", "blk", None),
            P("batch", "blk", None),
            P("batch", None),
            P("batch", "blk", None),
            P(),
            P(),
            P(),
            P(),
            P(),
            P(),
            P(),
            P(),
            P(),
            P(),
            P(),
            P(),
            P(),
            P(),
            P(),
            P(),
            P(),
            P(),
            P(),
            P(),
            P(),
            P(),
            P(),
            P(),
        ),
        out_specs=(
            P("batch", "blk", None),
            P("batch", "blk", None),
            P("batch", "blk", None),
            P("blk"),
            P("blk"),
            P("blk", None),
            P("blk"),
            P("blk", None),
            P("blk", None),
            P("blk"),
            P("blk", None),
            P("blk"),
            P("blk"),
            P("blk"),
            P("blk", None),
            P("blk"),
            P("blk", None),
            P("blk", None),
            P("blk"),
            P("blk", None),
            P("blk"),
            P("blk"),
            P("blk"),
            P("blk", None),
            P("blk"),
            P("blk", None),
            P("blk"),
        ),
        check_vma=False,
    )
```

```python
import typing

import jax
import jax.numpy as jnp
from jax import lax
from jax.experimental import pallas as pl
from jax.experimental.pallas import tpu as pltpu
from jax.sharding import PartitionSpec as P

HEADS = 8


NEG = -1e30
EPS = 1e-05
SQRT_HALF = 0.7071067811865476
INV_ROOT_TAU = 0.3989422804014327


def layer_norm(values, gain, shift):
    average = jnp.mean(values, -1, keepdims=True)
    centred = values - average
    factor = lax.rsqrt(jnp.mean(centred * centred, -1, keepdims=True) + EPS)
    normal = centred * factor
    return (normal * gain + shift, normal, factor)


def norm_back(gradient, normal, factor, gain):
    weighted = gradient * gain
    average_one = jnp.mean(weighted, -1, keepdims=True)
    average_two = jnp.mean(weighted * normal, -1, keepdims=True)
    return (
        factor * (weighted - average_one - normal * average_two),
        jnp.sum(gradient * normal, 0),
        jnp.sum(gradient, 0),
    )


def gelu_value(values):
    return 0.5 * values * (1.0 + lax.erf(values * SQRT_HALF))


def gelu_slope(values):
    return (
        0.5 * (1.0 + lax.erf(values * SQRT_HALF))
        + values * jnp.exp(-0.5 * values * values) * INV_ROOT_TAU
    )


def heads_of(matrix):
    return matrix.reshape(matrix.shape[0], HEADS, -1)


def complex_ids(lengths_row, positions):
    bounds = jnp.cumsum(lengths_row)
    return jnp.sum((positions[:, None] >= bounds[None, :]).astype(jnp.int32), 1)


def visible(query_pos, query_doc, key_pos, key_doc, causal):
    allowed = query_doc[:, None] == key_doc[None, :]
    if causal:
        allowed = allowed & (key_pos[None, :] <= query_pos[:, None])
    return allowed


def project(left, right):
    return jnp.dot(left, right, preferred_element_type=jnp.float32)


def pass_through(pieces):
    return (pieces[0].astype(jnp.bfloat16), pieces[1].astype(jnp.bfloat16))


def empty_state(tokens, head_size):
    return (
        jnp.full((HEADS, tokens), NEG, jnp.float32),
        jnp.zeros((HEADS, tokens), jnp.float32),
        jnp.zeros((HEADS, tokens, head_size), jnp.float32),
    )


def finish(state_out):
    running_max, running_sum, summed = state_out
    attended = (summed / running_sum[..., None]).transpose(1, 0, 2)
    return (attended.reshape(attended.shape[0], -1), (running_max + jnp.log(running_sum)).T)


def spread_of(grad_low, attended):
    return jnp.sum(heads_of(grad_low).astype(jnp.float32) * heads_of(attended), -1)


def forward_fold(queries, query_pos, query_doc, lengths_row, causal, prepare, carried, pieces):
    factor = queries.shape[-1] ** (-0.5)
    piece_rows = pieces[0].shape[0]
    key_pos = jnp.arange(piece_rows, dtype=jnp.int32)
    allowed = visible(query_pos, query_doc, key_pos, complex_ids(lengths_row, key_pos), causal)

    def active(state_in):
        running_max, running_sum, summed = state_in
        key_rows, value_rows = prepare(pieces)
        scores = (
            jnp.einsum(
                "qhd,khd->hqk", queries, heads_of(key_rows), preferred_element_type=jnp.float32
            )
            * factor
        )
        scores = jnp.where(allowed[None], scores, NEG)
        new_max = jnp.maximum(running_max, jnp.max(scores, -1))
        weights = jnp.where(allowed[None], jnp.exp(scores - new_max[..., None]), 0.0)
        running_sum = jnp.sum(weights, -1)
        summed = jnp.einsum(
            "hqk,khd->hqd",
            weights.astype(jnp.bfloat16),
            heads_of(value_rows),
            preferred_element_type=jnp.float32,
        )
        return (new_max, running_sum, summed)

    return lax.cond(jnp.any(allowed), active, lambda state_in: state_in, carried)


def query_fold(
    queries, grad_out, log_total, spread, query_pos, query_doc, lengths_row, causal, prepare
):
    factor = queries.shape[-1] ** (-0.5)
    log_rows = log_total.T[..., None]
    spread_rows = spread.T[..., None]

    def fold(carried, pieces, offset):
        piece_rows = pieces[0].shape[0]
        key_pos = jnp.arange(piece_rows, dtype=jnp.int32)
        allowed = visible(query_pos, query_doc, key_pos, complex_ids(lengths_row, key_pos), causal)

        def active(accum):
            key_rows, value_rows = prepare(pieces)
            key_heads = heads_of(key_rows)
            scores = (
                jnp.einsum("qhd,khd->hqk", queries, key_heads, preferred_element_type=jnp.float32)
                * factor
            )
            scores = jnp.where(allowed[None], scores, NEG)
            weights = jnp.where(allowed[None], jnp.exp(scores - log_rows), 0.0)
            slopes = jnp.einsum(
                "qhd,khd->hqk", grad_out, heads_of(value_rows), preferred_element_type=jnp.float32
            )
            tilted = (weights * (slopes - spread_rows)).astype(jnp.bfloat16)
            return (
                jnp.einsum("hqk,khd->qhd", tilted, key_heads, preferred_element_type=jnp.float32)
                * factor
            )

        return lax.cond(jnp.any(allowed), active, lambda accum: accum, carried)

    return fold


def key_fold(key_heads, value_heads, key_pos, key_doc, lengths_row, causal):
    factor = key_heads.shape[-1] ** (-0.5)

    def fold(carried, pieces, offset):
        queries, grad_out, log_total, spread = pieces
        piece_rows = queries.shape[0]
        query_pos = jnp.arange(piece_rows, dtype=jnp.int32)
        allowed = visible(query_pos, complex_ids(lengths_row, query_pos), key_pos, key_doc, causal)

        def active(sums_in):
            query_heads = heads_of(queries.astype(jnp.bfloat16))
            grad_heads = heads_of(grad_out.astype(jnp.bfloat16))
            scores = (
                jnp.einsum(
                    "qhd,khd->hqk", query_heads, key_heads, preferred_element_type=jnp.float32
                )
                * factor
            )
            scores = jnp.where(allowed[None], scores, NEG)
            weights = jnp.where(allowed[None], jnp.exp(scores - log_total.T[..., None]), 0.0)
            grad_values = jnp.einsum(
                "hqk,qhd->khd",
                weights.astype(jnp.bfloat16),
                grad_heads,
                preferred_element_type=jnp.float32,
            )
            slopes = jnp.einsum(
                "qhd,khd->hqk", grad_heads, value_heads, preferred_element_type=jnp.float32
            )
            tilted = (weights * (slopes - spread.T[..., None])).astype(jnp.bfloat16)
            grad_keys = (
                jnp.einsum("hqk,qhd->khd", tilted, query_heads, preferred_element_type=jnp.float32)
                * factor
            )
            return (grad_keys, grad_values)

        return lax.cond(jnp.any(allowed), active, lambda sums_in: sums_in, carried)

    return fold


def mutual_fold(
    queries,
    grad_out,
    log_total,
    spread,
    key_heads,
    value_heads,
    positions,
    docs,
    lengths_row,
    carried,
    pieces,
    offset,
):
    toward_queries = query_fold(
        queries, grad_out, log_total, spread, positions, docs, lengths_row, True, pass_through
    )
    toward_keys = key_fold(key_heads, value_heads, positions, docs, lengths_row, True)
    grad_query_acc, grad_keys, grad_values = carried
    remote_q, remote_grad, remote_log, remote_spread, remote_k, remote_v = pieces
    grad_query_acc = toward_queries(grad_query_acc, (remote_k, remote_v), offset)
    grad_keys, grad_values = toward_keys(
        (grad_keys, grad_values), (remote_q, remote_grad, remote_log, remote_spread), offset
    )
    return (grad_query_acc, grad_keys, grad_values)


def local(
    residues,
    memory,
    lengths,
    cotangent,
    self_norm_gain,
    self_norm_bias,
    self_query,
    self_query_bias,
    self_key,
    self_value,
    self_value_bias,
    self_output,
    self_output_bias,
    cross_norm_gain,
    cross_norm_bias,
    cross_query,
    cross_query_bias,
    cross_key,
    cross_value,
    cross_value_bias,
    cross_output,
    cross_output_bias,
    feed_norm_gain,
    feed_norm_bias,
    feed_in,
    feed_in_bias,
    feed_out,
    feed_out_bias,
):
    tokens = residues.shape[1]
    model_width = residues.shape[2]
    head_size = model_width // HEADS
    device_rank = lax.axis_index("blk")
    positions = device_rank * tokens + jnp.arange(tokens, dtype=jnp.int32)
    lengths_row = lengths[0]
    complexes = complex_ids(lengths_row, positions)
    inputs = residues[0].astype(jnp.float32)
    encoded = memory[0]
    upstream = cotangent[0].astype(jnp.float32)
    normed_one, unit_one, factor_one = layer_norm(inputs, self_norm_gain, self_norm_bias)
    normed_one = normed_one.astype(jnp.bfloat16)
    self_q = (project(normed_one, self_query) + self_query_bias).astype(jnp.bfloat16)
    self_k = project(normed_one, self_key).astype(jnp.bfloat16)
    self_v = (project(normed_one, self_value) + self_value_bias).astype(jnp.bfloat16)
    state_out = forward_fold(
        heads_of(self_q),
        positions,
        complexes,
        lengths_row,
        True,
        pass_through,
        empty_state(tokens, head_size),
        (
            lax.all_gather(self_k, "blk", axis=0, tiled=True),
            lax.all_gather(self_v, "blk", axis=0, tiled=True),
        ),
    )
    self_attended, self_log = finish(state_out)
    self_low = self_attended.astype(jnp.bfloat16)
    after_self = inputs + project(self_low, self_output) + self_output_bias
    normed_two, unit_two, factor_two = layer_norm(after_self, cross_norm_gain, cross_norm_bias)
    normed_two = normed_two.astype(jnp.bfloat16)
    cross_q = (project(normed_two, cross_query) + cross_query_bias).astype(jnp.bfloat16)
    cross_k = project(encoded, cross_key).astype(jnp.bfloat16)
    cross_v = (project(encoded, cross_value) + cross_value_bias).astype(jnp.bfloat16)
    state_out = forward_fold(
        heads_of(cross_q),
        positions,
        complexes,
        lengths_row,
        False,
        pass_through,
        empty_state(tokens, head_size),
        (
            lax.all_gather(cross_k, "blk", axis=0, tiled=True),
            lax.all_gather(cross_v, "blk", axis=0, tiled=True),
        ),
    )
    cross_attended, cross_log = finish(state_out)
    cross_low = cross_attended.astype(jnp.bfloat16)
    after_cross = after_self + project(cross_low, cross_output) + cross_output_bias
    normed_three, unit_three, factor_three = layer_norm(after_cross, feed_norm_gain, feed_norm_bias)
    normed_three = normed_three.astype(jnp.bfloat16)
    inner = project(normed_three, feed_in) + feed_in_bias
    activation = gelu_value(inner).astype(jnp.bfloat16)
    layer_out = after_cross + project(activation, feed_out) + feed_out_bias
    grad_branch = upstream.astype(jnp.bfloat16)
    grad_feed_out_bias = jnp.sum(grad_branch.astype(jnp.float32), 0)
    grad_feed_out = jnp.einsum(
        "tf,td->fd", activation, grad_branch, preferred_element_type=jnp.float32
    )
    grad_active = jnp.einsum("td,fd->tf", grad_branch, feed_out, preferred_element_type=jnp.float32)
    grad_inner = (grad_active * gelu_slope(inner)).astype(jnp.bfloat16)
    grad_feed_in_bias = jnp.sum(grad_inner.astype(jnp.float32), 0)
    grad_feed_in = jnp.einsum(
        "td,tf->df", normed_three, grad_inner, preferred_element_type=jnp.float32
    )
    grad_normed = jnp.einsum("tf,df->td", grad_inner, feed_in, preferred_element_type=jnp.float32)
    norm_grad, grad_feed_norm_gain, grad_feed_norm_bias = norm_back(
        grad_normed, unit_three, factor_three, feed_norm_gain
    )
    upstream_two = upstream + norm_grad
    feed_parts = (
        grad_feed_norm_gain,
        grad_feed_norm_bias,
        grad_feed_in,
        grad_feed_in_bias,
        grad_feed_out,
        grad_feed_out_bias,
    )
    grad_branch = upstream_two.astype(jnp.bfloat16)
    grad_cross_output_bias = jnp.sum(grad_branch.astype(jnp.float32), 0)
    grad_cross_output = jnp.einsum(
        "tc,te->ce", cross_low, grad_branch, preferred_element_type=jnp.float32
    )
    grad_attended = jnp.einsum(
        "te,ce->tc", grad_branch, cross_output, preferred_element_type=jnp.float32
    ).astype(jnp.bfloat16)
    spread = spread_of(grad_attended, cross_attended)
    query_start = jnp.zeros((tokens, HEADS, head_size), jnp.float32)
    grad_query_acc = query_fold(
        heads_of(cross_q),
        heads_of(grad_attended),
        cross_log,
        spread,
        positions,
        complexes,
        lengths_row,
        False,
        pass_through,
    )(
        query_start,
        (
            lax.all_gather(cross_k, "blk", axis=0, tiled=True),
            lax.all_gather(cross_v, "blk", axis=0, tiled=True),
        ),
        jnp.int32(0),
    )
    grad_keys_acc, grad_values_acc = key_fold(
        heads_of(cross_k), heads_of(cross_v), positions, complexes, lengths_row, False
    )(
        (query_start, query_start),
        (
            lax.all_gather(cross_q.astype(jnp.float32), "blk", axis=0, tiled=True),
            lax.all_gather(grad_attended.astype(jnp.float32), "blk", axis=0, tiled=True),
            lax.all_gather(cross_log, "blk", axis=0, tiled=True),
            lax.all_gather(spread, "blk", axis=0, tiled=True),
        ),
        jnp.int32(0),
    )
    grad_cq = grad_query_acc.reshape(tokens, model_width).astype(jnp.bfloat16)
    grad_ck = grad_keys_acc.reshape(tokens, model_width).astype(jnp.bfloat16)
    grad_cv = grad_values_acc.reshape(tokens, model_width).astype(jnp.bfloat16)
    grad_cross_query = jnp.einsum(
        "tc,te->ce", normed_two, grad_cq, preferred_element_type=jnp.float32
    )
    grad_cross_query_bias = jnp.sum(grad_cq.astype(jnp.float32), 0)
    grad_cross_key = jnp.einsum("tc,te->ce", encoded, grad_ck, preferred_element_type=jnp.float32)
    grad_cross_value = jnp.einsum("tc,te->ce", encoded, grad_cv, preferred_element_type=jnp.float32)
    grad_cross_value_bias = jnp.sum(grad_cv.astype(jnp.float32), 0)
    memory_grad = jnp.einsum(
        "te,ce->tc", grad_ck, cross_key, preferred_element_type=jnp.float32
    ) + jnp.einsum("te,ce->tc", grad_cv, cross_value, preferred_element_type=jnp.float32)
    grad_normed = jnp.einsum("te,ce->tc", grad_cq, cross_query, preferred_element_type=jnp.float32)
    norm_grad, grad_cross_norm_gain, grad_cross_norm_bias = norm_back(
        grad_normed, unit_two, factor_two, cross_norm_gain
    )
    upstream_one = upstream_two + norm_grad
    cross_parts = (
        grad_cross_norm_gain,
        grad_cross_norm_bias,
        grad_cross_query,
        grad_cross_query_bias,
        grad_cross_key,
        grad_cross_value,
        grad_cross_value_bias,
        grad_cross_output,
        grad_cross_output_bias,
    )
    grad_branch = upstream_one.astype(jnp.bfloat16)
    grad_self_output_bias = jnp.sum(grad_branch.astype(jnp.float32), 0)
    grad_self_output = jnp.einsum(
        "tc,te->ce", self_low, grad_branch, preferred_element_type=jnp.float32
    )
    grad_attended = jnp.einsum(
        "te,ce->tc", grad_branch, self_output, preferred_element_type=jnp.float32
    ).astype(jnp.bfloat16)
    spread = spread_of(grad_attended, self_attended)
    grad_query_acc, grad_keys_acc, grad_values_acc = mutual_fold(
        heads_of(self_q),
        heads_of(grad_attended),
        self_log,
        spread,
        heads_of(self_k),
        heads_of(self_v),
        positions,
        complexes,
        lengths_row,
        (query_start, query_start, query_start),
        (
            lax.all_gather(self_q.astype(jnp.float32), "blk", axis=0, tiled=True),
            lax.all_gather(grad_attended.astype(jnp.float32), "blk", axis=0, tiled=True),
            lax.all_gather(self_log, "blk", axis=0, tiled=True),
            lax.all_gather(spread, "blk", axis=0, tiled=True),
            lax.all_gather(self_k.astype(jnp.float32), "blk", axis=0, tiled=True),
            lax.all_gather(self_v.astype(jnp.float32), "blk", axis=0, tiled=True),
        ),
        jnp.int32(0),
    )
    grad_sq = grad_query_acc.reshape(tokens, model_width).astype(jnp.bfloat16)
    grad_sk = grad_keys_acc.reshape(tokens, model_width).astype(jnp.bfloat16)
    grad_sv = grad_values_acc.reshape(tokens, model_width).astype(jnp.bfloat16)
    grad_self_query = jnp.einsum(
        "tc,te->ce", normed_one, grad_sq, preferred_element_type=jnp.float32
    )
    grad_self_query_bias = jnp.sum(grad_sq.astype(jnp.float32), 0)
    grad_self_key = jnp.einsum("tc,te->ce", normed_one, grad_sk, preferred_element_type=jnp.float32)
    grad_self_value = jnp.einsum(
        "tc,te->ce", normed_one, grad_sv, preferred_element_type=jnp.float32
    )
    grad_self_value_bias = jnp.sum(grad_sv.astype(jnp.float32), 0)
    grad_normed = (
        jnp.einsum("te,ce->tc", grad_sq, self_query, preferred_element_type=jnp.float32)
        + jnp.einsum("te,ce->tc", grad_sk, self_key, preferred_element_type=jnp.float32)
        + jnp.einsum("te,ce->tc", grad_sv, self_value, preferred_element_type=jnp.float32)
    )
    norm_grad, grad_self_norm_gain, grad_self_norm_bias = norm_back(
        grad_normed, unit_one, factor_one, self_norm_gain
    )
    residues_grad = upstream_one + norm_grad
    self_parts = (
        grad_self_norm_gain,
        grad_self_norm_bias,
        grad_self_query,
        grad_self_query_bias,
        grad_self_key,
        grad_self_value,
        grad_self_value_bias,
        grad_self_output,
        grad_self_output_bias,
    )
    ordered = (
        lax.psum_scatter(self_parts[0], "blk", scatter_dimension=0, tiled=True),
        lax.psum_scatter(self_parts[1], "blk", scatter_dimension=0, tiled=True),
        lax.psum_scatter(self_parts[2], "blk", scatter_dimension=0, tiled=True),
        lax.psum_scatter(self_parts[3], "blk", scatter_dimension=0, tiled=True),
        lax.psum_scatter(self_parts[4], "blk", scatter_dimension=0, tiled=True),
        lax.psum_scatter(self_parts[5], "blk", scatter_dimension=0, tiled=True),
        lax.psum_scatter(self_parts[6], "blk", scatter_dimension=0, tiled=True),
        lax.psum_scatter(self_parts[7], "blk", scatter_dimension=0, tiled=True),
        lax.psum_scatter(self_parts[8], "blk", scatter_dimension=0, tiled=True),
        lax.psum_scatter(cross_parts[0], "blk", scatter_dimension=0, tiled=True),
        lax.psum_scatter(cross_parts[1], "blk", scatter_dimension=0, tiled=True),
        lax.psum_scatter(cross_parts[2], "blk", scatter_dimension=0, tiled=True),
        lax.psum_scatter(cross_parts[3], "blk", scatter_dimension=0, tiled=True),
        lax.psum_scatter(cross_parts[4], "blk", scatter_dimension=0, tiled=True),
        lax.psum_scatter(cross_parts[5], "blk", scatter_dimension=0, tiled=True),
        lax.psum_scatter(cross_parts[6], "blk", scatter_dimension=0, tiled=True),
        lax.psum_scatter(cross_parts[7], "blk", scatter_dimension=0, tiled=True),
        lax.psum_scatter(cross_parts[8], "blk", scatter_dimension=0, tiled=True),
        lax.psum_scatter(feed_parts[0], "blk", scatter_dimension=0, tiled=True),
        lax.psum_scatter(feed_parts[1], "blk", scatter_dimension=0, tiled=True),
        lax.psum_scatter(feed_parts[2], "blk", scatter_dimension=0, tiled=True),
        lax.psum_scatter(feed_parts[3], "blk", scatter_dimension=0, tiled=True),
        lax.psum_scatter(feed_parts[4], "blk", scatter_dimension=0, tiled=True),
        lax.psum_scatter(feed_parts[5], "blk", scatter_dimension=0, tiled=True),
    )
    totals = lax.psum(
        (
            ordered[0],
            ordered[1],
            ordered[2],
            ordered[3],
            ordered[4],
            ordered[5],
            ordered[6],
            ordered[7],
            ordered[8],
            ordered[9],
            ordered[10],
            ordered[11],
            ordered[12],
            ordered[13],
            ordered[14],
            ordered[15],
            ordered[16],
            ordered[17],
            ordered[18],
            ordered[19],
            ordered[20],
            ordered[21],
            ordered[22],
            ordered[23],
        ),
        "batch",
    )
    return (layer_out[None], residues_grad[None], memory_grad[None]) + tuple(totals)


BLOCK = 128
HALF = 64
CHIPS = 8
HEAD = 64
WIDE = 512
HIDDEN = 2048
ROUND = 16
MASKED = -1e30
ONES_LANE = 5
SELF, CROSS = 0, 1
FAR_FIRST = (5, 7, 4, 6, 1, 3, 2)
MESH = pl.DeviceIdType.MESH
VMEM = pl.BlockSpec(memory_space=pltpu.VMEM)
SMEM = pl.BlockSpec(memory_space=pltpu.SMEM)
PLACED = pl.BlockSpec(memory_space=pl.ANY)
BF16, F32 = jnp.bfloat16, jnp.float32

SQ, SK, SV, SO, CQ, CK, CV, CO = range(8)
(
    ROW_SELF_GAIN, ROW_SELF_SHIFT, ROW_SQ, ROW_SV, ROW_SO, ROW_CROSS_GAIN, ROW_CROSS_SHIFT, ROW_CQ, ROW_CV, ROW_CO,
    ROW_FEED_GAIN, ROW_FEED_SHIFT, ROW_OUT, ROW_IN,
) = range(14)
VECTOR_ROWS = 24
UNIT_OUT, UNIT_IN = 0, 4
UNIT_OF = {CO: 8, SO: 9, CQ: 10, CK: 11, CV: 12, SQ: 13, SV: 14, SK: 15}
UNITS = 16
G_OUT, G_MORE, G_IN, G_REST, G_EARLY, G_CROSS, G_SQ, G_SV, G_SK = range(9)
SPANS = ((0, 2), (2, 4), (4, 6), (6, 9), (9, 11), (11, 13), (13, 14), (14, 15), (15, 16))
COLUMN_FIRST = (G_OUT, G_EARLY, G_SK)
BY_CORE, BY_FIRST, BY_SECOND, BY_PLANES, BY_NEAR, BY_FAR, BY_HALVES = range(7)
PLANES_IN_PAIRS = (G_OUT, G_MORE, G_IN, G_REST)
X_SQ, X_SO, X_CQ, X_CO, X_CDO, X_CDQ, X_SDO, X_SDQ = range(8)


class Operands(typing.NamedTuple):
    residues: VMEM
    memory: VMEM
    lengths: SMEM
    cotangent: VMEM
    self_norm_gain: VMEM
    self_norm_bias: VMEM
    self_query: PLACED
    self_query_bias: VMEM
    self_key: PLACED
    self_value: PLACED
    self_value_bias: VMEM
    self_output: PLACED
    self_output_bias: VMEM
    cross_norm_gain: VMEM
    cross_norm_bias: VMEM
    cross_query: PLACED
    cross_query_bias: VMEM
    cross_key: PLACED
    cross_value: PLACED
    cross_value_bias: VMEM
    cross_output: PLACED
    cross_output_bias: VMEM
    feed_norm_gain: VMEM
    feed_norm_bias: VMEM
    feed_in: PLACED
    feed_in_bias: VMEM
    feed_out: PLACED
    feed_out_bias: VMEM


AT_LAYER, AT_RESIDUES, AT_MEMORY, AT_SQUARE, AT_IN, AT_OUT, AT_VECTORS = 0, 128, 256, 384, 640, 768, 896
RESULT_ROWS = AT_VECTORS + VECTOR_ROWS


class Scratch(typing.NamedTuple):
    final: pltpu.VMEM((RESULT_ROWS, WIDE), F32)
    w_square: pltpu.VMEM((8, WIDE, WIDE), BF16)
    w_in: pltpu.VMEM((WIDE, HIDDEN), BF16)
    w_out: pltpu.VMEM((HIDDEN, WIDE), BF16)
    kv_out: pltpu.VMEM((2, CHIPS, BLOCK, BLOCK), BF16)
    kv: pltpu.VMEM((2, 2 * CHIPS, BLOCK, BLOCK), BF16)
    narrow_out: pltpu.VMEM((8, CHIPS, HALF, BLOCK), BF16)
    narrow: pltpu.VMEM((8, CHIPS, HALF, BLOCK), BF16)
    dkv_out: pltpu.VMEM((2, CHIPS, BLOCK, BLOCK), BF16)
    dkv: pltpu.VMEM((2, CHIPS, BLOCK, BLOCK), BF16)
    dkv_part: pltpu.VMEM((2, CHIPS, 2, BLOCK, BLOCK), BF16)
    dkv_other: pltpu.VMEM((2, CHIPS, BLOCK, BLOCK), BF16)
    dq_turned: pltpu.VMEM((BLOCK, 1024), F32)
    q_rows: pltpu.VMEM((2, 1024, BLOCK), BF16)
    q_features: pltpu.VMEM((2, 1024, BLOCK), BF16)
    do_rows: pltpu.VMEM((2, 1024, BLOCK), BF16)
    o_rows: pltpu.VMEM((2, 1024, BLOCK), F32)
    do_features: pltpu.VMEM((1024, BLOCK), BF16)
    query_features: pltpu.VMEM((1024, BLOCK), BF16)
    key_features: pltpu.VMEM((2048, BLOCK), BF16)
    causal: pltpu.VMEM((256, 512), F32)
    causal_turned: pltpu.VMEM((512, 256), F32)
    units: pltpu.VMEM((3, BLOCK, WIDE), F32)
    factors: pltpu.VMEM((3, BLOCK, BLOCK), F32)
    normed: pltpu.VMEM((3, BLOCK, WIDE), BF16)
    attended: pltpu.VMEM((2, BLOCK, WIDE), BF16)
    upstream: pltpu.VMEM((BLOCK, WIDE), F32)
    grad_active: pltpu.VMEM((BLOCK, HIDDEN), F32)
    active: pltpu.VMEM((BLOCK, HIDDEN), BF16)
    grad_inner: pltpu.VMEM((BLOCK, HIDDEN), BF16)
    parts: pltpu.VMEM((UNITS, 2, 2, 2, 2, 2, ROUND, WIDE), BF16)
    by_core: pltpu.VMEM((UNITS, 2, 2, 2, 2, ROUND, WIDE), BF16)
    by_side: pltpu.VMEM((UNITS, 2, 2, 2, ROUND, WIDE), BF16)
    by_column: pltpu.VMEM((UNITS, 2, 2, ROUND, WIDE), BF16)
    by_plane: pltpu.VMEM((3, UNITS, ROUND, WIDE), BF16)
    by_near: pltpu.VMEM((UNITS, 2, ROUND, WIDE), BF16)
    halves: pltpu.VMEM((2, UNITS, ROUND, WIDE), BF16)
    vectors: pltpu.VMEM((VECTOR_ROWS, WIDE), F32)
    vec_in: pltpu.VMEM((CHIPS, VECTOR_ROWS, BLOCK), F32)
    vec_four: pltpu.VMEM((4, VECTOR_ROWS, BLOCK), F32)
    load_sems: pltpu.SemaphoreType.DMA((10,))
    narrow_sems: pltpu.SemaphoreType.DMA((8,))
    kv_sems: pltpu.SemaphoreType.DMA((2, CHIPS))
    dkv_sems: pltpu.SemaphoreType.DMA((2,))
    pass_sems: pltpu.SemaphoreType.DMA((2,))
    share_sems: pltpu.SemaphoreType.DMA((2, 4))
    sent_sems: pltpu.SemaphoreType.DMA((7,))
    reduce_sems: pltpu.SemaphoreType.DMA((len(SPANS), 7))
    reduce_sent: pltpu.SemaphoreType.DMA((len(SPANS),))
    vec_sems: pltpu.SemaphoreType.DMA((2,))
    final_sems: pltpu.SemaphoreType.DMA((6,))


def specs_of(kind):
    return tuple(kind.__annotations__.values())


def dot_nn(left, right):
    return lax.dot_general(left, right, (((1,), (0,)), ((), ())), preferred_element_type=F32)


def dot_nt(left, right):
    return lax.dot_general(left, right, (((1,), (1,)), ((), ())), preferred_element_type=F32)


def dot_tn(left, right):
    return lax.dot_general(left, right, (((0,), (0,)), ((), ())), preferred_element_type=F32)


def low_lanes(shape):
    return lax.broadcasted_iota(jnp.int32, shape, len(shape) - 1) < HEAD


def turn(block):
    return pltpu.roll(block, HEAD, 1)


def swap(first, second):
    keep = low_lanes(first.shape)
    return jnp.where(keep, first, turn(second)), jnp.where(keep, turn(first), second)


def column_sum(low):
    return jnp.sum(low.astype(F32), 0, keepdims=True)


def flat(ref):
    return ref[...].reshape(1, -1)


def fused_kernel(*refs):
    count = len(specs_of(Operands))
    a, result, s = Operands(*refs[:count]), refs[count], Scratch(*refs[count + 1 :])

    rank = lax.axis_index("blk")
    side = lax.axis_index("batch")
    chip, core = lax.div(rank, 2), lax.rem(rank, 2)
    plane, column = lax.div(chip, 2), lax.rem(chip, 2)

    plane_high, plane_low = lax.div(plane, 2), lax.rem(plane, 2)

    def peer(turned):
        high, low, side_by = (
            1 - bit if turned >> at & 1 else bit for at, bit in ((2, plane_high), (1, plane_low), (0, column))
        )
        return 4 * high + 2 * low + side_by

    def at_rank(index):
        return {"blk": index}

    partner = at_rank(2 * chip + 1 - core)
    beside = at_rank(2 * (2 * plane + 1 - column) + core)
    across = {"batch": 1 - side}
    opposite = {"blk": 2 * chip + 1 - core, "batch": 1 - side}

    def remote(src, dst, sems, device):
        return pltpu.make_async_remote_copy(
            src_ref=src, dst_ref=dst, send_sem=sems[0], recv_sem=sems[1], device_id=device, device_id_type=MESH
        )

    SENT_NARROW, SENT_KV, SENT_PASS, SENT_DKV, SENT_SHARE, SENT_VECTOR, SENT_FOUR = (
        s.sent_sems.at[which] for which in range(7)
    )

    finished = []

    def final_put(at, values):
        s.final[pl.ds(at, values.shape[0]), : values.shape[1]] = values

    def final_start(at, rows):
        span = pl.ds(at, rows)
        finished.append(pltpu.make_async_copy(s.final.at[span], result.at[span], s.final_sems.at[len(finished)]))
        finished[-1].start()

    loads = {}

    def load(*pairs):
        for which, source in pairs:
            target = s.w_square.at[which] if which < 8 else (s.w_out, s.w_in)[which - 8]
            loads[which] = pltpu.make_async_copy(source, target, s.load_sems.at[which])
            loads[which].start()

    load((SK, a.self_key), (SV, a.self_value), (SQ, a.self_query))

    def weight(which):
        if which in loads:
            loads.pop(which).wait()
        return s.w_square[which] if which < 8 else (s.w_out, s.w_in)[which - 8]

    barrier = pltpu.get_barrier_semaphore()
    for shift in range(1, CHIPS):
        pl.semaphore_signal(barrier, inc=1, device_id=at_rank(2 * peer(shift) + core), device_id_type=MESH)
    for other in (partner, across, opposite):
        pl.semaphore_signal(barrier, inc=1, device_id=other, device_id_type=MESH)

    class Exchange:
        def __init__(self, outgoing, incoming, sems, sent, which, by_source=False):
            self.outgoing, self.incoming, self.by_source = outgoing.at[which], incoming.at[which], by_source
            self.sems, self.sent = sems.at[which], sent

        def slot(self, source):
            return self.incoming.at[2 * source + core if self.by_source else source]

        def pair(self, source):
            return (self.sent, self.sems.at[source] if self.by_source else self.sems)

        def start(self):
            for shift in FAR_FIRST:
                to = peer(shift)
                remote(self.outgoing.at[to], self.slot(chip), self.pair(chip), at_rank(2 * to + core)).start()
            self.slot(chip)[...] = self.outgoing[chip]

        def start_to(self, to):
            @pl.when(chip != to)
            def _():
                remote(self.outgoing.at[to], self.slot(chip), self.pair(chip), at_rank(2 * to + core)).start()

            @pl.when(chip == to)
            def _():
                self.slot(chip)[...] = self.outgoing[to]

        def wait(self, shift):
            source = peer(shift)
            remote(
                self.outgoing.at[source], self.slot(source), self.pair(source), at_rank(2 * source + core)
            ).wait_recv()

        def wait_all(self):
            seven = pl.ds(0, CHIPS - 1)
            remote(self.outgoing.at[seven], self.incoming.at[seven], (self.sent, self.sems), partner).wait_recv()

    narrow = [Exchange(s.narrow_out, s.narrow, s.narrow_sems, SENT_NARROW, which) for which in range(8)]
    keys_values = [Exchange(s.kv_out, s.kv, s.kv_sems, SENT_KV, which, True) for which in (SELF, CROSS)]
    key_grads = [Exchange(s.dkv_out, s.dkv, s.dkv_sems, SENT_DKV, which) for which in (SELF, CROSS)]

    def pass_on(kind):
        for shift in range(CHIPS):
            if shift > 0:
                keys_values[kind].wait(shift)
            slot = s.kv.at[kind, 2 * peer(shift) + core]
            remote(slot, slot, (SENT_PASS, s.pass_sems.at[kind]), partner).start()

    def pass_wait(kind):
        eight = s.kv.at[kind, pl.ds(0, CHIPS)]
        remote(eight, eight, (SENT_PASS, s.pass_sems.at[kind]), partner).wait_recv()

    def pack_groups(matrix, which):
        for pair in range(CHIPS // 2):
            group = matrix[:, BLOCK * pair : BLOCK * (pair + 1)]
            one, two = swap(group[:HALF], group[HALF:])
            s.narrow_out[which, 2 * pair] = one.astype(BF16)
            s.narrow_out[which, 2 * pair + 1] = two.astype(BF16)

    def unpack_groups(which):
        groups = []
        for pair in range(CHIPS // 2):
            groups.append(
                jnp.concatenate(
                    swap(s.narrow[which, 2 * pair].astype(F32), s.narrow[which, 2 * pair + 1].astype(F32)), 0
                )
            )
        return jnp.concatenate(groups, 1).astype(BF16)

    def pack_pairs(keys, values, kind):
        for pair in range(CHIPS // 2):
            lanes = slice(BLOCK * pair, BLOCK * (pair + 1))
            one, two = swap(keys[:, lanes], values[:, lanes])
            s.kv_out[kind, 2 * pair] = one.astype(BF16)
            s.kv_out[kind, 2 * pair + 1] = two.astype(BF16)

    def unpack_pairs(kind):
        pairs = [
            swap(s.dkv[kind, 2 * pair].astype(F32), s.dkv[kind, 2 * pair + 1].astype(F32)) for pair in range(CHIPS // 2)
        ]
        return tuple(jnp.concatenate(each, 1).astype(BF16) for each in zip(*pairs, strict=True))

    def plane_rank(other):
        return at_rank(2 * (2 * other + column) + core)

    def reduce_copies(stage, group):
        first, last = SPANS[group]
        span = pl.ds(first, last - first)
        sems = (s.reduce_sent.at[group], s.reduce_sems.at[group, stage])
        columns = (stage == BY_FIRST) == (group in COLUMN_FIRST)
        if stage == BY_CORE:
            return [remote(s.parts.at[span, :, :, :, 1 - core], s.by_core.at[span], sems, partner)]
        if stage == BY_FIRST:
            source = s.by_core.at[span, :, :, 1 - column] if columns else s.by_core.at[span, :, :, :, 1 - side]
            return [remote(source, s.by_side.at[span], sems, beside if columns else across)]
        if stage == BY_SECOND:
            source = s.by_side.at[span, :, :, 1 - column if columns else 1 - side]
            return [remote(source, s.by_column.at[span], sems, beside if columns else across)]
        if stage == BY_PLANES:
            others = [lax.rem(plane + shift, 4) for shift in range(1, 4)]
            return [
                remote(
                    s.by_column.at[span, lax.div(to, 2), lax.rem(to, 2)], s.by_plane.at[at, span], sems, plane_rank(to)
                )
                for at, to in enumerate(others)
            ]
        if stage == BY_NEAR:
            to = plane_rank(2 * plane_high + 1 - plane_low)
            return [remote(s.by_column.at[span, :, 1 - plane_low], s.by_near.at[span], sems, to)]
        if stage == BY_FAR:
            to = plane_rank(2 * (1 - plane_high) + plane_low)
            return [remote(s.by_near.at[span, 1 - plane_high], s.by_plane.at[0, span], sems, to)]
        return [remote(s.halves.at[side, span], s.halves.at[side, span], sems, across)]

    def reduce_whole(stage, group):
        if stage != BY_PLANES:
            return reduce_copies(stage, group)[0]
        blocks = s.by_plane.at[:, pl.ds(SPANS[group][0], SPANS[group][1] - SPANS[group][0])]
        return remote(blocks, blocks, (s.reduce_sent.at[group], s.reduce_sems.at[group, stage]), partner)

    def reduce_next(stage, group):
        if stage == BY_SECOND:
            return BY_NEAR if group in PLANES_IN_PAIRS else BY_PLANES
        return {BY_CORE: BY_FIRST, BY_FIRST: BY_SECOND, BY_NEAR: BY_FAR}.get(stage, BY_HALVES)

    def reduce_start(stage, group):
        for copy in reduce_copies(stage, group):
            copy.start()

    def reduce_finish(stage, group):
        first, last = SPANS[group]
        if stage == BY_HALVES:
            half = s.halves.at[1 - side, pl.ds(first, last - first)]
            remote(half, half, (s.reduce_sent.at[group], s.reduce_sems.at[group, stage]), across).wait_recv()
            return
        reduce_whole(stage, group).wait_recv()
        columns = (stage == BY_FIRST) == (group in COLUMN_FIRST)

        def add(unit, nothing):
            if stage == BY_CORE:
                s.by_core[unit] = s.by_core[unit] + s.parts[unit, :, :, :, core]
            if stage == BY_FIRST:
                own = s.by_core[unit, :, :, column] if columns else s.by_core[unit, :, :, :, side]
                s.by_side[unit] = s.by_side[unit] + own
            if stage == BY_SECOND:
                s.by_column[unit] = s.by_column[unit] + s.by_side[unit, :, :, column if columns else side]
            if stage == BY_PLANES:
                total = s.by_column[unit, plane_high, plane_low].astype(F32)
                for each in range(3):
                    total = total + s.by_plane[each, unit].astype(F32)
                s.halves[side, unit] = total.astype(BF16)
            if stage == BY_NEAR:
                s.by_near[unit] = s.by_near[unit] + s.by_column[unit, :, plane_low]
            if stage == BY_FAR:
                s.halves[side, unit] = s.by_plane[0, unit] + s.by_near[unit, plane_high]
            return nothing

        lax.fori_loop(first, last, add, 0)

    def reduce_step(stage, group):
        reduce_finish(stage, group)
        reduce_whole(stage, group).wait_send()
        reduce_start(reduce_next(stage, group), group)

    def put_unit(unit, value):
        s.parts[unit] = value.astype(BF16).reshape(2, 2, 2, 2, 2, ROUND, WIDE)

    def put_vector(row, values):
        if values.shape[1] == WIDE:
            s.vectors[pl.ds(row, 1), :] = values
            return
        for at in range(HIDDEN // BLOCK):
            group, piece = divmod(at, 4)
            s.vectors[pl.ds(row + piece, 1), BLOCK * group : BLOCK * (group + 1)] = values[
                :, BLOCK * at : BLOCK * (at + 1)
            ]

    def norm(values, which, gain, shift):
        average = jnp.mean(values, -1, keepdims=True)
        centred = values - average
        factor = lax.rsqrt(jnp.mean(centred * centred, -1, keepdims=True) + EPS)
        normal = centred * factor
        s.units[which] = normal
        s.factors[which] = jnp.broadcast_to(factor, (BLOCK, BLOCK))
        low = (normal * flat(gain) + flat(shift)).astype(BF16)
        s.normed[which] = low
        return low

    def norm_gradient(gradient, which, gain, row):
        normal = s.units[which]
        weighted = gradient * flat(gain)
        one = jnp.mean(weighted, -1, keepdims=True)
        two = jnp.mean(weighted * normal, -1, keepdims=True)
        put_vector(row, jnp.sum(gradient * normal, 0, keepdims=True))
        put_vector(row + 1, jnp.sum(gradient, 0, keepdims=True))
        return s.factors[which][:, :1] * (weighted - one - normal * two)

    def query_rows(kind, which):
        keep = low_lanes((HALF, BLOCK))
        for block in range(CHIPS):
            piece = s.narrow[which, block].astype(F32)
            both = jnp.concatenate([jnp.where(keep, piece, 0.0), jnp.where(keep, turn(piece), 0.0)], 0)
            s.q_rows[kind, pl.ds(block * BLOCK, BLOCK), :] = both.astype(BF16)

    def key_block(kind, chunk):
        rows = s.kv[kind, pl.ds(4 * chunk, 4)].reshape(512, BLOCK)
        return jnp.concatenate([rows, s.key_features[pl.ds(512 * chunk, 512), :]], 1)

    def with_column(features, column_values):
        lane = lax.broadcasted_iota(jnp.int32, features.shape, 1)
        full = jnp.broadcast_to(column_values, features.shape)
        high = full.astype(BF16).astype(F32)
        middle = (full - high).astype(BF16).astype(F32)
        low = full - high - middle
        for at, piece in enumerate((high, middle, low)):
            features = jnp.where(lane == ONES_LANE + at, piece, features)
        return features.astype(BF16)

    def attend(kind, causal, which):
        for part in range(4):
            rows = pl.ds(part * 256, 256)
            queries = jnp.concatenate([s.q_rows[kind, rows, :], s.query_features[rows, :]], 1)
            highest, summed = None, None
            chunks = range(part, -1, -1) if causal else range(4)
            for chunk in chunks:
                keys = key_block(kind, chunk)
                scores = dot_nt(queries, keys)
                if causal and chunk == part:
                    scores = scores + s.causal[...]
                reach = scores[:, :BLOCK]
                for at in range(1, 4):
                    reach = jnp.maximum(reach, scores[:, BLOCK * at : BLOCK * (at + 1)])
                reach = jnp.max(reach, 1, keepdims=True)
                if summed is None:
                    summed = dot_nn(jnp.exp(scores - reach).astype(BF16), keys)
                else:
                    reach = jnp.maximum(highest, reach)
                    summed = summed * jnp.exp(highest - reach) + dot_nn(jnp.exp(scores - reach).astype(BF16), keys)
                highest = reach
            total = summed[:, BLOCK + ONES_LANE : BLOCK + ONES_LANE + 1]
            result = summed[:, :BLOCK] / total
            s.o_rows[kind, rows, :] = result
            s.q_features[kind, rows, :] = with_column(
                s.query_features[rows, :].astype(F32), -(highest + jnp.log(total))
            )
            keep = low_lanes((HALF, BLOCK))
            for half in range(2):
                block = result[BLOCK * half : BLOCK * (half + 1)]
                s.narrow_out[which, 2 * part + half] = jnp.where(keep, turn(block[:HALF]), block[HALF:]).astype(BF16)

    def attend_back(kind, causal, which_in, which_out, between):
        keep = low_lanes((HALF, BLOCK))
        for block in range(CHIPS):
            rows = pl.ds(block * BLOCK, BLOCK)
            piece = s.narrow[which_in, block].astype(F32)
            gradient = jnp.concatenate([jnp.where(keep, 0.0, turn(piece)), jnp.where(keep, 0.0, piece)], 0)
            s.do_rows[kind, rows, :] = gradient.astype(BF16)
            spread = jnp.sum(gradient * s.o_rows[kind, rows, :], 1, keepdims=True)
            s.do_features[rows, :] = with_column(jnp.zeros((BLOCK, BLOCK), F32), -spread)
        for chunk in range(4):
            keys = key_block(kind, chunk)
            total = None
            for part in range(chunk if causal else 0, 4):
                rows = pl.ds(part * 256, 256)
                queries, grads = s.q_rows[kind, rows, :], s.do_rows[kind, rows, :]
                scores = dot_nt(keys, jnp.concatenate([queries, s.q_features[kind, rows, :]], 1))
                if causal and part == chunk:
                    scores = scores + s.causal_turned[...]
                weights = jnp.exp(scores)
                slopes = dot_nt(keys, jnp.concatenate([grads, s.do_features[rows, :]], 1))
                tilted = (weights * slopes).astype(BF16)
                shares = dot_nn(
                    jnp.concatenate([tilted, weights.astype(BF16)], 1), jnp.concatenate([queries, grads], 0)
                )
                total = shares if total is None else total + shares
                toward = dot_tn(keys[:, :BLOCK], tilted)
                s.dq_turned[:, rows] = toward if chunk == 0 else s.dq_turned[:, rows] + toward
            s.dkv_part[kind, 2 * chunk : 2 * chunk + 2] = total.astype(BF16).reshape(2, 2, BLOCK, BLOCK)
            between(chunk)
        if not causal:
            for part in range(4):
                put_dq(which_out, part)

    def put_dq(which, part):
        for block in (2 * part, 2 * part + 1):
            s.narrow_out[which, block] = (
                s.dq_turned[:HEAD, BLOCK * block : BLOCK * (block + 1)] * (HEAD**-0.5)
            ).astype(BF16)

    def turned_rows(which):
        return s.narrow[which].reshape(WIDE, BLOCK).astype(F32).T.astype(BF16)

    def share_copy(kind, part):
        chips = pl.ds(2 * part, 2)
        return remote(
            s.dkv_part.at[kind, chips, 1 - core], s.dkv_other.at[kind, chips], (SENT_SHARE, s.share_sems.at[kind, part]),
            partner,
        )

    def share_finish(kind, part):
        share_copy(kind, part).wait_recv()
        chips = slice(2 * part, 2 * part + 2)
        s.dkv_out[kind, chips] = s.dkv_part[kind, chips, core] + s.dkv_other[kind, chips]

    inputs = a.residues[...].astype(F32)
    normed = norm(inputs, 0, a.self_norm_gain, a.self_norm_bias)
    keys = dot_nn(normed, weight(SK))
    values = dot_nn(normed, weight(SV)) + flat(a.self_value_bias)
    pack_pairs(keys, values, SELF)
    pl.semaphore_wait(barrier, CHIPS + 2)
    keys_values[SELF].start()
    load((CK, a.cross_key), (CV, a.cross_value), (8, a.feed_out), (SO, a.self_output))
    load((CQ, a.cross_query), (CO, a.cross_output), (9, a.feed_in))
    queries = (dot_nn(normed, weight(SQ)) + flat(a.self_query_bias)) * (HEAD**-0.5)
    pack_groups(queries, X_SQ)
    narrow[X_SQ].start()

    encoded = a.memory[...]
    keys = dot_nn(encoded, weight(CK))
    values = dot_nn(encoded, weight(CV)) + flat(a.cross_value_bias)
    pack_pairs(keys, values, CROSS)

    bounds, reach = [], 0
    for at in range(4):
        reach = reach + a.lengths[0, at]
        bounds.append(reach)
    lane = lax.broadcasted_iota(jnp.int32, (BLOCK, BLOCK), 1)
    row = lax.broadcasted_iota(jnp.int32, (BLOCK, BLOCK), 0)

    def documents(position):
        found = jnp.zeros((BLOCK, BLOCK), jnp.int32)
        for bound in bounds:
            found = found + (position >= bound).astype(jnp.int32)
        return found

    ones = jnp.where((lane >= ONES_LANE) & (lane < ONES_LANE + 3), 1.0, 0.0)

    def key_features(block, nothing):
        other = documents(row + block * BLOCK) != lane
        s.key_features[pl.ds(block * BLOCK, BLOCK), :] = jnp.where((lane < ONES_LANE) & other, MASKED, ones).astype(
            BF16
        )
        return nothing

    lax.fori_loop(0, 2 * CHIPS, key_features, 0)

    def query_features(block, nothing):
        same = documents(row + (2 * block + core) * BLOCK) == lane
        s.query_features[pl.ds(block * BLOCK, BLOCK), :] = jnp.where((lane < ONES_LANE) & same, 1.0, 0.0).astype(BF16)
        return nothing

    lax.fori_loop(0, CHIPS, query_features, 0)

    def query_place(at):
        return at + core * BLOCK + jnp.where(at >= BLOCK, BLOCK, 0)

    at_row = lax.broadcasted_iota(jnp.int32, (256, 512), 0)
    at_key = lax.broadcasted_iota(jnp.int32, (256, 512), 1)
    s.causal[...] = jnp.where(at_key <= query_place(at_row), 0.0, MASKED)
    at_key = lax.broadcasted_iota(jnp.int32, (512, 256), 0)
    at_row = lax.broadcasted_iota(jnp.int32, (512, 256), 1)
    s.causal_turned[...] = jnp.where(at_key <= query_place(at_row), 0.0, MASKED)
    pass_on(SELF)
    keys_values[CROSS].start()
    narrow[X_SQ].wait_all()
    query_rows(SELF, X_SQ)
    pass_wait(SELF)
    attend(SELF, True, X_SO)
    narrow[X_SO].start()
    grads = a.cotangent[...]
    weight(8)
    for piece in range(4):
        lanes = slice(512 * piece, 512 * (piece + 1))
        s.grad_active[:, lanes] = dot_nt(grads, s.w_out[lanes, :])
    pass_on(CROSS)
    narrow[X_SO].wait_all()
    self_low = unpack_groups(X_SO)
    s.attended[SELF] = self_low
    after_self = inputs + dot_nn(self_low, weight(SO)) + flat(a.self_output_bias)

    normed = norm(after_self, 1, a.cross_norm_gain, a.cross_norm_bias)
    queries = (dot_nn(normed, weight(CQ)) + flat(a.cross_query_bias)) * (HEAD**-0.5)
    pack_groups(queries, X_CQ)
    narrow[X_CQ].start()
    pass_wait(CROSS)
    narrow[X_CQ].wait_all()
    query_rows(CROSS, X_CQ)
    attend(CROSS, False, X_CO)
    narrow[X_CO].start()
    weight(9)
    narrow[X_CO].wait_all()
    cross_low = unpack_groups(X_CO)
    s.attended[CROSS] = cross_low
    after_cross = after_self + dot_nn(cross_low, weight(CO)) + flat(a.cross_output_bias)

    normed = norm(after_cross, 2, a.feed_norm_gain, a.feed_norm_bias)
    back = None
    for piece in range(4):
        lanes = slice(512 * piece, 512 * (piece + 1))
        inner = dot_nn(normed, s.w_in[:, lanes]) + flat(a.feed_in_bias)[:, lanes]
        bell = 0.5 * (1.0 + lax.erf(inner * SQRT_HALF))
        active = (inner * bell).astype(BF16)
        slope = bell + inner * jnp.exp(-0.5 * inner * inner) * INV_ROOT_TAU
        grad_inner = (s.grad_active[:, lanes] * slope).astype(BF16)
        s.active[:, lanes] = active
        s.grad_inner[:, lanes] = grad_inner
        toward = dot_nt(grad_inner, s.w_in[:, lanes])
        back = toward if back is None else back + toward
    s.final[AT_LAYER : AT_LAYER + BLOCK, :] = after_cross + flat(a.feed_out_bias)
    upstream = a.cotangent[...].astype(F32)
    upstream = upstream + norm_gradient(back, 2, a.feed_norm_gain, ROW_FEED_GAIN)

    branch = upstream.astype(BF16)
    pack_groups(dot_nt(branch, weight(CO)), X_CDO)
    narrow[X_CDO].start()
    s.upstream[...] = upstream
    put_vector(ROW_OUT, column_sum(a.cotangent[...]))
    put_vector(ROW_IN, column_sum(s.grad_inner[...]))
    put_vector(ROW_CO, column_sum(branch))
    for piece in range(4):
        lanes = slice(512 * piece, 512 * (piece + 1))
        part = dot_tn(s.active[:, lanes], a.cotangent[...]).astype(BF16).reshape(2, 2, 4, 2, ROUND, WIDE)
        for each in range(4):
            s.parts[UNIT_OUT + each, piece // 2, piece % 2] = part[:, :, each]
    reduce_start(BY_CORE, G_OUT)
    reduce_start(BY_CORE, G_MORE)
    for piece in range(4):
        lanes = slice(512 * piece, 512 * (piece + 1))
        put_unit(UNIT_IN + piece, dot_tn(s.normed[2], s.grad_inner[:, lanes]))
        if piece == 1:
            reduce_start(BY_CORE, G_IN)
            reduce_step(BY_CORE, G_MORE)
    put_unit(UNIT_OF[CO], dot_tn(s.attended[CROSS], branch))
    reduce_start(BY_CORE, G_REST)
    final_put(AT_LAYER, s.final[AT_LAYER : AT_LAYER + BLOCK, :] + dot_nn(s.active[...], s.w_out[...]))
    final_start(AT_LAYER, BLOCK)
    narrow[X_CDO].wait_all()

    def between_cross(chunk):
        if chunk == 0:
            reduce_step(BY_CORE, G_OUT)
            reduce_step(BY_CORE, G_IN)
        share_copy(CROSS, chunk).start()

    attend_back(CROSS, False, X_CDO, X_CDQ, between_cross)
    narrow[X_CDQ].start()
    for part in range(4):
        share_finish(CROSS, part)
    key_grads[CROSS].start()
    reduce_step(BY_FIRST, G_OUT)
    reduce_step(BY_CORE, G_REST)
    reduce_step(BY_FIRST, G_MORE)
    narrow[X_CDQ].wait_all()
    grad_query = turned_rows(X_CDQ)
    gradient = dot_nt(grad_query, weight(CQ))
    upstream = s.upstream[...] + norm_gradient(gradient, 1, a.cross_norm_gain, ROW_CROSS_GAIN)

    branch = upstream.astype(BF16)
    pack_groups(dot_nt(branch, weight(SO)), X_SDO)
    narrow[X_SDO].start()
    reduce_step(BY_SECOND, G_OUT)
    reduce_step(BY_FIRST, G_IN)
    s.upstream[...] = upstream
    put_vector(ROW_SO, column_sum(branch))
    put_vector(ROW_CQ, column_sum(grad_query))
    put_unit(UNIT_OF[SO], dot_tn(s.attended[SELF], branch))
    put_unit(UNIT_OF[CQ], dot_tn(s.normed[1], grad_query))
    reduce_start(BY_CORE, G_EARLY)
    key_grads[CROSS].wait_all()
    grad_key, grad_value = unpack_pairs(CROSS)
    put_vector(ROW_CV, column_sum(grad_value))
    put_unit(UNIT_OF[CK], dot_tn(a.memory[...], grad_key))
    put_unit(UNIT_OF[CV], dot_tn(a.memory[...], grad_value))
    reduce_start(BY_CORE, G_CROSS)
    reduce_step(BY_CORE, G_EARLY)
    final_put(AT_MEMORY, dot_nt(grad_key, weight(CK)) + dot_nt(grad_value, weight(CV)))
    final_start(AT_MEMORY, BLOCK)
    narrow[X_SDO].wait_all()
    reduce_step(BY_SECOND, G_MORE)
    reduce_step(BY_FIRST, G_REST)

    def between_self(chunk):
        put_dq(X_SDQ, chunk)
        share_copy(SELF, chunk).start()
        if chunk > 0:
            send_shares(chunk - 1)
        for to in (2 * chunk, 2 * chunk + 1):
            narrow[X_SDQ].start_to(to)
        if chunk == 0:
            reduce_step(BY_CORE, G_CROSS)
            reduce_step(BY_NEAR, G_OUT)
        if chunk == 1:
            reduce_step(BY_SECOND, G_IN)

    def send_shares(part):
        share_finish(SELF, part)
        for to in (2 * part, 2 * part + 1):
            key_grads[SELF].start_to(to)

    attend_back(SELF, True, X_SDO, X_SDQ, between_self)
    send_shares(3)
    reduce_step(BY_NEAR, G_MORE)
    reduce_step(BY_FAR, G_OUT)
    reduce_step(BY_FIRST, G_EARLY)
    reduce_step(BY_FIRST, G_CROSS)
    narrow[X_SDQ].wait_all()
    grad_query = turned_rows(X_SDQ)
    normed = s.normed[0]
    put_unit(UNIT_OF[SQ], dot_tn(normed, grad_query))
    reduce_start(BY_CORE, G_SQ)
    reduce_step(BY_SECOND, G_REST)
    reduce_step(BY_NEAR, G_IN)
    reduce_step(BY_CORE, G_SQ)
    key_grads[SELF].wait_all()
    grad_key, grad_value = unpack_pairs(SELF)
    put_unit(UNIT_OF[SV], dot_tn(normed, grad_value))
    reduce_start(BY_CORE, G_SV)
    put_unit(UNIT_OF[SK], dot_tn(normed, grad_key))
    reduce_start(BY_CORE, G_SK)
    put_vector(ROW_SQ, column_sum(grad_query))
    put_vector(ROW_SV, column_sum(grad_value))
    gradient = dot_nt(grad_query, weight(SQ)) + dot_nt(grad_key, weight(SK)) + dot_nt(grad_value, weight(SV))
    reduce_step(BY_CORE, G_SV)
    reduce_step(BY_CORE, G_SK)
    final_put(AT_RESIDUES, s.upstream[...] + norm_gradient(gradient, 0, a.self_norm_gain, ROW_SELF_GAIN))
    final_start(AT_RESIDUES, BLOCK)

    def vector_copy(shift):
        if shift < CHIPS:
            to = peer(shift)
            lanes = pl.ds(pl.multiple_of(lax.div(to, 2) * BLOCK, BLOCK), BLOCK)
            sems = (SENT_VECTOR, s.vec_sems.at[0])
            return remote(s.vectors.at[:, lanes], s.vec_in.at[shift], sems, at_rank(2 * to + core))
        other = (partner, across, opposite)[shift - CHIPS]
        return remote(s.vec_four.at[0], s.vec_four.at[shift - CHIPS + 1], (SENT_FOUR, s.vec_sems.at[1]), other)

    def vector_all(step):
        rows = s.vec_in.at[pl.ds(1, 7)] if step == 0 else s.vec_four.at[pl.ds(1, 3)]
        return remote(rows, rows, ((SENT_VECTOR, SENT_FOUR)[step], s.vec_sems.at[step]), partner)

    s.vectors[pl.ds(17, VECTOR_ROWS - 17), :] = jnp.zeros((VECTOR_ROWS - 17, WIDE), F32)
    for shift in FAR_FIRST:
        vector_copy(shift).start()
    reduce_step(BY_SECOND, G_EARLY)
    reduce_step(BY_SECOND, G_CROSS)
    reduce_step(BY_NEAR, G_REST)
    reduce_step(BY_FAR, G_MORE)
    reduce_step(BY_FAR, G_IN)
    reduce_step(BY_FIRST, G_SQ)
    lanes = pl.ds(pl.multiple_of(lax.div(chip, 2) * BLOCK, BLOCK), BLOCK)
    total = s.vectors[:, lanes]
    vector_all(0).wait_recv()
    for shift in range(1, CHIPS):
        total = total + s.vec_in[shift]
    s.vec_four[0] = total
    for other in range(3):
        vector_copy(CHIPS + other).start()
    reduce_step(BY_FIRST, G_SK)
    reduce_step(BY_FIRST, G_SV)
    reduce_step(BY_PLANES, G_EARLY)
    reduce_step(BY_SECOND, G_SQ)
    vector_all(1).wait_recv()
    total = (s.vec_four[0] + s.vec_four[2]) + (s.vec_four[1] + s.vec_four[3])
    place_in_group = lax.rem(rank, 4)
    s.final[pl.ds(AT_VECTORS, VECTOR_ROWS), :BLOCK] = pltpu.roll(total, lax.rem(BLOCK - 32 * place_in_group, BLOCK), 1)
    own = jnp.zeros((1, BLOCK), F32)
    for each in range(4):
        own = own + jnp.where(place_in_group == each, total[ROW_IN + each : ROW_IN + each + 1], 0.0)
    s.final[pl.ds(AT_VECTORS + ROW_IN, 1), :BLOCK] = own
    final_start(AT_VECTORS, VECTOR_ROWS)

    def unit_value(unit):
        return jnp.concatenate([s.halves[0, unit], s.halves[1, unit]], 0).astype(F32)

    def put_final_unit(at, unit):
        final_put(at, unit_value(unit))

    reduce_step(BY_SECOND, G_SK)
    reduce_step(BY_SECOND, G_SV)
    reduce_step(BY_FAR, G_REST)
    reduce_step(BY_PLANES, G_CROSS)
    reduce_step(BY_PLANES, G_SQ)
    for group in (G_OUT, G_MORE, G_IN, G_REST):
        reduce_finish(BY_HALVES, group)
    for piece in range(4):
        put_final_unit(AT_OUT + 32 * piece, UNIT_OUT + piece)
        put_final_unit(AT_IN + 32 * piece, UNIT_IN + piece)
    final_start(AT_IN, 2 * BLOCK)
    reduce_finish(BY_HALVES, G_EARLY)
    reduce_finish(BY_HALVES, G_CROSS)
    for which in (CO, CQ, CK, CV, SO):
        put_final_unit(AT_SQUARE + 32 * which, UNIT_OF[which])
    reduce_step(BY_PLANES, G_SK)
    reduce_step(BY_PLANES, G_SV)
    reduce_finish(BY_HALVES, G_SQ)
    reduce_finish(BY_HALVES, G_SK)
    reduce_finish(BY_HALVES, G_SV)
    for which in (SQ, SK, SV):
        put_final_unit(AT_SQUARE + 32 * which, UNIT_OF[which])
    final_start(AT_SQUARE, 256)
    for copy in finished:
        copy.wait()
    for group in range(len(SPANS)):
        reduce_whole(BY_HALVES, group).wait_send()
    seven = pl.ds(0, CHIPS - 1)
    for sent, blocks in (
        (SENT_NARROW, s.narrow_out.at[:, seven]), (SENT_KV, s.kv_out.at[:, seven]), (SENT_DKV, s.dkv_out.at[:, seven]),
        (SENT_PASS, s.kv.at[:, pl.ds(0, CHIPS)]), (SENT_SHARE, s.dkv_other),
    ):
        remote(blocks, blocks, (sent, s.vec_sems.at[0]), partner).wait_send()
    vector_all(0).wait_send()
    vector_all(1).wait_send()


def place_kernel(packed, *refs):
    results, vectors, sems = refs[:-2], refs[-2], refs[-1]
    copies = []

    def place(at, target):
        source = packed.at[pl.ds(at, target.shape[0]), pl.ds(0, target.shape[1])]
        copies.append(pltpu.make_async_copy(source, target, sems.at[len(copies)]))
        copies[-1].start()

    place(AT_VECTORS, vectors)
    for at, target in zip((AT_LAYER, AT_RESIDUES, AT_MEMORY), results[:3], strict=True):
        place(at, target)
    for which, at in SQUARE_RESULTS.items():
        place(AT_SQUARE + 32 * which, results[at])
    for piece in range(4):
        place(AT_IN + 32 * piece, results[23].at[:, pl.ds(512 * piece, 512)])
    place(AT_OUT, results[25])
    copies[0].wait()
    rows = vectors[...]
    for row, at in VECTOR_RESULTS.items():
        results[at][...] = rows[row, : results[at].shape[0]]
    for copy in copies[1:]:
        copy.wait()


SQUARE_RESULTS = {SQ: 5, SK: 7, SV: 8, SO: 10, CQ: 14, CK: 16, CV: 17, CO: 19}
VECTOR_RESULTS = {
    ROW_SELF_GAIN: 3, ROW_SELF_SHIFT: 4, ROW_SQ: 6, ROW_SV: 9, ROW_SO: 11, ROW_CROSS_GAIN: 12, ROW_CROSS_SHIFT: 13,
    ROW_CQ: 15, ROW_CV: 18, ROW_CO: 20, ROW_FEED_GAIN: 21, ROW_FEED_SHIFT: 22, ROW_OUT: 26, ROW_IN: 24,
}


def fused(residues, memory, lengths, cotangent, *parameters):
    packed = pl.pallas_call(
        fused_kernel,
        out_shape=jax.ShapeDtypeStruct((RESULT_ROWS, WIDE), F32),
        in_specs=specs_of(Operands),
        out_specs=PLACED,
        scratch_shapes=specs_of(Scratch),
        compiler_params=pltpu.CompilerParams(
            collective_id=0, has_side_effects=True, vmem_limit_bytes=60 * 1024 * 1024
        ),
    )(residues[0], memory[0], lengths, cotangent[0], *parameters)
    shapes = [jax.ShapeDtypeStruct((BLOCK, WIDE), F32)] * 3
    for parameter in parameters:
        shapes.append(jax.ShapeDtypeStruct((parameter.shape[0] // (2 * CHIPS),) + parameter.shape[1:], F32))
    results = pl.pallas_call(
        place_kernel,
        out_shape=shapes,
        in_specs=(PLACED,),
        out_specs=(VMEM,) * len(shapes),
        scratch_shapes=(pltpu.VMEM((VECTOR_ROWS, BLOCK), F32), pltpu.SemaphoreType.DMA((17,))),
        compiler_params=pltpu.CompilerParams(vmem_limit_bytes=60 * 1024 * 1024),
    )(packed)
    return tuple(each[None] for each in results[:3]) + tuple(results[3:])


def solution(mesh):
    fits = mesh.shape["blk"] == 2 * CHIPS and mesh.shape["batch"] == 2
    return jax.shard_map(
        fused if fits else local,
        mesh=mesh,
        in_specs=(
            P("batch", "blk", None),
            P("batch", "blk", None),
            P("batch", None),
            P("batch", "blk", None),
            P(),
            P(),
            P(),
            P(),
            P(),
            P(),
            P(),
            P(),
            P(),
            P(),
            P(),
            P(),
            P(),
            P(),
            P(),
            P(),
            P(),
            P(),
            P(),
            P(),
            P(),
            P(),
            P(),
            P(),
        ),
        out_specs=(
            P("batch", "blk", None),
            P("batch", "blk", None),
            P("batch", "blk", None),
            P("blk"),
            P("blk"),
            P("blk", None),
            P("blk"),
            P("blk", None),
            P("blk", None),
            P("blk"),
            P("blk", None),
            P("blk"),
            P("blk"),
            P("blk"),
            P("blk", None),
            P("blk"),
            P("blk", None),
            P("blk", None),
            P("blk"),
            P("blk", None),
            P("blk"),
            P("blk"),
            P("blk"),
            P("blk", None),
            P("blk"),
            P("blk", None),
            P("blk"),
        ),
        check_vma=False,
    )
```
